32 devices in a mesh: dp: 2 (over y), expert: 16 (over z, x, core).
Axes of the slice: x: 2, y: 2, z: 4, core: 2. Of those that a mesh axis runs over, the one named last changes fastest.
Arguments:
- tokens: bfloat16 [12288, 1024], P(('dp', 'expert')), may hold values from -6 to 6
- cotangent: bfloat16 [12288, 1024], P(('dp', 'expert')), may hold values from -6 to 6
- routes: int32 [12288, 8], P(('dp', 'expert')), may hold values from 0 to 15, all different within a row
- cont_group: int32 [32], P(('dp', 'expert')), may hold values from 0 to 1
- attn_gain: float32 [1024], P('dp'), may hold values from 0.5 to 1.5
- qkv_weight: float32 [1024, 2048], P('dp'), may hold values from -0.1875 to 0.1875
- out_weight: float32 [1024, 1024], P('dp'), may hold values from -3 to 3
- ffn_gain: float32 [1024], P('dp'), may hold values from 0.5 to 1.5
- router_weight: float32 [1024, 16], P('dp'), may hold values from -0.09375 to 0.09375
- gate_up_weight: float32 [16, 1024, 1024], P('expert', 'dp'), may hold values from -0.1875 to 0.1875
- down_weight: float32 [16, 512, 1024], P('expert', 'dp'), may hold values from -1 to 1
- mean_attn_gain: float32 [1024], P('dp'), may hold values from -0.625 to 0.625
- mean_qkv_weight: float32 [1024, 2048], P('dp'), may hold values from -0.625 to 0.625
- mean_out_weight: float32 [1024, 1024], P('dp'), may hold values from -0.625 to 0.625
- mean_ffn_gain: float32 [1024], P('dp'), may hold values from -0.625 to 0.625
- mean_router_weight: float32 [1024, 16], P('dp'), may hold values from -0.625 to 0.625
- mean_gate_up_weight: float32 [16, 1024, 1024], P('expert', 'dp'), may hold values from -0.625 to 0.625
- mean_down_weight: float32 [16, 512, 1024], P('expert', 'dp'), may hold values from -0.125 to 0.125
- square_attn_gain: float32 [1024], P('dp'), may hold values from 0.1 to 1
- square_qkv_weight: float32 [1024, 2048], P('dp'), may hold values from 0.1 to 1
- square_out_weight: float32 [1024, 1024], P('dp'), may hold values from 0.0005 to 0.005
- square_ffn_gain: float32 [1024], P('dp'), may hold values from 0.1 to 1
- square_router_weight: float32 [1024, 16], P('dp'), may hold values from 0.1 to 1
- square_gate_up_weight: float32 [16, 1024, 1024], P('expert', 'dp'), may hold values from 0.002 to 0.02
- square_down_weight: float32 [16, 512, 1024], P('expert', 'dp'), may hold values from 5e-05 to 0.0005
Outputs:
- output: bfloat16 [12288, 1024], P(('dp', 'expert'))
- input_grad: float32 [12288, 1024], P(('dp', 'expert'))
- update_attn_gain: float32 [1024], replicated
- update_qkv_weight: float32 [1024, 2048], replicated
- update_out_weight: float32 [1024, 1024], replicated
- update_ffn_gain: float32 [1024], replicated
- update_router_weight: float32 [1024, 16], replicated
- update_gate_up_weight: float32 [16, 1024, 1024], P('expert')
- update_down_weight: float32 [16, 512, 1024], P('expert')
- new_mean_attn_gain: float32 [1024], P('dp')
- new_mean_qkv_weight: float32 [1024, 2048], P('dp')
- new_mean_out_weight: float32 [1024, 1024], P('dp')
- new_mean_ffn_gain: float32 [1024], P('dp')
- new_mean_router_weight: float32 [1024, 16], P('dp')
- new_mean_gate_up_weight: float32 [16, 1024, 1024], P('expert', 'dp')
- new_mean_down_weight: float32 [16, 512, 1024], P('expert', 'dp')
- new_square_attn_gain: float32 [1024], P('dp')
- new_square_qkv_weight: float32 [1024, 2048], P('dp')
- new_square_out_weight: float32 [1024, 1024], P('dp')
- new_square_ffn_gain: float32 [1024], P('dp')
- new_square_router_weight: float32 [1024, 16], P('dp')
- new_square_gate_up_weight: float32 [16, 1024, 1024], P('expert', 'dp')
- new_square_down_weight: float32 [16, 512, 1024], P('expert', 'dp')
The draws below stay inside these ranges and needn't reach their ends.
Inputs may be any that keep to these rules, and one draw needn't show every extreme that they name: `routes`: each row names 8 different experts.
All inputs are finite; a program needn't handle non-finite values.
Results may differ from the reference program's by a relative error of at most 0.04.
Values may be sent and summed in bfloat16 or wider, within the bound.
No kernel may reach another device: no remote copies, remote signals or barrier semaphores. Data moves between devices by JAX's collectives and lax.ppermute only.
A program may use at most 320 MiB of HBM per device.

```python
import math
import jax
import jax.numpy as jnp
from jax import lax

D = 1024
HEADS = 16
KV_HEADS = 8
HEAD_DIM = 64
EXP_FF = 512
TOPK = 8
NPROMPT = 2
PROMPT_DEV = 128
CLEN = 128
MEMBERS = 16
EXPERTS = 16
PROMPT_LEN = 2048
TOK_DEV = 384
CONTS = 32
TOKENS = 12288
CAP = 240
N_DP = 2


def set_ends(array, rng, smallest, largest):
    spot = [jax.random.randint(jax.random.fold_in(rng, axis), (), 0, length) for axis, length in enumerate(array.shape)]
    widest = array.shape.index(max(array.shape))
    next_to = spot[:widest] + [(spot[widest] + 1) % array.shape[widest]] + spot[widest + 1:]
    return array.at[tuple(spot)].set(smallest).at[tuple(next_to)].set(largest)


def level_of(stream_key, shape, cuts, smallest, high):
    loudness = 1.0
    for dim, shards_of in cuts:
        steps = jax.random.uniform(jax.random.fold_in(jax.random.fold_in(stream_key, 6), dim), (shards_of,), jnp.float32, smallest / len(cuts), high / len(cuts))
        loudness = loudness * jnp.repeat(jnp.exp(steps), shape[dim] // shards_of).reshape((-1,) + (1,) * (len(shape) - 1 - dim))
    return loudness


def picks_of(stream_key, rows, count, top, lift):
    order = jax.random.permutation(jax.random.fold_in(stream_key, 1), count)
    boost = order
    for power in range(3):
        boost = boost * boost // count
    boost = boost * lift // count
    chance = jax.random.randint(jax.random.fold_in(stream_key, 2), (rows, count), 0, 4096) + boost
    sure = jax.random.permutation(jax.random.fold_in(stream_key, 3), rows)[jnp.arange(count) % rows]
    chance = jnp.where(jnp.arange(rows)[:, None] == sure[None, :], 1 << 14, chance)
    score = chance * count + jnp.arange(count)
    return lax.top_k(score.astype(jnp.int32), top)[1].astype(jnp.int32)


def gaussian(rng, extent, width, limit, cuts=(), held_as=jnp.bfloat16):
    values = width * jax.random.normal(rng, extent, jnp.float32)
    if cuts:
        values = values * level_of(rng, extent, cuts, -0.22, 0.18)
    return jnp.clip(values, -limit, limit).astype(held_as)


def setup_inputs(seed: int = 0) -> dict:
    key_list = jax.random.split(jax.random.key(seed), 26)
    return {
        "tokens": gaussian(key_list[0], (TOKENS, D), 1.0, 6.0, ((0, 32),)),
        "cotangent": gaussian(key_list[1], (TOKENS, D), 1.0, 6.0, ((0, 32),)),
        "routes": picks_of(key_list[2], TOKENS, EXPERTS, TOPK, 4096),
        "cont_group": set_ends(jax.random.randint(key_list[3], (CONTS,), 0, NPROMPT), jax.random.fold_in(key_list[3], 1), 0, NPROMPT - 1).astype(jnp.int32),
        "attn_gain": jnp.clip(1.0 + 0.1 * jax.random.normal(key_list[4], (D,), jnp.float32), 0.5, 1.5),
        "qkv_weight": gaussian(key_list[5], (D, (HEADS + 2 * KV_HEADS) * HEAD_DIM), D ** -0.5, 0.1875, ((0, 2),), jnp.float32),
        "out_weight": gaussian(key_list[6], (HEADS * HEAD_DIM, D), 4 ** -0.5, 3.0, ((0, 2),), jnp.float32),
        "ffn_gain": jnp.clip(1.0 + 0.1 * jax.random.normal(key_list[7], (D,), jnp.float32), 0.5, 1.5),
        "router_weight": gaussian(key_list[8], (D, EXPERTS), (4 * D) ** -0.5, 0.09375, ((0, 2),), jnp.float32),
        "gate_up_weight": gaussian(key_list[9], (EXPERTS, D, 2 * EXP_FF), D ** -0.5, 0.1875, ((0, 16), (1, 2)), jnp.float32),
        "down_weight": gaussian(key_list[10], (EXPERTS, EXP_FF, D), (EXP_FF // 16) ** -0.5, 1.0, ((0, 16), (1, 2)), jnp.float32),
        "mean_attn_gain": gaussian(key_list[11], (D,), 0.1, 0.625, ((0, 2),), jnp.float32),
        "mean_qkv_weight": gaussian(key_list[12], (D, (HEADS + 2 * KV_HEADS) * HEAD_DIM), 0.1, 0.625, ((0, 2),), jnp.float32),
        "mean_out_weight": gaussian(key_list[13], (HEADS * HEAD_DIM, D), 0.1, 0.625, ((0, 2),), jnp.float32),
        "mean_ffn_gain": gaussian(key_list[14], (D,), 0.1, 0.625, ((0, 2),), jnp.float32),
        "mean_router_weight": gaussian(key_list[15], (D, EXPERTS), 0.1, 0.625, ((0, 2),), jnp.float32),
        "mean_gate_up_weight": gaussian(key_list[16], (EXPERTS, D, 2 * EXP_FF), 0.1, 0.625, ((0, 16), (1, 2)), jnp.float32),
        "mean_down_weight": gaussian(key_list[17], (EXPERTS, EXP_FF, D), 0.02, 0.125, ((0, 16), (1, 2)), jnp.float32),
        "square_attn_gain": jnp.clip(jnp.exp(math.log(1.0) - 2.3025851 * jax.random.uniform(key_list[18], (D,), jnp.float32) ** level_of(key_list[18], (D,), ((0, 2),), -0.2, 0.2)), 0.1, 1.0),
        "square_qkv_weight": jnp.clip(jnp.exp(math.log(1.0) - 2.3025851 * jax.random.uniform(key_list[19], (D, (HEADS + 2 * KV_HEADS) * HEAD_DIM), jnp.float32) ** level_of(key_list[19], (D, (HEADS + 2 * KV_HEADS) * HEAD_DIM), ((0, 2),), -0.2, 0.2)), 0.1, 1.0),
        "square_out_weight": jnp.clip(jnp.exp(math.log(0.005) - 2.30258502 * jax.random.uniform(key_list[20], (HEADS * HEAD_DIM, D), jnp.float32) ** level_of(key_list[20], (HEADS * HEAD_DIM, D), ((0, 2),), -0.2, 0.2)), 0.0005, 0.005),
        "square_ffn_gain": jnp.clip(jnp.exp(math.log(1.0) - 2.3025851 * jax.random.uniform(key_list[21], (D,), jnp.float32) ** level_of(key_list[21], (D,), ((0, 2),), -0.2, 0.2)), 0.1, 1.0),
        "square_router_weight": jnp.clip(jnp.exp(math.log(1.0) - 2.3025851 * jax.random.uniform(key_list[22], (D, EXPERTS), jnp.float32) ** level_of(key_list[22], (D, EXPERTS), ((0, 2),), -0.2, 0.2)), 0.1, 1.0),
        "square_gate_up_weight": jnp.clip(jnp.exp(math.log(0.02) - 2.30258502 * jax.random.uniform(key_list[23], (EXPERTS, D, 2 * EXP_FF), jnp.float32) ** level_of(key_list[23], (EXPERTS, D, 2 * EXP_FF), ((0, 16), (1, 2)), -0.2, 0.2)), 0.002, 0.02),
        "square_down_weight": jnp.clip(jnp.exp(math.log(0.0005) - 2.3025852 * jax.random.uniform(key_list[24], (EXPERTS, EXP_FF, D), jnp.float32) ** level_of(key_list[24], (EXPERTS, EXP_FF, D), ((0, 16), (1, 2)), -0.2, 0.2)), 4.999999873689376e-05, 0.0005),
    }


norm_eps = 1e-05
masked_score = -1e+30
highest = lax.Precision.HIGHEST
decay_rate = 0.1
adam_eps = 1e-08
bias_first = 0.999973438601112
bias_second = 0.99407947078

@jax.custom_vjp
def low(v):
    return lax.optimization_barrier(v.astype(jnp.bfloat16)).astype(jnp.float32)

@jax.custom_vjp
def low_back(v):
    return v

def low_keep(v):
    return (low(v), None)

def low_pass(kept, grad):
    return (grad,)

def back_keep(v):
    return (v, None)

def back_low(kept, grad):
    return (low(grad),)
low.defvjp(low_keep, low_pass)
low_back.defvjp(back_keep, back_low)

def matmul(left_side, right_side):
    return jnp.dot(left_side, right_side, precision=highest, preferred_element_type=jnp.float32)

def rms_scale(values, gain_row):
    return values * lax.rsqrt(lax.optimization_barrier(jnp.mean(values * values, axis=-1, keepdims=True)) + norm_eps) * gain_row

def rotary(values, position):
    half_dim = HEAD_DIM // 2
    frequency = jnp.exp(jnp.arange(half_dim, dtype=jnp.float32) * (-2.0 * math.log(10000.0) / HEAD_DIM))
    angles = position.astype(jnp.float32)[:, None] * frequency[None, :]
    cosine = jnp.cos(angles)[:, None, :]
    sine_part = jnp.sin(angles)[:, None, :]
    first_half = values[..., :half_dim]
    second_half = values[..., half_dim:]
    return jnp.concatenate([first_half * cosine - second_half * sine_part, second_half * cosine + first_half * sine_part], axis=-1)

def token_positions():
    row_index = jnp.arange(TOKENS, dtype=jnp.int32)
    within = row_index % TOK_DEV
    member = row_index // TOK_DEV % MEMBERS
    prompt_rows = NPROMPT * PROMPT_DEV
    return jnp.where(within < prompt_rows, member * PROMPT_DEV + within // NPROMPT, PROMPT_LEN + within - prompt_rows)

def attend(query_block, key_block, value_block, allowed):
    row_count = query_block.shape[0]
    grouped = query_block.reshape(row_count, KV_HEADS, HEADS // KV_HEADS, HEAD_DIM)
    scores = jnp.einsum('rnpd,snd->nprs', grouped, key_block, precision=highest) * HEAD_DIM ** (-0.5)
    scores = low_back(scores)
    scores = jnp.where(allowed, scores, masked_score)
    prob_rows = low(jax.nn.softmax(scores, axis=-1))
    mixed = jnp.einsum('nprs,snd->rnpd', prob_rows, value_block, precision=highest)
    return mixed.reshape(row_count, HEADS * HEAD_DIM)

def attention(queries, key_rows, value_rows, cont_group):
    prompt_rows = NPROMPT * PROMPT_DEV

    def prompt_layout(values):
        head_count = values.shape[1]
        blocks = values.reshape(N_DP, MEMBERS, TOK_DEV, head_count, HEAD_DIM)[:, :, :prompt_rows]
        blocks = blocks.reshape(N_DP, MEMBERS, PROMPT_DEV, NPROMPT, head_count, HEAD_DIM)
        return blocks.transpose(0, 3, 1, 2, 4, 5).reshape(N_DP * NPROMPT, PROMPT_LEN, head_count, HEAD_DIM)

    def cont_layout(values):
        head_count = values.shape[1]
        blocks = values.reshape(N_DP, MEMBERS, TOK_DEV, head_count, HEAD_DIM)[:, :, prompt_rows:]
        return blocks.reshape(CONTS, CLEN, head_count, HEAD_DIM)
    prompt_query, prompt_key, prompt_value = (prompt_layout(queries), prompt_layout(key_rows), prompt_layout(value_rows))
    cont_query, cont_key, cont_value = (cont_layout(queries), cont_layout(key_rows), cont_layout(value_rows))
    block_rows = math.gcd(512, PROMPT_LEN)
    block_count = PROMPT_LEN // block_rows
    key_pos = jnp.arange(PROMPT_LEN, dtype=jnp.int32)

    def prompt_block(item_index):
        sequence = item_index // block_count
        first_row = item_index % block_count * block_rows
        query_block = lax.dynamic_slice_in_dim(prompt_query[sequence], first_row, block_rows, 0)
        query_pos = first_row + jnp.arange(block_rows, dtype=jnp.int32)
        allowed = key_pos[None, :] <= query_pos[:, None]
        return attend(query_block, prompt_key[sequence], prompt_value[sequence], allowed)
    prompt_out = lax.map(jax.checkpoint(prompt_block), jnp.arange(N_DP * NPROMPT * block_count, dtype=jnp.int32))
    prompt_out = prompt_out.reshape(N_DP, NPROMPT, MEMBERS, PROMPT_DEV, HEADS * HEAD_DIM)
    prompt_out = prompt_out.transpose(0, 2, 3, 1, 4).reshape(N_DP, MEMBERS, prompt_rows, HEADS * HEAD_DIM)
    cont_pos = jnp.arange(CLEN, dtype=jnp.int32)
    causal = cont_pos[None, :] <= cont_pos[:, None]
    allowed_cont = jnp.concatenate([jnp.ones((CLEN, PROMPT_LEN), jnp.bool_), causal], axis=1)

    def cont_item(item_index):
        sequence = item_index // MEMBERS * NPROMPT + cont_group[item_index]
        key_block = jnp.concatenate([prompt_key[sequence], cont_key[item_index]], axis=0)
        value_block = jnp.concatenate([prompt_value[sequence], cont_value[item_index]], axis=0)
        return attend(cont_query[item_index], key_block, value_block, allowed_cont)
    cont_out = lax.map(jax.checkpoint(cont_item), jnp.arange(CONTS, dtype=jnp.int32))
    cont_out = cont_out.reshape(N_DP, MEMBERS, CLEN, HEADS * HEAD_DIM)
    return jnp.concatenate([prompt_out, cont_out], axis=2).reshape(TOKENS, HEADS * HEAD_DIM)

def adamw(weight, mean_in, square_in, gradient, grad_scale, decay_factor):
    scaled = gradient * grad_scale
    mean_out = 0.9 * mean_in + 0.1 * scaled
    square_out = 0.95 * square_in + 0.05 * scaled * scaled
    update = mean_out / bias_first / (jnp.sqrt(square_out / bias_second) + adam_eps)
    return (update + decay_factor * weight, mean_out, square_out)

def reference(tokens, cotangent, routes, cont_group, attn_gain, qkv_weight, out_weight, ffn_gain, router_weight, gate_up_weight, down_weight, mean_attn_gain, mean_qkv_weight, mean_out_weight, mean_ffn_gain, mean_router_weight, mean_gate_up_weight, mean_down_weight, square_attn_gain, square_qkv_weight, square_out_weight, square_ffn_gain, square_router_weight, square_gate_up_weight, square_down_weight):
    position = token_positions()
    pair_block = TOK_DEV * TOPK
    flat_routes = routes.reshape(CONTS, pair_block)
    expert_ids = jnp.arange(EXPERTS, dtype=jnp.int32)
    one_hot = (flat_routes[:, :, None] == expert_ids[None, None, :]).astype(jnp.int32)
    placed = lax.optimization_barrier(jnp.sum((jnp.cumsum(one_hot, axis=1) - one_hot) * one_hot, axis=-1))
    kept_pairs = placed < CAP
    target = jnp.where(kept_pairs, flat_routes * CAP + placed, EXPERTS * CAP)
    pair_ids = jnp.arange(TOKENS * TOPK, dtype=jnp.int32).reshape(CONTS, pair_block)
    block_ids = jnp.arange(CONTS, dtype=jnp.int32)[:, None]
    slot_table = jnp.full((CONTS, EXPERTS * CAP), TOKENS * TOPK, jnp.int32).at[block_ids, target].set(pair_ids, mode='drop')
    slot_table = slot_table.reshape(CONTS, EXPERTS, CAP).transpose(1, 0, 2).reshape(EXPERTS, CONTS * CAP)
    kept_flat = kept_pairs.reshape(TOKENS * TOPK)
    query_width = HEADS * HEAD_DIM
    key_width = KV_HEADS * HEAD_DIM

    def forward(tok_float, gain_attn, weight_qkv, weight_out, gain_ffn, weight_router, weight_gate_up, weight_down):
        gain_attn = low(gain_attn)
        weight_qkv = low(weight_qkv)
        weight_out = low(weight_out)
        gain_ffn = low(gain_ffn)
        weight_router = low(weight_router)
        weight_gate_up = low(weight_gate_up)
        weight_down = low(weight_down)
        attn_in = low(rms_scale(tok_float, gain_attn))
        projected = matmul(attn_in, weight_qkv)
        queries = low(rotary(low_back(projected[:, :query_width]).reshape(TOKENS, HEADS, HEAD_DIM), position))
        key_rows = low(rotary(low_back(projected[:, query_width:query_width + key_width]).reshape(TOKENS, KV_HEADS, HEAD_DIM), position))
        value_rows = low(low_back(projected[:, query_width + key_width:])).reshape(TOKENS, KV_HEADS, HEAD_DIM)
        mixed_heads = low(low_back(attention(queries, key_rows, value_rows, cont_group)))
        hidden = tok_float + low_back(matmul(mixed_heads, weight_out))
        ffn_in = low(rms_scale(hidden, gain_ffn))
        logits = low_back(matmul(ffn_in, weight_router))
        chosen = jnp.take_along_axis(logits, routes, axis=1)
        gate_probs = jax.nn.softmax(chosen, axis=-1)
        gate_kept = jnp.where(kept_flat, gate_probs.reshape(TOKENS * TOPK), 0.0)

        def expert_part(expert):
            pair_rows = slot_table[expert]
            filled = pair_rows < TOKENS * TOPK
            safe_rows = jnp.where(filled, pair_rows, 0)
            owners = safe_rows // TOPK
            rows_in = low_back(jnp.where(filled[:, None], ffn_in[owners], 0.0))
            gate_up = low_back(matmul(rows_in, weight_gate_up[expert]))
            activated = low(jax.nn.silu(gate_up[:, :EXP_FF]) * gate_up[:, EXP_FF:])
            expert_out = low(low_back(matmul(activated, weight_down[expert])))
            weighted = jnp.where(filled, gate_kept[safe_rows], 0.0)[:, None] * expert_out
            return jnp.zeros((TOKENS, D), jnp.float32).at[owners].add(weighted)
        part_fn = jax.checkpoint(expert_part)

        def expert_step(running, expert):
            return (running + part_fn(expert), None)
        mixture, _ = lax.scan(expert_step, jnp.zeros((TOKENS, D), jnp.float32), jnp.arange(EXPERTS, dtype=jnp.int32))
        return hidden + mixture
    output, pullback = jax.vjp(forward, tokens.astype(jnp.float32), attn_gain, qkv_weight, out_weight, ffn_gain, router_weight, gate_up_weight, down_weight)
    gradients = pullback(cotangent.astype(jnp.float32))
    grad_scale = TOKENS ** (-0.5)
    first_gain = adamw(attn_gain, mean_attn_gain, square_attn_gain, gradients[1], grad_scale, 0.0)
    qkv_new = adamw(qkv_weight, mean_qkv_weight, square_qkv_weight, gradients[2], grad_scale, decay_rate)
    out_new = adamw(out_weight, mean_out_weight, square_out_weight, gradients[3], grad_scale, decay_rate)
    second_gain = adamw(ffn_gain, mean_ffn_gain, square_ffn_gain, gradients[4], grad_scale, 0.0)
    router_new = adamw(router_weight, mean_router_weight, square_router_weight, gradients[5], grad_scale, decay_rate)
    gate_up_new = adamw(gate_up_weight, mean_gate_up_weight, square_gate_up_weight, gradients[6], grad_scale, decay_rate)
    down_new = adamw(down_weight, mean_down_weight, square_down_weight, gradients[7], grad_scale, decay_rate)
    return (output.astype(jnp.bfloat16), gradients[0], first_gain[0], qkv_new[0], out_new[0], second_gain[0], router_new[0], gate_up_new[0], down_new[0], first_gain[1], qkv_new[1], out_new[1], second_gain[1], router_new[1], gate_up_new[1], down_new[1], first_gain[2], qkv_new[2], out_new[2], second_gain[2], router_new[2], gate_up_new[2], down_new[2])
```

```python
import functools
import math

import jax
import jax.numpy as jnp
from jax import lax
from jax.experimental import pallas as pl
from jax.experimental.pallas import tpu as pltpu
from jax.sharding import Mesh
from jax.sharding import PartitionSpec as P

HEADS = 16
KV_HEADS = 8
HEAD_DIM = 64
EXP_FF = 512
TOPK = 8
NPROMPT = 2
PROMPT_DEV = 128
CLEN = 128
REPEAT = HEADS // KV_HEADS
PROMPT_ROWS = NPROMPT * PROMPT_DEV

norm_eps = 1e-05
masked_score = -1e30
decay_rate = 0.1
adam_eps = 1e-08
bias_first = 0.999973438601112
bias_second = 0.99407947078
score_scale = HEAD_DIM ** (-0.5)

bf16 = jnp.bfloat16
f32 = jnp.float32


def dot(left, right):
    return jnp.dot(left, right, preferred_element_type=f32)


def dot_tn(left, right):
    return lax.dot_general(left, right, (((0,), (0,)), ((), ())), preferred_element_type=f32)


def dot_nt(left, right):
    return lax.dot_general(left, right, (((1,), (1,)), ((), ())), preferred_element_type=f32)


def norm_back(values, scale_rows, gain_row, grad_rows):
    normed = values * scale_rows
    grad_normed = grad_rows * gain_row
    grad_values = scale_rows * (
        grad_normed - normed * jnp.mean(grad_normed * normed, axis=-1, keepdims=True)
    )
    return (grad_values, jnp.sum(grad_rows * normed, axis=0))


def adamw(weight, mean_in, square_in, gradient, grad_scale, decay_factor):
    scaled = gradient * grad_scale
    mean_out = 0.9 * mean_in + 0.1 * scaled
    square_out = 0.95 * square_in + 0.05 * scaled * scaled
    spread = square_out * (1.0 / bias_second)
    spread = spread * lax.rsqrt(spread) + adam_eps
    update = mean_out * (1.0 / bias_first) / spread
    return (update + decay_factor * weight, mean_out, square_out)


def split_rows(values):
    head = values[:PROMPT_ROWS].reshape(PROMPT_DEV, NPROMPT, -1).transpose(1, 0, 2)
    return jnp.concatenate([head.reshape(PROMPT_ROWS, -1), values[PROMPT_ROWS:]], axis=0)


def merge_rows(values):
    head = values[:PROMPT_ROWS].reshape(NPROMPT, PROMPT_DEV, -1).transpose(1, 0, 2)
    return jnp.concatenate([head.reshape(PROMPT_ROWS, -1), values[PROMPT_ROWS:]], axis=0)


def swap(values):
    return lax.ppermute(values, "core", [(0, 1), (1, 0)])


class Ring:
    def __init__(self, chips):
        rows = 4 if chips % 4 == 0 else chips
        cols = chips // rows
        cycle = [(0, x) for x in range(cols)]
        for z in range(1, rows):
            line = [(z, x) for x in range(1, cols)]
            cycle += line[::-1] if z % 2 == 1 else line
        if cols > 1:
            cycle += [(z, 0) for z in range(rows - 1, 0, -1)]
        else:
            cycle = [(z, 0) for z in range(rows)]
        self.chips = chips
        self.order = [z * cols + x for z, x in cycle]
        self.forward = [
            (self.order[k], self.order[(k + 1) % chips]) for k in range(chips)
        ]
        self.backward = [(b, a) for a, b in self.forward]
        self.half = chips // 2
        self.by_distance = [r for group in self.groups() for r in group]

    def chips_from(self, me):
        table = [[0] * self.chips for _ in range(self.chips)]
        for k in range(self.chips):
            for column, offset in enumerate(self.by_distance):
                table[self.order[k]][column] = self.order[(k + offset) % self.chips]
        return lax.dynamic_index_in_dim(jnp.asarray(table, jnp.int32), me, 0, False)

    def gather_steps(self, block):
        gather = RingGather(self, block)
        yield {0: block}
        for _ in range(self.half):
            yield gather.step()

    @staticmethod
    def cut(block):
        return block.shape[0] // 32 * 16

    def groups(self):
        return [[0]] + [[-s, s] for s in range(1, self.half)] + [[self.half]]


class RingGather:
    def __init__(self, ring, block):
        self.ring = ring
        self.place = 0
        self.ahead = self.behind = block
        self.blocks = {0: block}

    def ends(self):
        return (self.ahead, self.behind)

    def step(self, *others):
        ring = self.ring
        self.place += 1
        if others:
            self.ahead, self.behind = after(self.ends(), others)
        self.before = self.ends()
        if self.place < ring.half:
            self.ahead = lax.ppermute(self.ahead, "chip", ring.forward)
            self.behind = lax.ppermute(self.behind, "chip", ring.backward)
            arrived = {-self.place: self.ahead, self.place: self.behind}
        else:
            cut = ring.cut(self.ahead)
            first = lax.ppermute(self.ahead[:cut], "chip", ring.forward)
            second = lax.ppermute(self.behind[cut:], "chip", ring.backward)
            arrived = {ring.half: jnp.concatenate([first, second], axis=0)}
        self.blocks.update(arrived)
        return arrived


class RingSum:
    def __init__(self, ring, part):
        cut = ring.cut(part)
        self.ring = ring
        self.place = ring.half
        self.cut = cut
        self.sent = (part[:cut], part[cut:])
        self.send()

    def send(self):
        self.ahead = lax.ppermute(self.sent[0], "chip", self.ring.forward)
        self.behind = lax.ppermute(self.sent[1], "chip", self.ring.backward)

    def arrived(self):
        return (self.ahead, self.behind)

    def add(self, parts, *others):
        ring, cut = self.ring, self.cut
        self.place -= 1
        up, down = parts[self.place], parts[-self.place]
        if others:
            up, down = after((up, down), others)
        self.ahead, self.behind = lax.optimization_barrier((self.ahead, self.behind))
        if self.place == ring.half - 1:
            ahead = jnp.concatenate([self.ahead + up[:cut], up[cut:]], axis=0)
            behind = jnp.concatenate([down[:cut], self.behind + down[cut:]], axis=0)
        else:
            ahead, behind = self.ahead + up, self.behind + down
        self.sent = (ahead, behind)
        self.send()

    def finish(self, part):
        return part.astype(f32) + self.ahead.astype(f32) + self.behind.astype(f32)


def after(values, *others):
    return lax.optimization_barrier((values, others))[0]


def total_stages(values, axes):
    for axis in axes:
        size = lax.axis_size(axis)
        reach = 1
        while reach < size:
            values = values + lax.ppermute(values, axis, [(k, k ^ reach) for k in range(size)])
            reach *= 2
            yield values


def dp_shards(values):
    size = lax.axis_size("dp")
    pieces = [values]
    for shift in range(1, size):
        perm = [(k, (k - shift) % size) for k in range(size)]
        pieces.append(lax.ppermute(values, "dp", perm))
    return pieces


def join_dp(pieces, axis):
    size = len(pieces)
    dp = lax.axis_index("dp")
    if size == 2:
        return jnp.concatenate(
            [
                jnp.where(dp == 0, pieces[0], pieces[1]),
                jnp.where(dp == 0, pieces[1], pieces[0]),
            ],
            axis=axis,
        )
    twice = jnp.concatenate(pieces + pieces, axis=axis)
    shard = pieces[0].shape[axis]
    return lax.dynamic_slice_in_dim(twice, (size - dp) % size * shard, size * shard, axis)


def gather_dp(values, axis):
    return join_dp(dp_shards(values), axis)


def pick_core(first, second):
    return jnp.where(lax.axis_index("core") == 0, first, second)


LOG2E = 1.4426950408889634


def stack_heads(wide):
    wide = wide.astype(f32)
    first, second = wide[:, :128], wide[:, 128:]
    lane = lax.broadcasted_iota(jnp.int32, first.shape, 1)
    low_lanes = lane < HEAD_DIM
    zero = jnp.zeros_like(first)
    return jnp.concatenate(
        [
            jnp.where(low_lanes, first, zero),
            jnp.where(low_lanes, pltpu.roll(first, HEAD_DIM, 1), zero),
            jnp.where(low_lanes, zero, pltpu.roll(second, HEAD_DIM, 1)),
            jnp.where(low_lanes, zero, second),
        ],
        axis=0,
    )


def unstack_heads(tall):
    rows = tall.shape[0] // 4
    parts = [tall[k * rows : (k + 1) * rows] for k in range(4)]
    lane = lax.broadcasted_iota(jnp.int32, parts[0].shape, 1)
    low_lanes = lane < HEAD_DIM
    return jnp.concatenate(
        [
            jnp.where(low_lanes, parts[0], pltpu.roll(parts[1], HEAD_DIM, 1)),
            jnp.where(low_lanes, pltpu.roll(parts[2], HEAD_DIM, 1), parts[3]),
        ],
        axis=1,
    )


def row_of(column_sum_of):
    return jnp.sum(jnp.transpose(column_sum_of), axis=0, keepdims=True)


def tile_masks(meta_ref, half, is_cont):
    shape = (PROMPT_ROWS, 4 * PROMPT_DEV)
    key = lax.broadcasted_iota(jnp.int32, shape, 0)
    query = lax.broadcasted_iota(jnp.int32, shape, 1) % PROMPT_DEV
    key_member = jnp.where(key < PROMPT_DEV, meta_ref[2], meta_ref[3])
    key_pos = key_member * PROMPT_DEV + key % PROMPT_DEV
    query_pos = meta_ref[2 + half] * PROMPT_DEV + query
    own = (key_pos <= query_pos) | is_cont
    shape = (CLEN, 4 * CLEN)
    key = lax.broadcasted_iota(jnp.int32, shape, 0)
    query = lax.broadcasted_iota(jnp.int32, shape, 1) % CLEN
    self_seen = (key <= query) & is_cont
    return own, self_seen


META = 8


def block_bias(meta_ref, is_cont, first_block, blocks):
    chips = [meta_ref[META + first_block + k] for k in range(blocks)]
    return [jnp.where(is_cont | (c <= meta_ref[6]), 0.0, masked_score) for c in chips]


def attend_kernel(first_block, blocks, first, last, meta_ref, q_ref, *refs):
    kv_refs, refs = refs[:blocks], refs[blocks:]
    if first:
        self_ref, refs = refs[0], refs[1:]
    else:
        acc_in, stat_in = refs[:2]
        refs = refs[2:]
    if last:
        out_ref, low_ref, lse_ref, scores = refs
    else:
        acc_out, stat_out, scores = refs
    tile = pl.program_id(0)
    half = tile // 3
    part = tile % 3
    is_cont = part == NPROMPT
    prompt = jnp.where(is_cont, meta_ref[half], part)
    rows = pl.ds(pl.multiple_of(prompt * PROMPT_ROWS, PROMPT_ROWS), PROMPT_ROWS)
    if first:
        own, self_seen = tile_masks(meta_ref, half, is_cont)
    bias = block_bias(meta_ref, is_cont, first_block, blocks)
    scale = score_scale * LOG2E
    k_width = KV_HEADS // 2 * HEAD_DIM
    for pair in range(2):
        lanes = pl.ds(pair * 128, 128)
        v_lanes = pl.ds(k_width + pair * 128, 128)
        q = stack_heads(q_ref[:, pair * 256 : (pair + 1) * 256]).astype(bf16)
        if first:
            s_self = jnp.where(self_seen, dot_nt(self_ref[0, :, lanes], q), masked_score)
            top = jnp.max(s_self, axis=0, keepdims=True)
        else:
            old = stat_in[0, pair, :1, :]
            top = old
        for k in range(blocks):
            s = dot_nt(kv_refs[k][rows, lanes], q)
            if first:
                s = jnp.where(own, s, masked_score)
            scores[pl.ds(k * PROMPT_ROWS, PROMPT_ROWS), :] = s
            top = jnp.maximum(top, jnp.max(s, axis=0, keepdims=True) + bias[k])
        top2 = top * scale
        if first:
            p = jnp.exp2(s_self * scale - top2)
            total = jnp.sum(p, axis=0, keepdims=True)
            acc = dot(jnp.transpose(self_ref[0, :, v_lanes]), p.astype(bf16))
        else:
            factor = jnp.exp2(old * scale - top2)
            total = stat_in[0, pair, 1:2, :] * factor
            acc = acc_in[0, pair] * factor
        for k in range(blocks):
            s = scores[pl.ds(k * PROMPT_ROWS, PROMPT_ROWS), :]
            p = jnp.exp2(s * scale - (top2 - bias[k]))
            total = total + jnp.sum(p, axis=0, keepdims=True)
            acc = acc + dot(jnp.transpose(kv_refs[k][rows, v_lanes]), p.astype(bf16))
        if last:
            out = unstack_heads(jnp.transpose(acc / total))
            out_ref[:, pair * 256 : (pair + 1) * 256] = out
            low_ref[:, pair * 256 : (pair + 1) * 256] = out.astype(bf16)
            lse = top2 + jnp.log2(total)
            for head in range(4):
                lse_ref[pl.ds(pair * 4 + head, 1), :] = lse[
                    :, head * PROMPT_DEV : (head + 1) * PROMPT_DEV
                ]
        else:
            acc_out[0, pair] = acc
            stat_out[0, pair, :1, :] = top
            stat_out[0, pair, 1:2, :] = total


def attend_back_kernel(first_block, blocks, first, last, meta_ref, q_ref, do_ref, out_ref, lse_ref, *refs):
    kv_refs, refs = refs[:blocks], refs[blocks:]
    if last:
        self_ref, cos_ref, sin_ref = refs[:3]
        refs = refs[3:]
    if not first:
        dq_in, refs = refs[0], refs[1:]
    dkv_refs, refs = refs[:blocks], refs[blocks:]
    if last:
        dq_ref, dself_ref, acc = refs
    else:
        dq_out, acc = refs
    tile = pl.program_id(0)
    half = tile // 3
    part = tile % 3
    is_cont = part == NPROMPT
    prompt = jnp.where(is_cont, meta_ref[half], part)
    start = pl.multiple_of(prompt * PROMPT_ROWS, PROMPT_ROWS)
    rows = pl.ds(start, PROMPT_ROWS)
    if last:
        own, self_seen = tile_masks(meta_ref, half, is_cont)
    bias = block_bias(meta_ref, is_cont, first_block, blocks)
    scale = score_scale * LOG2E
    k_width = KV_HEADS // 2 * HEAD_DIM

    @pl.when(tile == 0)
    def _():
        acc[...] = jnp.zeros_like(acc)

    for pair in range(2):
        lanes = pl.ds(pair * 128, 128)
        v_lanes = pl.ds(k_width + pair * 128, 128)
        cut = slice(pair * 256, (pair + 1) * 256)
        q = stack_heads(q_ref[:, cut]).astype(bf16)
        do_wide = stack_heads(do_ref[:, cut])
        delta = row_of(do_wide * stack_heads(out_ref[:, cut]))
        do = do_wide.astype(bf16)
        lse = jnp.concatenate(
            [lse_ref[pl.ds(pair * 4 + head, 1), :] for head in range(4)], axis=1
        )
        dq = jnp.zeros((128, 4 * PROMPT_DEV), f32) if first else dq_in[0, pair]
        for k in range(blocks):
            key, value = kv_refs[k][rows, lanes], kv_refs[k][rows, v_lanes]
            s = dot_nt(key, q)
            if last:
                s = jnp.where(own, s, masked_score)
            p = jnp.exp2(s * scale - (lse - bias[k]))
            ds = (p * (dot_nt(value, do) - delta)).astype(bf16)
            dq = dq + dot(jnp.transpose(key), ds)
            acc[k, rows, lanes] += dot(ds, q)
            acc[k, rows, v_lanes] += dot(p.astype(bf16), do)
        if last:
            key, value = self_ref[0, :, lanes], self_ref[0, :, v_lanes]
            s = jnp.where(self_seen, dot_nt(key, q), masked_score)
            p = jnp.exp2(s * scale - lse)
            ds = (p * (dot_nt(value, do) - delta)).astype(bf16)
            dq = dq + dot(jnp.transpose(key), ds)
            dself_ref[0, :, lanes] = dot(ds, q) * score_scale
            dself_ref[0, :, v_lanes] = dot(p.astype(bf16), do)
            wide = unstack_heads(jnp.transpose(dq)) * score_scale
            for group in range(2):
                turned = turn(wide[:, group * 128 : (group + 1) * 128], cos_ref[...], -sin_ref[...])
                lo = pair * 256 + group * 128
                dq_ref[:, lo : lo + 128] = turned.astype(bf16)
        else:
            dq_out[0, pair] = dq

    @pl.when(tile == pl.num_programs(0) - 1)
    def _():
        for k in range(blocks):
            dkv_refs[k][:, :k_width] = (acc[k, :, :k_width] * score_scale).astype(bf16)
            dkv_refs[k][:, k_width:] = acc[k, :, k_width:].astype(bf16)


def turn(values, cosine, sine_signed):
    lane = lax.broadcasted_iota(jnp.int32, values.shape, 1) % HEAD_DIM
    swapped = jnp.where(
        lane < HEAD_DIM // 2,
        pltpu.roll(values, 128 - HEAD_DIM // 2, 1),
        pltpu.roll(values, HEAD_DIM // 2, 1),
    )
    return values * cosine + swapped * sine_signed


VMEM_LIMIT = 40 * 1024 * 1024
SMALL_LIMIT = 24 * 1024 * 1024
WHOLE_LIMIT = 60 * 1024 * 1024


def whole_spec(array):
    return pl.BlockSpec(
        array.shape, lambda *_: (0,) * array.ndim, pipeline_mode=pl.Buffered(1)
    )


def attend(meta, queries, first_block, kv_blocks, state, cont_kv=None, last=False):
    blocks = len(kv_blocks)
    first = state is None
    rows, q_width = queries.shape
    tiles = rows // PROMPT_DEV
    columns = 4 * PROMPT_DEV
    row_spec = pl.BlockSpec((PROMPT_DEV, q_width), lambda t, meta: (t, 0))
    lse_spec = pl.BlockSpec((HEADS // 2, PROMPT_DEV), lambda t, meta: (0, t))
    acc_spec = pl.BlockSpec((1, 2, 128, columns), lambda t, meta: (t, 0, 0, 0))
    stat_spec = pl.BlockSpec((1, 2, 8, columns), lambda t, meta: (t, 0, 0, 0))
    pairs = rows * HEADS // 2 * blocks * PROMPT_ROWS
    in_specs = [row_spec] + [whole_spec(b) for b in kv_blocks]
    operands = [meta, queries, *kv_blocks]
    if first:
        in_specs.append(pl.BlockSpec((1,) + cont_kv.shape[1:], lambda t, meta: (t // 3, 0, 0)))
        operands.append(cont_kv)
    else:
        in_specs += [acc_spec, stat_spec]
        operands += list(state)
    if last:
        out_specs = [row_spec, row_spec, lse_spec]
        out_shape = [
            jax.ShapeDtypeStruct((rows, q_width), f32),
            jax.ShapeDtypeStruct((rows, q_width), bf16),
            jax.ShapeDtypeStruct((HEADS // 2, rows), f32),
        ]
    else:
        out_specs = [acc_spec, stat_spec]
        out_shape = [
            jax.ShapeDtypeStruct((tiles, 2, 128, columns), f32),
            jax.ShapeDtypeStruct((tiles, 2, 8, columns), f32),
        ]
    return pl.pallas_call(
        functools.partial(attend_kernel, first_block, blocks, first, last),
        grid_spec=pltpu.PrefetchScalarGridSpec(
            num_scalar_prefetch=1,
            grid=(tiles,),
            in_specs=in_specs,
            out_specs=out_specs,
            scratch_shapes=[pltpu.VMEM((blocks * PROMPT_ROWS, columns), f32)],
        ),
        out_shape=out_shape,
        compiler_params=pltpu.CompilerParams(vmem_limit_bytes=VMEM_LIMIT),
        cost_estimate=pl.CostEstimate(
            flops=48 * 64 * pairs, bytes_accessed=12 << 20, transcendentals=pairs
        ),
        name="attend",
    )(*operands)


def attend_back(meta, queries, grads, mixed, lse, first_block, kv_blocks, dq, own=None):
    blocks = len(kv_blocks)
    first, last = dq is None, own is not None
    rows, q_width = queries.shape
    tiles = rows // PROMPT_DEV
    columns = 4 * PROMPT_DEV
    row_spec = pl.BlockSpec((PROMPT_DEV, q_width), lambda t, meta: (t, 0))
    lse_spec = pl.BlockSpec((HEADS // 2, PROMPT_DEV), lambda t, meta: (0, t))
    dq_spec = pl.BlockSpec((1, 2, 128, columns), lambda t, meta: (t, 0, 0, 0))
    block = kv_blocks[0]
    pairs = rows * HEADS // 2 * blocks * PROMPT_ROWS
    in_specs = [row_spec, row_spec, row_spec, lse_spec] + [whole_spec(b) for b in kv_blocks]
    operands = [meta, queries, grads, mixed, lse, *kv_blocks]
    out_specs = [whole_spec(b) for b in kv_blocks]
    out_shape = [jax.ShapeDtypeStruct(b.shape, bf16) for b in kv_blocks]
    if last:
        cont_kv, cosine, sine = own
        self_spec = pl.BlockSpec((1,) + cont_kv.shape[1:], lambda t, meta: (t // 3, 0, 0))
        turn_spec = pl.BlockSpec((PROMPT_DEV, 128), lambda t, meta: (t, 0))
        in_specs += [self_spec, turn_spec, turn_spec]
        operands += [cont_kv, cosine, sine]
        out_specs += [row_spec, self_spec]
        out_shape += [
            jax.ShapeDtypeStruct((rows, q_width), bf16),
            jax.ShapeDtypeStruct(cont_kv.shape, f32),
        ]
    else:
        out_specs.append(dq_spec)
        out_shape.append(jax.ShapeDtypeStruct((tiles, 2, 128, columns), f32))
    if not first:
        in_specs.append(dq_spec)
        operands.append(dq)
    return pl.pallas_call(
        functools.partial(attend_back_kernel, first_block, blocks, first, last),
        grid_spec=pltpu.PrefetchScalarGridSpec(
            num_scalar_prefetch=1,
            grid=(tiles,),
            in_specs=in_specs,
            out_specs=out_specs,
            scratch_shapes=[pltpu.VMEM((blocks,) + block.shape, f32)],
        ),
        out_shape=out_shape,
        compiler_params=pltpu.CompilerParams(vmem_limit_bytes=VMEM_LIMIT),
        cost_estimate=pl.CostEstimate(
            flops=110 * 64 * pairs, bytes_accessed=16 << 20, transcendentals=pairs
        ),
        name="attend_back",
    )(*operands)


def core_pieces(columns, core, dp_size):
    width = columns.shape[-1] // (2 * dp_size)
    pieces = []
    for s in range(dp_size):
        lo = 2 * s * width
        pieces.append(
            jnp.where(core == 0, columns[:, lo : lo + width], columns[:, lo + width : lo + 2 * width])
        )
    return pieces


def core_heads(columns, core, dp_size):
    q, k = HEADS * HEAD_DIM, KV_HEADS * HEAD_DIM
    cuts = [columns[:, :q], columns[:, q : q + k], columns[:, q + k :]]
    return jnp.concatenate([p for cut in cuts for p in core_pieces(cut, core, dp_size)], axis=1)


def all_heads(mine, other, core, dp_size):
    first, second = jnp.where(core == 0, mine, other), jnp.where(core == 0, other, mine)
    q, k = HEADS // 2 * HEAD_DIM, KV_HEADS // 2 * HEAD_DIM
    pieces = []
    for lo, size in ((0, q), (q, k), (q + k, k)):
        width = size // dp_size
        for s in range(dp_size):
            cut = slice(lo + s * width, lo + (s + 1) * width)
            pieces += [first[:, cut], second[:, cut]]
    return jnp.concatenate(pieces, axis=1)


def cast_kernel(dp_size, meta_ref, weight_ref, out_ref):
    out_ref[...] = core_heads(weight_ref[...], meta_ref[0], dp_size).astype(bf16)


def cast_core_columns(core, weight, dp_size):
    rows, columns = weight.shape
    tile = rows // 4
    return pl.pallas_call(
        functools.partial(cast_kernel, dp_size),
        grid_spec=pltpu.PrefetchScalarGridSpec(
            num_scalar_prefetch=1,
            grid=(4,),
            in_specs=[pl.BlockSpec((tile, columns), lambda t, meta: (t, 0))],
            out_specs=pl.BlockSpec((tile, columns // 2), lambda t, meta: (t, 0)),
        ),
        out_shape=jax.ShapeDtypeStruct((rows, columns // 2), bf16),
        compiler_params=pltpu.CompilerParams(vmem_limit_bytes=SMALL_LIMIT),
        cost_estimate=pl.CostEstimate(
            flops=rows * columns, bytes_accessed=5 * rows * columns, transcendentals=0
        ),
        name="cast_core_columns",
    )(core[None], weight)


def project_kernel(shards, meta_ref, own_ref, other_ref, *refs):
    weights = refs[:shards]
    cos_ref, sin_ref, q_ref, prompt_ref, cont_ref = refs[shards:]
    half = pl.program_id(0)
    depth = weights[0].shape[0]
    q_width = q_ref.shape[-1]
    k_width = cont_ref.shape[-1] // 2
    cosine, sine = cos_ref[...], sin_ref[...]

    def run(x_ref):
        xs = []
        for k in range(shards):
            start = pl.multiple_of((meta_ref[5] + k) % shards * depth, depth)
            xs.append(x_ref[:, pl.ds(start, depth)])
        for lo in range(0, q_width + 2 * k_width, 128):
            if lo % 256 == 0:
                out = sum(dot(x, w[:, lo : lo + 256]) for x, w in zip(xs, weights))
            piece = out[:, lo % 256 : lo % 256 + 128]
            if lo < q_width + k_width:
                piece = turn(piece, cosine, sine)
            piece = piece.astype(bf16)
            if lo < q_width:
                q_ref[:, lo : lo + 128] = piece
            else:
                at = lo - q_width
                for g in range(NPROMPT):
                    rows = piece[g * PROMPT_DEV : (g + 1) * PROMPT_DEV]
                    prompt_ref[g, 0, :, at : at + 128] = rows
                cont_ref[0, :, at : at + 128] = piece[PROMPT_ROWS:]

    pl.when(half == 0)(lambda: run(own_ref))
    pl.when(half == 1)(lambda: run(other_ref))


def project(meta, own, other, weights, cosine, sine):
    rows, width = own.shape
    columns = weights[0].shape[1]
    kv_width = columns // 2
    turn_spec = pl.BlockSpec((rows, 128), lambda h, meta: (h, 0))
    return pl.pallas_call(
        functools.partial(project_kernel, len(weights)),
        grid_spec=pltpu.PrefetchScalarGridSpec(
            num_scalar_prefetch=1,
            grid=(2,),
            in_specs=[whole_spec(a) for a in (own, other, *weights)] + [turn_spec] * 2,
            out_specs=[
                pl.BlockSpec((rows, columns - kv_width), lambda h, meta: (h, 0)),
                pl.BlockSpec((NPROMPT, 1, PROMPT_DEV, kv_width), lambda h, meta: (0, h, 0, 0)),
                pl.BlockSpec((1, CLEN, kv_width), lambda h, meta: (h, 0, 0)),
            ],
        ),
        out_shape=[
            jax.ShapeDtypeStruct((2 * rows, columns - kv_width), bf16),
            jax.ShapeDtypeStruct((NPROMPT, 2, PROMPT_DEV, kv_width), bf16),
            jax.ShapeDtypeStruct((2, CLEN, kv_width), bf16),
        ],
        compiler_params=pltpu.CompilerParams(vmem_limit_bytes=SMALL_LIMIT),
        cost_estimate=pl.CostEstimate(
            flops=4 * rows * width * columns, bytes_accessed=8 << 20, transcendentals=0
        ),
        name="project",
    )(meta, own, other, *weights, cosine, sine)


def projected_grad_kernel(dq_ref, *refs):
    dkv_refs = refs[:3]
    dself_ref, cos_ref, sin_ref, out_ref = refs[3:]
    q_width = dq_ref.shape[-1]
    k_width = dself_ref.shape[-1] // 2
    out_ref[:, :q_width] = dq_ref[...]
    parts = [sum(ref[g, 0].astype(f32) for ref in dkv_refs) for g in range(NPROMPT)]
    dkv = jnp.concatenate(parts + [dself_ref[0]], axis=0)
    cosine, sine = cos_ref[...], -sin_ref[...]
    for lo in range(0, 2 * k_width, 128):
        piece = dkv[:, lo : lo + 128]
        if lo < k_width:
            piece = turn(piece, cosine, sine)
        out_ref[:, q_width + lo : q_width + lo + 128] = piece.astype(bf16)


def projected_grad(dq, dkv_parts, dself, cosine, sine):
    rows2, q_width = dq.shape
    rows = rows2 // 2
    kv_width = dself.shape[-1]
    dkv_parts = [p.reshape(NPROMPT, 2, PROMPT_DEV, kv_width) for p in dkv_parts]
    turn_spec = pl.BlockSpec((rows, 128), lambda h: (h, 0))
    return pl.pallas_call(
        projected_grad_kernel,
        grid=(2,),
        in_specs=[pl.BlockSpec((rows, q_width), lambda h: (h, 0))]
        + [pl.BlockSpec((NPROMPT, 1, PROMPT_DEV, kv_width), lambda h: (0, h, 0, 0))] * 3
        + [pl.BlockSpec((1, CLEN, kv_width), lambda h: (h, 0, 0)), turn_spec, turn_spec],
        out_specs=pl.BlockSpec((rows, q_width + kv_width), lambda h: (h, 0)),
        out_shape=jax.ShapeDtypeStruct((rows2, q_width + kv_width), bf16),
        compiler_params=pltpu.CompilerParams(vmem_limit_bytes=SMALL_LIMIT),
        cost_estimate=pl.CostEstimate(
            flops=20 * rows2 * kv_width, bytes_accessed=6 << 20, transcendentals=0
        ),
        name="projected_grad",
    )(dq, *dkv_parts, dself, cosine, sine)


def order_kernel(meta_ref, qkv_ref, out_ref, parts_ref):
    top = qkv_ref.shape[1]
    shards = qkv_ref.shape[0]
    rows = top + out_ref.shape[1]
    for s in range(shards):
        parts_ref[0, s * rows : s * rows + top, :] = qkv_ref[s]
        parts_ref[0, s * rows + top : (s + 1) * rows, :] = out_ref[s]


def order_parts(meta, qkv, out, chips, dp_size):
    width = qkv.shape[1]
    qkv = qkv.reshape(dp_size, -1, width)
    out = out.reshape(dp_size, -1, width)
    rows = [a.shape[1] // chips for a in (qkv, out)]
    return pl.pallas_call(
        order_kernel,
        grid_spec=pltpu.PrefetchScalarGridSpec(
            num_scalar_prefetch=1,
            grid=(chips,),
            in_specs=[
                pl.BlockSpec((dp_size, r, width), lambda k, meta: (0, meta[META + k], 0))
                for r in rows
            ],
            out_specs=pl.BlockSpec((1, dp_size * sum(rows), width), lambda k, meta: (k, 0, 0)),
        ),
        out_shape=jax.ShapeDtypeStruct((chips, dp_size * sum(rows), width), bf16),
        compiler_params=pltpu.CompilerParams(vmem_limit_bytes=SMALL_LIMIT),
        cost_estimate=pl.CostEstimate(
            flops=qkv.size, bytes_accessed=6 * qkv.size, transcendentals=0
        ),
        name="order_parts",
    )(meta, qkv, out)


def step_kernel(dp_size, grad_scale, meta_ref, grad_ref, *refs):
    qkv, out, step_ref = refs[:3], refs[3:6], refs[6]
    top = qkv[0].shape[0]
    grad = grad_ref[...].astype(f32)
    args = [core_heads(ref[...], meta_ref[4], dp_size) for ref in qkv]
    step_ref[:top, :] = adamw(*args, grad[:top], grad_scale, decay_rate)[0].astype(bf16)
    args = [ref[...] for ref in out]
    step_ref[top:, :] = adamw(*args, grad[top:], grad_scale, decay_rate)[0].astype(bf16)


def shard_step(meta, grad, qkv, out, chips, dp_size, grad_scale):
    qkv_rows, out_rows = qkv[0].shape[0] // chips, out[0].shape[0] // (2 * chips)
    width = grad.shape[1]
    return pl.pallas_call(
        functools.partial(step_kernel, dp_size, grad_scale),
        grid_spec=pltpu.PrefetchScalarGridSpec(
            num_scalar_prefetch=1,
            grid=(1,),
            in_specs=[whole_spec(grad)]
            + [pl.BlockSpec((qkv_rows, 2 * width), lambda t, meta: (meta[6], 0))] * 3
            + [pl.BlockSpec((out_rows, width), lambda t, meta: (meta[4] * chips + meta[6], 0))] * 3,
            out_specs=whole_spec(grad),
        ),
        out_shape=jax.ShapeDtypeStruct(grad.shape, bf16),
        compiler_params=pltpu.CompilerParams(vmem_limit_bytes=WHOLE_LIMIT),
        cost_estimate=pl.CostEstimate(
            flops=20 * grad.size, bytes_accessed=16 * grad.size, transcendentals=grad.size
        ),
        name="shard_step",
    )(meta, grad, *qkv, *out)


def optimizer_kernel(blocks, dp_size, grad_scale, spill, meta_ref, *refs):
    mine, refs = refs[:blocks], refs[blocks:]
    other, refs = refs[:blocks], refs[blocks:]
    qkv, out = refs[:3], refs[3:6]
    refs = refs[6 + spill :]
    step_qkv, mean_qkv, square_qkv, step_out, mean_out, square_out = refs
    core = meta_ref[4]
    top = qkv[0].shape[0]

    def run(mine_ref, other_ref):
        for shift in range(dp_size):
            a, b = mine_ref[shift], other_ref[shift]
            whole = all_heads(a[:top], b[:top], core, dp_size).astype(f32)
            low = jnp.concatenate(
                [
                    jnp.where(core == 0, a[top:], b[top:])[None],
                    jnp.where(core == 0, b[top:], a[top:])[None],
                ],
                axis=0,
            ).astype(f32)
            if shift == 0:
                whole, mean, square = adamw(*[r[...] for r in qkv], whole, grad_scale, decay_rate)
                whole = whole.astype(bf16).astype(f32)
                mean_qkv[...] = mean
                square_qkv[...] = square
                low, mean, square = adamw(*[r[...] for r in out], low, grad_scale, decay_rate)
                low = low.astype(bf16).astype(f32)
                mean_out[...] = mean
                square_out[...] = square
            at = (meta_ref[5] + shift) % dp_size
            step_qkv[pl.ds(at, 1)] = whole[None]
            step_out[pl.ds(at, 1)] = low[None]

    for k in range(blocks):
        if blocks == 1:
            run(mine[k], other[k])
        else:
            pl.when(pl.program_id(0) == k)(functools.partial(run, mine[k], other[k]))


def optimize(meta, first_block, mine, other, qkv, out, buffers, chips, dp_size, grad_scale):
    blocks = len(mine)
    spill = 0 if buffers is None else 6
    qkv_rows = qkv[0].shape[0] // chips
    out_rows = out[0].shape[0] // (2 * chips)
    width = out[0].shape[1]
    out = [a.reshape(2, a.shape[0] // 2, width) for a in out]

    def at_chip(block, meta):
        return meta[META + first_block + block]

    own_qkv = pl.BlockSpec((qkv_rows, 2 * width), lambda b, meta: (at_chip(b, meta), 0))
    own_out = pl.BlockSpec((2, out_rows, width), lambda b, meta: (0, at_chip(b, meta), 0))
    step_qkv = pl.BlockSpec(
        (dp_size, qkv_rows, 2 * width), lambda b, meta: (0, at_chip(b, meta), 0)
    )
    step_out = pl.BlockSpec(
        (dp_size, 2, out_rows, width), lambda b, meta: (0, 0, at_chip(b, meta), 0)
    )
    shapes = [
        (dp_size,) + qkv[0].shape,
        qkv[0].shape,
        qkv[0].shape,
        (dp_size,) + out[0].shape,
        out[0].shape,
        out[0].shape,
    ]
    specs = [step_qkv, own_qkv, own_qkv, step_out, own_out, own_out]
    first = 1 + 2 * blocks + 6
    return pl.pallas_call(
        functools.partial(optimizer_kernel, blocks, dp_size, grad_scale, spill),
        grid_spec=pltpu.PrefetchScalarGridSpec(
            num_scalar_prefetch=1,
            grid=(blocks,),
            in_specs=[whole_spec(a) for a in (*mine, *other)]
            + [own_qkv] * 3
            + [own_out] * 3
            + [pl.BlockSpec(memory_space=pl.ANY)] * spill,
            out_specs=specs,
        ),
        out_shape=[jax.ShapeDtypeStruct(shape, f32) for shape in shapes],
        input_output_aliases={first + k: k for k in range(spill)},
        compiler_params=pltpu.CompilerParams(vmem_limit_bytes=WHOLE_LIMIT),
        cost_estimate=pl.CostEstimate(
            flops=blocks * qkv_rows * width * 60,
            bytes_accessed=blocks * qkv_rows * width * 90,
            transcendentals=blocks * qkv_rows * width * 3,
        ),
        name="optimize",
    )(meta, *mine, *other, *qkv, *out, *(buffers or ()))


def expert_kernel(count, tok, spill, meta_ref, *refs):
    x_refs, refs = refs[:count], refs[count:]
    cot_refs, refs = refs[:count], refs[count:]
    gate_ups, downs = refs[:2], refs[2:4]
    refs = refs[4 + spill :]
    mix_refs, refs = refs[:count], refs[count:]
    grad_refs, refs = refs[:count], refs[count:]
    x_all, cot_all, act_all, dgu_all = refs
    width = x_all.shape[-1]

    def run(x_ref, cot_ref, mix_ref, grad_ref):
        x = x_ref[:tok, :]
        cot = cot_ref[...]
        x_all[...] = x
        cot_all[...] = cot
        extra = x_ref[tok:, :].astype(f32)
        extra = extra[:, :tok] + extra[:, tok : 2 * tok]
        row = lax.broadcasted_iota(jnp.int32, extra.shape, 0)
        gates = jnp.zeros_like(extra)
        for e in range(2):
            mine = row == meta_ref[2 + e]
            weight = jnp.sum(jnp.where(mine, extra, 0.0), axis=0, keepdims=True)
            weight = jnp.transpose(jnp.broadcast_to(weight, (128, tok)))
            weight = jnp.concatenate([weight, weight], axis=1)
            gate_grad = jnp.zeros((tok, 1), f32)
            for lo in range(0, EXP_FF, 256):
                hi = lo + 256
                gate = dot(x, gate_ups[e][:, lo:hi])
                up = dot(x, gate_ups[e][:, EXP_FF + lo : EXP_FF + hi])
                dact = dot_nt(cot, downs[e][lo:hi, :])
                sig = 0.5 * jnp.tanh(0.5 * gate) + 0.5
                silu = gate * sig
                act = silu * up
                gate_grad = gate_grad + jnp.sum(act * dact, axis=-1, keepdims=True)
                act_all[:, e * EXP_FF + lo : e * EXP_FF + hi] = (act * weight).astype(bf16)
                dact = dact * weight
                dgate = dact * up * (sig + silu * (1.0 - sig))
                at = 2 * e * EXP_FF
                dgu_all[:, at + lo : at + hi] = dgate.astype(bf16)
                dgu_all[:, at + EXP_FF + lo : at + EXP_FF + hi] = (dact * silu).astype(bf16)
            gate_row = jnp.transpose(jnp.broadcast_to(gate_grad, (tok, 128)))[:1, :]
            gates = jnp.where(mine, gate_row, gates)
        acts = [act_all[:, e * EXP_FF : (e + 1) * EXP_FF] for e in range(2)]
        dgus = [dgu_all[:, 2 * e * EXP_FF : 2 * (e + 1) * EXP_FF] for e in range(2)]
        for lo in range(0, width, 256):
            mix = sum(dot(acts[e], downs[e][:, lo : lo + 256]) for e in range(2))
            mix_ref[:, lo : lo + 256] = mix.astype(bf16)
        for lo in range(0, width, 256):
            grad = sum(dot_nt(dgus[e], gate_ups[e][lo : lo + 256, :]) for e in range(2))
            grad_ref[:tok, lo : lo + 256] = grad.astype(bf16)
        high = gates.astype(bf16)
        grad_ref[tok:, :tok] = high
        grad_ref[tok:, tok : 2 * tok] = (gates - high.astype(f32)).astype(bf16)
        grad_ref[tok:, 2 * tok :] = jnp.zeros((extra.shape[0], width - 2 * tok), bf16)

    for b in range(count):
        body = functools.partial(run, x_refs[b], cot_refs[b], mix_refs[b], grad_refs[b])
        if count == 1:
            body()
        else:
            pl.when(pl.program_id(0) == b)(body)


def run_experts(meta, x_blocks, cot_blocks, weights, buffers, place, total):
    count = len(x_blocks)
    packed, width = x_blocks[0].shape
    tok = cot_blocks[0].shape[0]
    rows = count * tok
    spill = 0 if buffers is None else 4
    any_spec = pl.BlockSpec(memory_space=pl.ANY)
    stream_width = [width, width, 2 * EXP_FF, 4 * EXP_FF]
    stream = [pl.BlockSpec((tok, w), lambda g, ids: (place + g, 0)) for w in stream_width]
    out = pl.pallas_call(
        functools.partial(expert_kernel, count, tok, spill),
        grid_spec=pltpu.PrefetchScalarGridSpec(
            num_scalar_prefetch=1,
            grid=(count,),
            in_specs=[
                whole_spec(a) for a in (*x_blocks, *cot_blocks, *weights)
            ]
            + [any_spec] * spill,
            out_specs=[whole_spec(c) for c in cot_blocks]
            + [whole_spec(x) for x in x_blocks]
            + stream,
        ),
        out_shape=[jax.ShapeDtypeStruct(c.shape, bf16) for c in cot_blocks]
        + [jax.ShapeDtypeStruct(x.shape, bf16) for x in x_blocks]
        + [jax.ShapeDtypeStruct((total, w), bf16) for w in stream_width],
        input_output_aliases={1 + 2 * count + 4 + k: 2 * count + k for k in range(spill)},
        compiler_params=pltpu.CompilerParams(vmem_limit_bytes=VMEM_LIMIT),
        cost_estimate=pl.CostEstimate(
            flops=2 * 2 * rows * width * EXP_FF * 6,
            bytes_accessed=rows * width * 20 + 6 * width * width,
            transcendentals=2 * rows * EXP_FF,
        ),
        name="experts",
    )(meta, *x_blocks, *cot_blocks, *weights, *(buffers or ()))
    return out[:count], out[count : 2 * count], out[2 * count :]


def per_device(
    ring,
    tokens,
    cotangent,
    routes,
    cont_group,
    attn_gain,
    qkv_weight,
    out_weight,
    ffn_gain,
    router_weight,
    gate_up_weight,
    down_weight,
    mean_attn_gain,
    mean_qkv_weight,
    mean_out_weight,
    mean_ffn_gain,
    mean_router_weight,
    mean_gate_up_weight,
    mean_down_weight,
    square_attn_gain,
    square_qkv_weight,
    square_out_weight,
    square_ffn_gain,
    square_router_weight,
    square_gate_up_weight,
    square_down_weight,
):
    chips = ring.chips
    dp_size = lax.axis_size("dp")
    dp = lax.axis_index("dp")
    chip = lax.axis_index("chip")
    core = lax.axis_index("core")
    members = 2 * chips
    tok_count, width = tokens.shape
    experts = router_weight.shape[1]
    capacity = 5 * tok_count * TOPK // (4 * experts)
    prompt_len = PROMPT_DEV * members
    core_heads = HEADS // 2
    core_kv = KV_HEADS // 2
    q_width = core_heads * HEAD_DIM
    k_width = core_kv * HEAD_DIM

    member_pair = jnp.stack([2 * chip + core, 2 * chip + 1 - core])
    groups = jnp.concatenate([cont_group, swap(cont_group)])
    own_place = jnp.stack([core, dp, chip, 0])
    meta = jnp.concatenate([groups, member_pair, own_place, ring.chips_from(chip)])

    tokens = split_rows(tokens)
    cotangent = split_rows(cotangent)
    routes = split_rows(routes)
    tok_float = tokens.astype(f32)

    qkv_core = cast_core_columns(core, qkv_weight, dp_size)
    small = jnp.concatenate([attn_gain[None], ffn_gain[None], router_weight.T], axis=0).astype(bf16)
    small = gather_dp(small, 1)
    qkv_shards = dp_shards(qkv_core)
    gain_attn = small[0].astype(f32)
    gain_ffn = small[1].astype(f32)
    proj_router_t = small[2:]

    scale_attn = lax.rsqrt(jnp.mean(tok_float * tok_float, axis=-1, keepdims=True) + norm_eps)
    attn_in = (tok_float * scale_attn * gain_attn).astype(bf16)
    within = jnp.arange(PROMPT_DEV, dtype=jnp.int32)
    prompt_pos = member_pair[:, None] * PROMPT_DEV + within
    cont_pos = jnp.broadcast_to(prompt_len + within, (2, CLEN))
    position = jnp.stack([prompt_pos, prompt_pos, cont_pos], axis=1).reshape(-1)
    half_dim = HEAD_DIM // 2
    frequency = jnp.exp(
        jnp.arange(half_dim, dtype=f32) * (-2.0 * math.log(10000.0) / HEAD_DIM)
    )
    angles = position.astype(f32)[:, None] * frequency[None, :]
    cosine_part, sine_part = jnp.cos(angles), jnp.sin(angles)
    cosine = jnp.concatenate([cosine_part] * 4, axis=1)
    sine_signed = jnp.concatenate([-sine_part, sine_part] * 2, axis=1)
    cot_ring = RingGather(ring, cotangent)
    cot_ring.step()
    attn_in = after(attn_in, cot_ring.ends())
    half_rows = out_weight.shape[0] // 2
    late_gate_up, late_down, late_out = after(
        (gate_up_weight[0], down_weight[0], out_weight), cot_ring.ends()
    )
    out_core = pick_core(late_out[:half_rows], late_out[half_rows:]).astype(bf16)
    own_gate_up = lax.all_gather(late_gate_up.astype(bf16), "dp", axis=0, tiled=True)
    own_down = lax.all_gather(late_down.astype(bf16), "dp", axis=0, tiled=True)
    expert_weights = [own_gate_up, swap(own_gate_up), own_down, swap(own_down)]
    cot_ring.step(cosine, sine_signed)
    attn_other = swap(attn_in)
    attn_in2 = jnp.concatenate([attn_in, attn_other], axis=0)
    qkv_shards = after(qkv_shards, cot_ring.ends())
    while cot_ring.place < ring.half - 1:
        cot_ring.step()
    rows2 = 2 * tok_count
    queries, prompt_kv, cont_kv = project(
        meta, attn_in, attn_other, qkv_shards, cosine, sine_signed
    )
    prompt_kv = prompt_kv.reshape(2 * PROMPT_ROWS, 2 * k_width)
    prompt_kv = after(prompt_kv, cot_ring.ends())
    proj_out = gather_dp(after(out_core, qkv_shards), 0)
    kv_blocks, state = {}, None
    for arrived in ring.gather_steps(prompt_kv):
        kv_blocks.update(arrived)
        if 2 in arrived:
            proj_qkv = join_dp(after(qkv_shards, state), 0)
        if ring.half in arrived:
            state, proj_qkv = after((state, proj_qkv))
        state = attend(
            meta,
            queries,
            ring.by_distance.index(min(arrived)),
            list(arrived.values()),
            state,
            cont_kv if 0 in arrived else None,
            ring.half in arrived,
        )
    mixed, mixed_low, lse = state
    cot_blocks = cot_ring.blocks

    part = dot(mixed_low, proj_out)
    other = swap(part[tok_count:].astype(bf16))
    hidden = tok_float + part[:tok_count] + other.astype(f32)
    scale_ffn = lax.rsqrt(jnp.mean(hidden * hidden, axis=-1, keepdims=True) + norm_eps)
    ffn_in = (hidden * scale_ffn * gain_ffn).astype(bf16)
    logits = dot_nt(proj_router_t, ffn_in)
    expert_ids = jnp.arange(experts, dtype=jnp.int32)
    hot = jnp.any(routes.T[None] == expert_ids[:, None, None], axis=1)
    hot_float = hot.astype(f32)
    shown = jnp.where(hot, logits, masked_score)
    raised = jnp.where(hot, jnp.exp(shown - jnp.max(shown, axis=0, keepdims=True)), 0.0)
    gate_probs = raised / jnp.sum(raised, axis=0, keepdims=True)
    spot = jnp.arange(tok_count, dtype=jnp.int32)
    spot = jnp.where(
        spot < PROMPT_ROWS, (spot % PROMPT_DEV) * NPROMPT + spot // PROMPT_DEV, spot
    )
    earlier = (spot[:, None] < spot[None, :]).astype(bf16)
    placed = dot(hot.astype(bf16), earlier)
    kept = hot & (placed < capacity)
    pair_weight = jnp.where(kept, gate_probs, 0.0)
    weight_high = lax.reduce_precision(pair_weight, 8, 7)
    weight_rows = jnp.concatenate([weight_high, pair_weight - weight_high], axis=1).astype(bf16)
    weight_rows = jnp.pad(weight_rows, ((0, 0), (0, width - 2 * tok_count)))
    packed = jnp.concatenate([ffn_in, weight_rows], axis=0)

    total_rows = chips * tok_count
    mix_parts, grad_parts = {}, {}
    buffers = None
    packed = after(packed, cot_ring.ends())
    ffn_ring = RingGather(ring, packed)
    arrived, place = {0: packed}, 0
    while arrived:
        later = {}
        if ffn_ring.place < ring.half:
            later = ffn_ring.step(*(buffers or ()))
        if ring.half in later:
            cot_ring.step(ffn_ring.before)
        mixes, grads, buffers = run_experts(
            meta,
            list(arrived.values()),
            [cot_blocks[r] for r in arrived],
            expert_weights,
            buffers,
            place,
            total_rows,
        )
        mix_parts.update(zip(arrived, mixes))
        grad_parts.update(zip(arrived, grads))
        place += len(arrived)
        arrived = later

    grad_sum = RingSum(ring, grad_parts[ring.half])
    grad_sum.add(grad_parts)
    x_all, cot_all, act_all, dgu_all = after(buffers, grad_sum.sent)
    other_gate_up = dot_tn(x_all, dgu_all[:, 2 * EXP_FF :]).astype(bf16)
    other_down = dot_tn(act_all[:, EXP_FF:], cot_all).astype(bf16)
    grad_sum.add(grad_parts, other_gate_up, other_down)
    other_gate_up, other_down = after((other_gate_up, other_down), grad_sum.sent)
    other_gate_up, other_down = swap(other_gate_up), swap(other_down)
    while grad_sum.place > 1:
        grad_sum.add(grad_parts, other_gate_up, other_down)
    x_all, cot_all, act_all, dgu_all = after(buffers, grad_sum.sent)
    grad_gate_up = dot_tn(x_all, dgu_all[:, : 2 * EXP_FF]) + other_gate_up.astype(f32)
    grad_gate_up = grad_gate_up.astype(bf16)
    grad_down = dot_tn(act_all[:, :EXP_FF], cot_all) + other_down.astype(f32)
    grad_down = grad_down.astype(bf16)
    grad_packed, grad_gate_up, grad_down = lax.optimization_barrier(
        (grad_sum.finish(grad_parts[0]), grad_gate_up, grad_down)
    )
    mix_sum = RingSum(ring, after(mix_parts[ring.half], grad_sum.arrived()))

    def shards_dp(whole):
        pieces = whole.reshape((dp_size, whole.shape[0] // dp_size) + whole.shape[1:])
        out = [lax.dynamic_index_in_dim(pieces, dp, 0, False)]
        for shift in range(1, dp_size):
            perm = [(k, (k + shift) % dp_size) for k in range(dp_size)]
            part = lax.dynamic_index_in_dim(pieces, (dp + shift) % dp_size, 0, False)
            out.append(lax.ppermute(part, "dp", perm))
        return out

    def sum_of(pieces, *others):
        return sum(piece.astype(f32) for piece in after(pieces, others))


    grad_gate = grad_packed[tok_count:, :tok_count] + grad_packed[tok_count:, tok_count : 2 * tok_count]
    grad_gate = jnp.where(kept, grad_gate, 0.0)
    grad_chosen = gate_probs * (grad_gate - jnp.sum(gate_probs * grad_gate, axis=0, keepdims=True))
    grad_logits = (hot_float * grad_chosen).astype(bf16)
    grad_router_t = dot(grad_logits, ffn_in)
    grad_ffn = grad_packed[:tok_count] + dot_tn(grad_logits, proj_router_t)
    grad_output = cotangent.astype(f32)
    grad_hidden_norm, grad_gain_ffn = norm_back(hidden, scale_ffn, gain_ffn, grad_ffn)
    grad_hidden = grad_output + grad_hidden_norm
    grad_attn = after(grad_hidden.astype(bf16), mix_sum.arrived())
    grad_attn2 = jnp.concatenate([grad_attn, swap(grad_attn)], axis=0)
    grad_mixed = dot_nt(grad_attn2, proj_out).astype(bf16)
    mix_sum.add(mix_parts, grad_mixed)

    grad_scale = (tok_count * dp_size * members) ** (-0.5)

    dq, dkv, dkv_sum = None, (), None
    for turn_no, places in enumerate(ring.groups()[::-1]):
        if turn_no >= 2:
            grad_mixed = after(grad_mixed, dkv_before)
        if 0 in places or (turn_no % 2 == 0 and mix_sum.place > 3):
            grad_mixed = after(grad_mixed, mix_sum.arrived())
            if 0 not in places:
                mix_sum.add(mix_parts, dkv)
        dkv = attend_back(
            meta,
            queries,
            grad_mixed,
            mixed,
            lse,
            ring.by_distance.index(min(places)),
            [kv_blocks[r] for r in places],
            dq,
            (cont_kv, cosine, sine_signed) if 0 in places else None,
        )
        parts = dict(zip(places, dkv))
        if ring.half in places:
            dkv_sum = RingSum(ring, parts[ring.half])
        elif 0 not in places:
            grad_out_weight = dot_tn(after(mixed_low, dkv), grad_attn2)
            if turn_no == 1:
                late_gate_up, late_down = after((grad_gate_up, grad_down), dkv)
                gate_up_shards, down_shards = shards_dp(late_gate_up), shards_dp(late_down)
            dkv_before = dkv_sum.arrived()
            dkv_sum.add(parts)
        if 0 not in places:
            dq = dkv[len(places)]
    grad_projected = projected_grad(
        dkv[1], (parts[0], *dkv_sum.arrived()), dkv[2], cosine, sine_signed
    )
    grad_qkv_weight = dot_tn(attn_in2, grad_projected)
    part = dot_nt(grad_projected, proj_qkv)
    other_part = swap(part[tok_count:].astype(bf16))

    qkv_rows = width // dp_size // chips
    out_rows = HEADS * HEAD_DIM // dp_size // 2 // chips
    dense_parts = order_parts(
        meta, grad_qkv_weight.astype(bf16), grad_out_weight.astype(bf16), chips, dp_size
    )
    parts = {r: dense_parts[k] for k, r in enumerate(ring.by_distance)}
    dense_sum = RingSum(ring, parts[ring.half])
    dense_sum.add(parts)
    gate_up_new = adamw(
        gate_up_weight,
        mean_gate_up_weight,
        square_gate_up_weight,
        sum_of(gate_up_shards, dense_sum.sent)[None],
        grad_scale,
        decay_rate,
    )
    dense_sum.add(parts, gate_up_new, other_part)
    grad_attn_in = part[:tok_count] + after(other_part, dense_sum.sent).astype(f32)
    grad_tok_norm, grad_gain_attn = norm_back(tok_float, scale_attn, gain_attn, grad_attn_in)
    input_grad = grad_hidden + grad_tok_norm
    small_grad = jnp.concatenate(
        [grad_gain_attn[None], grad_gain_ffn[None], grad_router_t], axis=0
    )
    down_new = adamw(
        down_weight,
        mean_down_weight,
        square_down_weight,
        sum_of(down_shards, dense_sum.sent)[None],
        grad_scale,
        decay_rate,
    )
    dense_sum.add(parts, down_new, small_grad)
    while dense_sum.place > 1:
        dense_sum.add(parts)
    for small_grad in total_stages(small_grad, ("core", "dp")):
        pass
    dense = after(dense_sum.finish(parts[0]), small_grad)
    dense = dense.reshape(dp_size, qkv_rows + out_rows, width)
    mix_sum.add(mix_parts, dense)
    shard = lax.dynamic_index_in_dim(dense, dp, 0, False)
    for shift in range(1, dp_size):
        perm = [(k, (k + shift) % dp_size) for k in range(dp_size)]
        sent = lax.dynamic_index_in_dim(dense, (dp + shift) % dp_size, 0, False)
        shard = shard + lax.ppermute(sent.astype(bf16), "dp", perm).astype(f32)
    shard_low = shard.astype(bf16)

    qkv_state = (qkv_weight, mean_qkv_weight, square_qkv_weight)
    out_state = (out_weight, mean_out_weight, square_out_weight)
    step_shard = shard_step(
        meta, shard_low, qkv_state, out_state, chips, dp_size, grad_scale
    )
    carried = jnp.stack([shard_low, *dp_shards(step_shard)[1:]])
    carried = after(carried, mix_sum.arrived())
    while mix_sum.place > 1:
        mix_sum.add(mix_parts, step_shard)
    output = hidden + mix_sum.finish(mix_parts[0])
    carried = carried.reshape(dp_size * (qkv_rows + out_rows), width)
    dense_new = None
    shape = (dp_size, qkv_rows + out_rows, width)
    dense_ring = RingGather(ring, carried)
    arrived, first_place, earlier = dict(dense_ring.blocks), 0, ()
    while arrived:
        later = {}
        if dense_ring.place < ring.half:
            later = dense_ring.step(*earlier)
        earlier = tuple(dense_new or ())
        dense_new = optimize(
            meta,
            first_place,
            [m.reshape(shape) for m in arrived.values()],
            [swap(m).reshape(shape) for m in arrived.values()],
            qkv_state,
            out_state,
            dense_new,
            chips,
            dp_size,
            grad_scale,
        )
        first_place += len(arrived)
        arrived = later
    dense_new = [a.reshape(-1, a.shape[-1]) for a in dense_new]

    small_grad = after(small_grad, dense_ring.blocks[ring.half - 1])
    for small_grad in total_stages(small_grad, ("chip",)):
        pass
    shard_cols = width // dp_size
    small_shard = lax.dynamic_slice_in_dim(small_grad, dp * shard_cols, shard_cols, 1)
    attn_new = adamw(
        attn_gain, mean_attn_gain, square_attn_gain, small_shard[0], grad_scale, 0.0
    )
    ffn_new = adamw(ffn_gain, mean_ffn_gain, square_ffn_gain, small_shard[1], grad_scale, 0.0)
    router_new = adamw(
        router_weight,
        mean_router_weight,
        square_router_weight,
        small_shard[2:].T,
        grad_scale,
        decay_rate,
    )
    small_step = jnp.concatenate(
        [attn_new[0][None], ffn_new[0][None], router_new[0].T], axis=0
    ).astype(bf16)
    small_step = gather_dp(small_step, 1).astype(f32)

    step_gate_up = lax.all_gather(gate_up_new[0].astype(bf16), "dp", axis=1, tiled=True)
    step_down = lax.all_gather(down_new[0].astype(bf16), "dp", axis=1, tiled=True)
    return (
        merge_rows(output.astype(bf16)),
        merge_rows(input_grad),
        small_step[0],
        dense_new[0],
        dense_new[3],
        small_step[1],
        small_step[2:].T,
        step_gate_up.astype(f32),
        step_down.astype(f32),
        attn_new[1],
        dense_new[1],
        dense_new[4],
        ffn_new[1],
        router_new[1],
        gate_up_new[1],
        down_new[1],
        attn_new[2],
        dense_new[2],
        dense_new[5],
        ffn_new[2],
        router_new[2],
        gate_up_new[2],
        down_new[2],
    )


def solution(mesh):
    dp_size, members = mesh.shape["dp"], mesh.shape["expert"]
    chips = members // 2
    fine = Mesh(mesh.devices.reshape(dp_size, chips, 2), ("dp", "chip", "core"))
    ring = Ring(chips)
    member = ("chip", "core")
    token = P(("dp",) + member, None)
    matrices = (P("dp"), P("dp", None), P("dp", None), P("dp"), P("dp", None))
    expert = (P(member, "dp", None), P(member, "dp", None))

    def body(*arrays):
        return per_device(ring, *arrays)

    return jax.shard_map(
        body,
        mesh=fine,
        in_specs=(token, token, token, P(("dp",) + member)) + (matrices + expert) * 3,
        out_specs=(token, token)
        + (P(),) * 5
        + (P(member, None, None),) * 2
        + (matrices + expert) * 2,
        check_vma=False,
    )
```

```python
import functools
import math

import jax
import jax.numpy as jnp
from jax import lax
from jax.experimental import pallas as pl
from jax.experimental.pallas import tpu as pltpu
from jax.sharding import Mesh
from jax.sharding import PartitionSpec as P

HEADS = 16
KV_HEADS = 8
HEAD_DIM = 64
EXP_FF = 512
TOPK = 8
NPROMPT = 2
PROMPT_DEV = 128
CLEN = 128
REPEAT = HEADS // KV_HEADS
PROMPT_ROWS = NPROMPT * PROMPT_DEV

norm_eps = 1e-05
masked_score = -1e30
decay_rate = 0.1
adam_eps = 1e-08
bias_first = 0.999973438601112
bias_second = 0.99407947078
score_scale = HEAD_DIM ** (-0.5)

bf16 = jnp.bfloat16
f32 = jnp.float32


def dot(left, right):
    return jnp.dot(left, right, preferred_element_type=f32)


def dot_tn(left, right):
    return lax.dot_general(left, right, (((0,), (0,)), ((), ())), preferred_element_type=f32)


def dot_nt(left, right):
    return lax.dot_general(left, right, (((1,), (1,)), ((), ())), preferred_element_type=f32)


def norm_back(values, scale_rows, gain_row, grad_rows):
    normed = values * scale_rows
    grad_normed = grad_rows * gain_row
    grad_values = scale_rows * (
        grad_normed - normed * jnp.mean(grad_normed * normed, axis=-1, keepdims=True)
    )
    return (grad_values, jnp.sum(grad_rows * normed, axis=0))


def adamw(weight, mean_in, square_in, gradient, grad_scale, decay_factor):
    scaled = gradient * grad_scale
    mean_out = 0.9 * mean_in + 0.1 * scaled
    square_out = 0.95 * square_in + 0.05 * scaled * scaled
    spread = square_out * (1.0 / bias_second)
    spread = spread * lax.rsqrt(spread) + adam_eps
    update = mean_out * (1.0 / bias_first) / spread
    return (update + decay_factor * weight, mean_out, square_out)


def split_rows(values):
    head = values[:PROMPT_ROWS].reshape(PROMPT_DEV, NPROMPT, -1).transpose(1, 0, 2)
    return jnp.concatenate([head.reshape(PROMPT_ROWS, -1), values[PROMPT_ROWS:]], axis=0)


def merge_rows(values):
    head = values[:PROMPT_ROWS].reshape(NPROMPT, PROMPT_DEV, -1).transpose(1, 0, 2)
    return jnp.concatenate([head.reshape(PROMPT_ROWS, -1), values[PROMPT_ROWS:]], axis=0)


def swap(values):
    return lax.ppermute(values, "core", [(0, 1), (1, 0)])


class Ring:
    def __init__(self, chips):
        rows = 4 if chips % 4 == 0 else chips
        cols = chips // rows
        cycle = [(0, x) for x in range(cols)]
        for z in range(1, rows):
            line = [(z, x) for x in range(1, cols)]
            cycle += line[::-1] if z % 2 == 1 else line
        if cols > 1:
            cycle += [(z, 0) for z in range(rows - 1, 0, -1)]
        else:
            cycle = [(z, 0) for z in range(rows)]
        self.chips = chips
        self.order = [z * cols + x for z, x in cycle]
        self.forward = [
            (self.order[k], self.order[(k + 1) % chips]) for k in range(chips)
        ]
        self.backward = [(b, a) for a, b in self.forward]
        self.half = chips // 2
        self.by_distance = [r for group in self.groups() for r in group]

    def chips_from(self, me):
        table = [[0] * self.chips for _ in range(self.chips)]
        for k in range(self.chips):
            for column, offset in enumerate(self.by_distance):
                table[self.order[k]][column] = self.order[(k + offset) % self.chips]
        return lax.dynamic_index_in_dim(jnp.asarray(table, jnp.int32), me, 0, False)

    def gather_steps(self, block):
        gather = RingGather(self, block)
        yield {0: block}
        for _ in range(self.half):
            yield gather.step()

    @staticmethod
    def cut(block):
        return block.shape[0] // 32 * 16

    def groups(self):
        return [[0]] + [[-s, s] for s in range(1, self.half)] + [[self.half]]


class RingGather:
    def __init__(self, ring, block):
        self.ring = ring
        self.place = 0
        self.ahead = self.behind = block
        self.blocks = {0: block}

    def ends(self):
        return (self.ahead, self.behind)

    def step(self, *others):
        ring = self.ring
        self.place += 1
        if others:
            self.ahead, self.behind = after(self.ends(), others)
        self.before = self.ends()
        if self.place < ring.half:
            self.ahead = lax.ppermute(self.ahead, "chip", ring.forward)
            self.behind = lax.ppermute(self.behind, "chip", ring.backward)
            arrived = {-self.place: self.ahead, self.place: self.behind}
        else:
            cut = ring.cut(self.ahead)
            first = lax.ppermute(self.ahead[:cut], "chip", ring.forward)
            second = lax.ppermute(self.behind[cut:], "chip", ring.backward)
            arrived = {ring.half: jnp.concatenate([first, second], axis=0)}
        self.blocks.update(arrived)
        return arrived


class RingSum:
    def __init__(self, ring, part):
        cut = ring.cut(part)
        self.ring = ring
        self.place = ring.half
        self.cut = cut
        self.sent = (part[:cut], part[cut:])
        self.send()

    def send(self):
        self.ahead = lax.ppermute(self.sent[0], "chip", self.ring.forward)
        self.behind = lax.ppermute(self.sent[1], "chip", self.ring.backward)

    def arrived(self):
        return (self.ahead, self.behind)

    def add(self, parts, *others):
        ring, cut = self.ring, self.cut
        self.place -= 1
        up, down = parts[self.place], parts[-self.place]
        if others:
            up, down = after((up, down), others)
        self.ahead, self.behind = lax.optimization_barrier((self.ahead, self.behind))
        if self.place == ring.half - 1:
            ahead = jnp.concatenate([self.ahead + up[:cut], up[cut:]], axis=0)
            behind = jnp.concatenate([down[:cut], self.behind + down[cut:]], axis=0)
        else:
            ahead, behind = self.ahead + up, self.behind + down
        self.sent = (ahead, behind)
        self.send()

    def finish(self, part):
        return part.astype(f32) + self.ahead.astype(f32) + self.behind.astype(f32)


def after(values, *others):
    return lax.optimization_barrier((values, others))[0]


def total_stages(values, axes):
    for axis in axes:
        size = lax.axis_size(axis)
        reach = 1
        while reach < size:
            values = values + lax.ppermute(values, axis, [(k, k ^ reach) for k in range(size)])
            reach *= 2
            yield values


def dp_shards(values):
    size = lax.axis_size("dp")
    pieces = [values]
    for shift in range(1, size):
        perm = [(k, (k - shift) % size) for k in range(size)]
        pieces.append(lax.ppermute(values, "dp", perm))
    return pieces


def join_dp(pieces, axis):
    size = len(pieces)
    dp = lax.axis_index("dp")
    if size == 2:
        return jnp.concatenate(
            [
                jnp.where(dp == 0, pieces[0], pieces[1]),
                jnp.where(dp == 0, pieces[1], pieces[0]),
            ],
            axis=axis,
        )
    twice = jnp.concatenate(pieces + pieces, axis=axis)
    shard = pieces[0].shape[axis]
    return lax.dynamic_slice_in_dim(twice, (size - dp) % size * shard, size * shard, axis)


def gather_dp(values, axis):
    return join_dp(dp_shards(values), axis)


def pick_core(first, second):
    return jnp.where(lax.axis_index("core") == 0, first, second)


LOG2E = 1.4426950408889634


def stack_heads(wide):
    wide = wide.astype(f32)
    first, second = wide[:, :128], wide[:, 128:]
    lane = lax.broadcasted_iota(jnp.int32, first.shape, 1)
    low_lanes = lane < HEAD_DIM
    zero = jnp.zeros_like(first)
    return jnp.concatenate(
        [
            jnp.where(low_lanes, first, zero),
            jnp.where(low_lanes, pltpu.roll(first, HEAD_DIM, 1), zero),
            jnp.where(low_lanes, zero, pltpu.roll(second, HEAD_DIM, 1)),
            jnp.where(low_lanes, zero, second),
        ],
        axis=0,
    )


def unstack_heads(tall):
    rows = tall.shape[0] // 4
    parts = [tall[k * rows : (k + 1) * rows] for k in range(4)]
    lane = lax.broadcasted_iota(jnp.int32, parts[0].shape, 1)
    low_lanes = lane < HEAD_DIM
    return jnp.concatenate(
        [
            jnp.where(low_lanes, parts[0], pltpu.roll(parts[1], HEAD_DIM, 1)),
            jnp.where(low_lanes, pltpu.roll(parts[2], HEAD_DIM, 1), parts[3]),
        ],
        axis=1,
    )


def row_of(column_sum_of):
    return jnp.sum(jnp.transpose(column_sum_of), axis=0, keepdims=True)


def tile_masks(meta_ref, half, is_cont):
    shape = (PROMPT_ROWS, 4 * PROMPT_DEV)
    key = lax.broadcasted_iota(jnp.int32, shape, 0)
    query = lax.broadcasted_iota(jnp.int32, shape, 1) % PROMPT_DEV
    key_member = jnp.where(key < PROMPT_DEV, meta_ref[2], meta_ref[3])
    key_pos = key_member * PROMPT_DEV + key % PROMPT_DEV
    query_pos = meta_ref[2 + half] * PROMPT_DEV + query
    own = (key_pos <= query_pos) | is_cont
    shape = (CLEN, 4 * CLEN)
    key = lax.broadcasted_iota(jnp.int32, shape, 0)
    query = lax.broadcasted_iota(jnp.int32, shape, 1) % CLEN
    self_seen = (key <= query) & is_cont
    return own, self_seen


META = 8


def block_bias(meta_ref, is_cont, first_block, blocks):
    chips = [meta_ref[META + first_block + k] for k in range(blocks)]
    return [jnp.where(is_cont | (c <= meta_ref[6]), 0.0, masked_score) for c in chips]


def attend_kernel(first_block, blocks, first, last, meta_ref, q_ref, *refs):
    kv_refs, refs = refs[:blocks], refs[blocks:]
    if first:
        self_ref, refs = refs[0], refs[1:]
    else:
        acc_in, stat_in = refs[:2]
        refs = refs[2:]
    if last:
        out_ref, low_ref, lse_ref, scores = refs
    else:
        acc_out, stat_out, scores = refs
    tile = pl.program_id(0)
    half = tile // 3
    part = tile % 3
    is_cont = part == NPROMPT
    prompt = jnp.where(is_cont, meta_ref[half], part)
    rows = pl.ds(pl.multiple_of(prompt * PROMPT_ROWS, PROMPT_ROWS), PROMPT_ROWS)
    if first:
        own, self_seen = tile_masks(meta_ref, half, is_cont)
    bias = block_bias(meta_ref, is_cont, first_block, blocks)
    scale = score_scale * LOG2E
    k_width = KV_HEADS // 2 * HEAD_DIM
    for pair in range(2):
        lanes = pl.ds(pair * 128, 128)
        v_lanes = pl.ds(k_width + pair * 128, 128)
        q = stack_heads(q_ref[:, pair * 256 : (pair + 1) * 256]).astype(bf16)
        if first:
            s_self = jnp.where(self_seen, dot_nt(self_ref[0, :, lanes], q), masked_score)
            top = jnp.max(s_self, axis=0, keepdims=True)
        else:
            old = stat_in[0, pair, :1, :]
            top = old
        for k in range(blocks):
            s = dot_nt(kv_refs[k][rows, lanes], q)
            if first:
                s = jnp.where(own, s, masked_score)
            scores[pl.ds(k * PROMPT_ROWS, PROMPT_ROWS), :] = s
            top = jnp.maximum(top, jnp.max(s, axis=0, keepdims=True) + bias[k])
        top2 = top * scale
        if first:
            p = jnp.exp2(s_self * scale - top2)
            total = jnp.sum(p, axis=0, keepdims=True)
            acc = dot(jnp.transpose(self_ref[0, :, v_lanes]), p.astype(bf16))
        else:
            factor = jnp.exp2(old * scale - top2)
            total = stat_in[0, pair, 1:2, :] * factor
            acc = acc_in[0, pair] * factor
        for k in range(blocks):
            s = scores[pl.ds(k * PROMPT_ROWS, PROMPT_ROWS), :]
            p = jnp.exp2(s * scale - (top2 - bias[k]))
            total = total + jnp.sum(p, axis=0, keepdims=True)
            acc = acc + dot(jnp.transpose(kv_refs[k][rows, v_lanes]), p.astype(bf16))
        if last:
            out = unstack_heads(jnp.transpose(acc / total))
            out_ref[:, pair * 256 : (pair + 1) * 256] = out
            low_ref[:, pair * 256 : (pair + 1) * 256] = out.astype(bf16)
            lse = top2 + jnp.log2(total)
            for head in range(4):
                lse_ref[pl.ds(pair * 4 + head, 1), :] = lse[
                    :, head * PROMPT_DEV : (head + 1) * PROMPT_DEV
                ]
        else:
            acc_out[0, pair] = acc
            stat_out[0, pair, :1, :] = top
            stat_out[0, pair, 1:2, :] = total


def attend_back_kernel(first_block, blocks, first, last, meta_ref, q_ref, do_ref, out_ref, lse_ref, *refs):
    kv_refs, refs = refs[:blocks], refs[blocks:]
    if last:
        self_ref, cos_ref, sin_ref = refs[:3]
        refs = refs[3:]
    if not first:
        dq_in, refs = refs[0], refs[1:]
    dkv_refs, refs = refs[:blocks], refs[blocks:]
    if last:
        dq_ref, dself_ref, acc = refs
    else:
        dq_out, acc = refs
    tile = pl.program_id(0)
    half = tile // 3
    part = tile % 3
    is_cont = part == NPROMPT
    prompt = jnp.where(is_cont, meta_ref[half], part)
    start = pl.multiple_of(prompt * PROMPT_ROWS, PROMPT_ROWS)
    rows = pl.ds(start, PROMPT_ROWS)
    if last:
        own, self_seen = tile_masks(meta_ref, half, is_cont)
    bias = block_bias(meta_ref, is_cont, first_block, blocks)
    scale = score_scale * LOG2E
    k_width = KV_HEADS // 2 * HEAD_DIM

    @pl.when(tile == 0)
    def _():
        acc[...] = jnp.zeros_like(acc)

    for pair in range(2):
        lanes = pl.ds(pair * 128, 128)
        v_lanes = pl.ds(k_width + pair * 128, 128)
        cut = slice(pair * 256, (pair + 1) * 256)
        q = stack_heads(q_ref[:, cut]).astype(bf16)
        do_wide = stack_heads(do_ref[:, cut])
        delta = row_of(do_wide * stack_heads(out_ref[:, cut]))
        do = do_wide.astype(bf16)
        lse = jnp.concatenate(
            [lse_ref[pl.ds(pair * 4 + head, 1), :] for head in range(4)], axis=1
        )
        dq = jnp.zeros((128, 4 * PROMPT_DEV), f32) if first else dq_in[0, pair]
        for k in range(blocks):
            key, value = kv_refs[k][rows, lanes], kv_refs[k][rows, v_lanes]
            s = dot_nt(key, q)
            if last:
                s = jnp.where(own, s, masked_score)
            p = jnp.exp2(s * scale - (lse - bias[k]))
            ds = (p * (dot_nt(value, do) - delta)).astype(bf16)
            dq = dq + dot(jnp.transpose(key), ds)
            acc[k, rows, lanes] += dot(ds, q)
            acc[k, rows, v_lanes] += dot(p.astype(bf16), do)
        if last:
            key, value = self_ref[0, :, lanes], self_ref[0, :, v_lanes]
            s = jnp.where(self_seen, dot_nt(key, q), masked_score)
            p = jnp.exp2(s * scale - lse)
            ds = (p * (dot_nt(value, do) - delta)).astype(bf16)
            dq = dq + dot(jnp.transpose(key), ds)
            dself_ref[0, :, lanes] = dot(ds, q) * score_scale
            dself_ref[0, :, v_lanes] = dot(p.astype(bf16), do)
            wide = unstack_heads(jnp.transpose(dq)) * score_scale
            for group in range(2):
                turned = turn(wide[:, group * 128 : (group + 1) * 128], cos_ref[...], -sin_ref[...])
                lo = pair * 256 + group * 128
                dq_ref[:, lo : lo + 128] = turned.astype(bf16)
        else:
            dq_out[0, pair] = dq

    @pl.when(tile == pl.num_programs(0) - 1)
    def _():
        for k in range(blocks):
            dkv_refs[k][:, :k_width] = (acc[k, :, :k_width] * score_scale).astype(bf16)
            dkv_refs[k][:, k_width:] = acc[k, :, k_width:].astype(bf16)


def turn(values, cosine, sine_signed):
    lane = lax.broadcasted_iota(jnp.int32, values.shape, 1) % HEAD_DIM
    swapped = jnp.where(
        lane < HEAD_DIM // 2,
        pltpu.roll(values, 128 - HEAD_DIM // 2, 1),
        pltpu.roll(values, HEAD_DIM // 2, 1),
    )
    return values * cosine + swapped * sine_signed


VMEM_LIMIT = 40 * 1024 * 1024
SMALL_LIMIT = 24 * 1024 * 1024
WHOLE_LIMIT = 60 * 1024 * 1024


def whole_spec(array):
    return pl.BlockSpec(
        array.shape, lambda *_: (0,) * array.ndim, pipeline_mode=pl.Buffered(1)
    )


def attend(meta, queries, first_block, kv_blocks, state, cont_kv=None, last=False):
    blocks = len(kv_blocks)
    first = state is None
    rows, q_width = queries.shape
    tiles = rows // PROMPT_DEV
    columns = 4 * PROMPT_DEV
    row_spec = pl.BlockSpec((PROMPT_DEV, q_width), lambda t, meta: (t, 0))
    lse_spec = pl.BlockSpec((HEADS // 2, PROMPT_DEV), lambda t, meta: (0, t))
    acc_spec = pl.BlockSpec((1, 2, 128, columns), lambda t, meta: (t, 0, 0, 0))
    stat_spec = pl.BlockSpec((1, 2, 8, columns), lambda t, meta: (t, 0, 0, 0))
    pairs = rows * HEADS // 2 * blocks * PROMPT_ROWS
    in_specs = [row_spec] + [whole_spec(b) for b in kv_blocks]
    operands = [meta, queries, *kv_blocks]
    if first:
        in_specs.append(pl.BlockSpec((1,) + cont_kv.shape[1:], lambda t, meta: (t // 3, 0, 0)))
        operands.append(cont_kv)
    else:
        in_specs += [acc_spec, stat_spec]
        operands += list(state)
    if last:
        out_specs = [row_spec, row_spec, lse_spec]
        out_shape = [
            jax.ShapeDtypeStruct((rows, q_width), f32),
            jax.ShapeDtypeStruct((rows, q_width), bf16),
            jax.ShapeDtypeStruct((HEADS // 2, rows), f32),
        ]
    else:
        out_specs = [acc_spec, stat_spec]
        out_shape = [
            jax.ShapeDtypeStruct((tiles, 2, 128, columns), f32),
            jax.ShapeDtypeStruct((tiles, 2, 8, columns), f32),
        ]
    return pl.pallas_call(
        functools.partial(attend_kernel, first_block, blocks, first, last),
        grid_spec=pltpu.PrefetchScalarGridSpec(
            num_scalar_prefetch=1,
            grid=(tiles,),
            in_specs=in_specs,
            out_specs=out_specs,
            scratch_shapes=[pltpu.VMEM((blocks * PROMPT_ROWS, columns), f32)],
        ),
        out_shape=out_shape,
        compiler_params=pltpu.CompilerParams(vmem_limit_bytes=VMEM_LIMIT),
        cost_estimate=pl.CostEstimate(
            flops=48 * 64 * pairs, bytes_accessed=12 << 20, transcendentals=pairs
        ),
        name="attend",
    )(*operands)


def attend_back(meta, queries, grads, mixed, lse, first_block, kv_blocks, dq, own=None):
    blocks = len(kv_blocks)
    first, last = dq is None, own is not None
    rows, q_width = queries.shape
    tiles = rows // PROMPT_DEV
    columns = 4 * PROMPT_DEV
    row_spec = pl.BlockSpec((PROMPT_DEV, q_width), lambda t, meta: (t, 0))
    lse_spec = pl.BlockSpec((HEADS // 2, PROMPT_DEV), lambda t, meta: (0, t))
    dq_spec = pl.BlockSpec((1, 2, 128, columns), lambda t, meta: (t, 0, 0, 0))
    block = kv_blocks[0]
    pairs = rows * HEADS // 2 * blocks * PROMPT_ROWS
    in_specs = [row_spec, row_spec, row_spec, lse_spec] + [whole_spec(b) for b in kv_blocks]
    operands = [meta, queries, grads, mixed, lse, *kv_blocks]
    out_specs = [whole_spec(b) for b in kv_blocks]
    out_shape = [jax.ShapeDtypeStruct(b.shape, bf16) for b in kv_blocks]
    if last:
        cont_kv, cosine, sine = own
        self_spec = pl.BlockSpec((1,) + cont_kv.shape[1:], lambda t, meta: (t // 3, 0, 0))
        turn_spec = pl.BlockSpec((PROMPT_DEV, 128), lambda t, meta: (t, 0))
        in_specs += [self_spec, turn_spec, turn_spec]
        operands += [cont_kv, cosine, sine]
        out_specs += [row_spec, self_spec]
        out_shape += [
            jax.ShapeDtypeStruct((rows, q_width), bf16),
            jax.ShapeDtypeStruct(cont_kv.shape, f32),
        ]
    else:
        out_specs.append(dq_spec)
        out_shape.append(jax.ShapeDtypeStruct((tiles, 2, 128, columns), f32))
    if not first:
        in_specs.append(dq_spec)
        operands.append(dq)
    return pl.pallas_call(
        functools.partial(attend_back_kernel, first_block, blocks, first, last),
        grid_spec=pltpu.PrefetchScalarGridSpec(
            num_scalar_prefetch=1,
            grid=(tiles,),
            in_specs=in_specs,
            out_specs=out_specs,
            scratch_shapes=[pltpu.VMEM((blocks,) + block.shape, f32)],
        ),
        out_shape=out_shape,
        compiler_params=pltpu.CompilerParams(vmem_limit_bytes=VMEM_LIMIT),
        cost_estimate=pl.CostEstimate(
            flops=110 * 64 * pairs, bytes_accessed=16 << 20, transcendentals=pairs
        ),
        name="attend_back",
    )(*operands)


def core_pieces(columns, core, dp_size):
    width = columns.shape[-1] // (2 * dp_size)
    pieces = []
    for s in range(dp_size):
        lo = 2 * s * width
        pieces.append(
            jnp.where(core == 0, columns[:, lo : lo + width], columns[:, lo + width : lo + 2 * width])
        )
    return pieces


def core_heads(columns, core, dp_size):
    q, k = HEADS * HEAD_DIM, KV_HEADS * HEAD_DIM
    cuts = [columns[:, :q], columns[:, q : q + k], columns[:, q + k :]]
    return jnp.concatenate([p for cut in cuts for p in core_pieces(cut, core, dp_size)], axis=1)


def all_heads(mine, other, core, dp_size):
    first, second = jnp.where(core == 0, mine, other), jnp.where(core == 0, other, mine)
    q, k = HEADS // 2 * HEAD_DIM, KV_HEADS // 2 * HEAD_DIM
    pieces = []
    for lo, size in ((0, q), (q, k), (q + k, k)):
        width = size // dp_size
        for s in range(dp_size):
            cut = slice(lo + s * width, lo + (s + 1) * width)
            pieces += [first[:, cut], second[:, cut]]
    return jnp.concatenate(pieces, axis=1)


def cast_kernel(dp_size, meta_ref, weight_ref, out_ref):
    out_ref[...] = core_heads(weight_ref[...], meta_ref[0], dp_size).astype(bf16)


def cast_core_columns(core, weight, dp_size):
    rows, columns = weight.shape
    tile = rows // 4
    return pl.pallas_call(
        functools.partial(cast_kernel, dp_size),
        grid_spec=pltpu.PrefetchScalarGridSpec(
            num_scalar_prefetch=1,
            grid=(4,),
            in_specs=[pl.BlockSpec((tile, columns), lambda t, meta: (t, 0))],
            out_specs=pl.BlockSpec((tile, columns // 2), lambda t, meta: (t, 0)),
        ),
        out_shape=jax.ShapeDtypeStruct((rows, columns // 2), bf16),
        compiler_params=pltpu.CompilerParams(vmem_limit_bytes=SMALL_LIMIT),
        cost_estimate=pl.CostEstimate(
            flops=rows * columns, bytes_accessed=5 * rows * columns, transcendentals=0
        ),
        name="cast_core_columns",
    )(core[None], weight)


def project_kernel(shards, meta_ref, own_ref, other_ref, *refs):
    weights = refs[:shards]
    cos_ref, sin_ref, q_ref, prompt_ref, cont_ref = refs[shards:]
    half = pl.program_id(0)
    depth = weights[0].shape[0]
    q_width = q_ref.shape[-1]
    k_width = cont_ref.shape[-1] // 2
    cosine, sine = cos_ref[...], sin_ref[...]

    def run(x_ref):
        xs = []
        for k in range(shards):
            start = pl.multiple_of((meta_ref[5] + k) % shards * depth, depth)
            xs.append(x_ref[:, pl.ds(start, depth)])
        for lo in range(0, q_width + 2 * k_width, 128):
            if lo % 256 == 0:
                out = sum(dot(x, w[:, lo : lo + 256]) for x, w in zip(xs, weights))
            piece = out[:, lo % 256 : lo % 256 + 128]
            if lo < q_width + k_width:
                piece = turn(piece, cosine, sine)
            piece = piece.astype(bf16)
            if lo < q_width:
                q_ref[:, lo : lo + 128] = piece
            else:
                at = lo - q_width
                for g in range(NPROMPT):
                    rows = piece[g * PROMPT_DEV : (g + 1) * PROMPT_DEV]
                    prompt_ref[g, 0, :, at : at + 128] = rows
                cont_ref[0, :, at : at + 128] = piece[PROMPT_ROWS:]

    pl.when(half == 0)(lambda: run(own_ref))
    pl.when(half == 1)(lambda: run(other_ref))


def project(meta, own, other, weights, cosine, sine):
    rows, width = own.shape
    columns = weights[0].shape[1]
    kv_width = columns // 2
    turn_spec = pl.BlockSpec((rows, 128), lambda h, meta: (h, 0))
    return pl.pallas_call(
        functools.partial(project_kernel, len(weights)),
        grid_spec=pltpu.PrefetchScalarGridSpec(
            num_scalar_prefetch=1,
            grid=(2,),
            in_specs=[whole_spec(a) for a in (own, other, *weights)] + [turn_spec] * 2,
            out_specs=[
                pl.BlockSpec((rows, columns - kv_width), lambda h, meta: (h, 0)),
                pl.BlockSpec((NPROMPT, 1, PROMPT_DEV, kv_width), lambda h, meta: (0, h, 0, 0)),
                pl.BlockSpec((1, CLEN, kv_width), lambda h, meta: (h, 0, 0)),
            ],
        ),
        out_shape=[
            jax.ShapeDtypeStruct((2 * rows, columns - kv_width), bf16),
            jax.ShapeDtypeStruct((NPROMPT, 2, PROMPT_DEV, kv_width), bf16),
            jax.ShapeDtypeStruct((2, CLEN, kv_width), bf16),
        ],
        compiler_params=pltpu.CompilerParams(vmem_limit_bytes=SMALL_LIMIT),
        cost_estimate=pl.CostEstimate(
            flops=4 * rows * width * columns, bytes_accessed=8 << 20, transcendentals=0
        ),
        name="project",
    )(meta, own, other, *weights, cosine, sine)


def projected_grad_kernel(dq_ref, *refs):
    dkv_refs = refs[:3]
    dself_ref, cos_ref, sin_ref, out_ref = refs[3:]
    q_width = dq_ref.shape[-1]
    k_width = dself_ref.shape[-1] // 2
    out_ref[:, :q_width] = dq_ref[...]
    parts = [sum(ref[g, 0].astype(f32) for ref in dkv_refs) for g in range(NPROMPT)]
    dkv = jnp.concatenate(parts + [dself_ref[0]], axis=0)
    cosine, sine = cos_ref[...], -sin_ref[...]
    for lo in range(0, 2 * k_width, 128):
        piece = dkv[:, lo : lo + 128]
        if lo < k_width:
            piece = turn(piece, cosine, sine)
        out_ref[:, q_width + lo : q_width + lo + 128] = piece.astype(bf16)


def projected_grad(dq, dkv_parts, dself, cosine, sine):
    rows2, q_width = dq.shape
    rows = rows2 // 2
    kv_width = dself.shape[-1]
    dkv_parts = [p.reshape(NPROMPT, 2, PROMPT_DEV, kv_width) for p in dkv_parts]
    turn_spec = pl.BlockSpec((rows, 128), lambda h: (h, 0))
    return pl.pallas_call(
        projected_grad_kernel,
        grid=(2,),
        in_specs=[pl.BlockSpec((rows, q_width), lambda h: (h, 0))]
        + [pl.BlockSpec((NPROMPT, 1, PROMPT_DEV, kv_width), lambda h: (0, h, 0, 0))] * 3
        + [pl.BlockSpec((1, CLEN, kv_width), lambda h: (h, 0, 0)), turn_spec, turn_spec],
        out_specs=pl.BlockSpec((rows, q_width + kv_width), lambda h: (h, 0)),
        out_shape=jax.ShapeDtypeStruct((rows2, q_width + kv_width), bf16),
        compiler_params=pltpu.CompilerParams(vmem_limit_bytes=SMALL_LIMIT),
        cost_estimate=pl.CostEstimate(
            flops=20 * rows2 * kv_width, bytes_accessed=6 << 20, transcendentals=0
        ),
        name="projected_grad",
    )(dq, *dkv_parts, dself, cosine, sine)


def order_kernel(meta_ref, qkv_ref, out_ref, parts_ref):
    top = qkv_ref.shape[1]
    shards = qkv_ref.shape[0]
    rows = top + out_ref.shape[1]
    for s in range(shards):
        parts_ref[0, s * rows : s * rows + top, :] = qkv_ref[s]
        parts_ref[0, s * rows + top : (s + 1) * rows, :] = out_ref[s]


def order_parts(meta, qkv, out, chips, dp_size):
    width = qkv.shape[1]
    qkv = qkv.reshape(dp_size, -1, width)
    out = out.reshape(dp_size, -1, width)
    rows = [a.shape[1] // chips for a in (qkv, out)]
    return pl.pallas_call(
        order_kernel,
        grid_spec=pltpu.PrefetchScalarGridSpec(
            num_scalar_prefetch=1,
            grid=(chips,),
            in_specs=[
                pl.BlockSpec((dp_size, r, width), lambda k, meta: (0, meta[META + k], 0))
                for r in rows
            ],
            out_specs=pl.BlockSpec((1, dp_size * sum(rows), width), lambda k, meta: (k, 0, 0)),
        ),
        out_shape=jax.ShapeDtypeStruct((chips, dp_size * sum(rows), width), bf16),
        compiler_params=pltpu.CompilerParams(vmem_limit_bytes=SMALL_LIMIT),
        cost_estimate=pl.CostEstimate(
            flops=qkv.size, bytes_accessed=6 * qkv.size, transcendentals=0
        ),
        name="order_parts",
    )(meta, qkv, out)


def step_kernel(dp_size, grad_scale, meta_ref, grad_ref, *refs):
    qkv, out, step_ref = refs[:3], refs[3:6], refs[6]
    top = qkv[0].shape[0]
    grad = grad_ref[...].astype(f32)
    args = [core_heads(ref[...], meta_ref[4], dp_size) for ref in qkv]
    step_ref[:top, :] = adamw(*args, grad[:top], grad_scale, decay_rate)[0].astype(bf16)
    args = [ref[...] for ref in out]
    step_ref[top:, :] = adamw(*args, grad[top:], grad_scale, decay_rate)[0].astype(bf16)


def shard_step(meta, grad, qkv, out, chips, dp_size, grad_scale):
    qkv_rows, out_rows = qkv[0].shape[0] // chips, out[0].shape[0] // (2 * chips)
    width = grad.shape[1]
    return pl.pallas_call(
        functools.partial(step_kernel, dp_size, grad_scale),
        grid_spec=pltpu.PrefetchScalarGridSpec(
            num_scalar_prefetch=1,
            grid=(1,),
            in_specs=[whole_spec(grad)]
            + [pl.BlockSpec((qkv_rows, 2 * width), lambda t, meta: (meta[6], 0))] * 3
            + [pl.BlockSpec((out_rows, width), lambda t, meta: (meta[4] * chips + meta[6], 0))] * 3,
            out_specs=whole_spec(grad),
        ),
        out_shape=jax.ShapeDtypeStruct(grad.shape, bf16),
        compiler_params=pltpu.CompilerParams(vmem_limit_bytes=WHOLE_LIMIT),
        cost_estimate=pl.CostEstimate(
            flops=20 * grad.size, bytes_accessed=16 * grad.size, transcendentals=grad.size
        ),
        name="shard_step",
    )(meta, grad, *qkv, *out)


def optimizer_kernel(blocks, dp_size, grad_scale, spill, meta_ref, *refs):
    mine, refs = refs[:blocks], refs[blocks:]
    other, refs = refs[:blocks], refs[blocks:]
    qkv, out = refs[:3], refs[3:6]
    refs = refs[6 + spill :]
    step_qkv, mean_qkv, square_qkv, step_out, mean_out, square_out = refs
    core = meta_ref[4]
    top, out_rows = qkv[0].shape[0], out[0].shape[1]

    def run(mine_ref, other_ref):
        for shift in range(dp_size):
            rows = slice(shift * (top + out_rows), (shift + 1) * (top + out_rows))
            a, b = mine_ref[rows, :], other_ref[rows, :]
            whole = all_heads(a[:top], b[:top], core, dp_size).astype(f32)
            low = jnp.concatenate(
                [
                    jnp.where(core == 0, a[top:], b[top:])[None],
                    jnp.where(core == 0, b[top:], a[top:])[None],
                ],
                axis=0,
            ).astype(f32)
            if shift == 0:
                whole, mean, square = adamw(*[r[...] for r in qkv], whole, grad_scale, decay_rate)
                whole = whole.astype(bf16).astype(f32)
                mean_qkv[...] = mean
                square_qkv[...] = square
                low, mean, square = adamw(*[r[...] for r in out], low, grad_scale, decay_rate)
                low = low.astype(bf16).astype(f32)
                mean_out[...] = mean
                square_out[...] = square
            at = (meta_ref[5] + shift) % dp_size
            step_qkv[pl.ds(at, 1)] = whole[None]
            step_out[pl.ds(at, 1)] = low[None]

    for k in range(blocks):
        if blocks == 1:
            run(mine[k], other[k])
        else:
            pl.when(pl.program_id(0) == k)(functools.partial(run, mine[k], other[k]))


def optimize(meta, first_block, mine, other, qkv, out, buffers, chips, dp_size, grad_scale):
    blocks = len(mine)
    spill = 0 if buffers is None else 6
    qkv_rows = qkv[0].shape[0] // chips
    out_rows = out[0].shape[0] // (2 * chips)
    width = out[0].shape[1]
    out = [a.reshape(2, a.shape[0] // 2, width) for a in out]

    def at_chip(block, meta):
        return meta[META + first_block + block]

    own_qkv = pl.BlockSpec((qkv_rows, 2 * width), lambda b, meta: (at_chip(b, meta), 0))
    own_out = pl.BlockSpec((2, out_rows, width), lambda b, meta: (0, at_chip(b, meta), 0))
    step_qkv = pl.BlockSpec(
        (dp_size, qkv_rows, 2 * width), lambda b, meta: (0, at_chip(b, meta), 0)
    )
    step_out = pl.BlockSpec(
        (dp_size, 2, out_rows, width), lambda b, meta: (0, 0, at_chip(b, meta), 0)
    )
    shapes = [
        (dp_size,) + qkv[0].shape,
        qkv[0].shape,
        qkv[0].shape,
        (dp_size,) + out[0].shape,
        out[0].shape,
        out[0].shape,
    ]
    specs = [step_qkv, own_qkv, own_qkv, step_out, own_out, own_out]
    first = 1 + 2 * blocks + 6
    return pl.pallas_call(
        functools.partial(optimizer_kernel, blocks, dp_size, grad_scale, spill),
        grid_spec=pltpu.PrefetchScalarGridSpec(
            num_scalar_prefetch=1,
            grid=(blocks,),
            in_specs=[whole_spec(a) for a in (*mine, *other)]
            + [own_qkv] * 3
            + [own_out] * 3
            + [pl.BlockSpec(memory_space=pl.ANY)] * spill,
            out_specs=specs,
        ),
        out_shape=[jax.ShapeDtypeStruct(shape, f32) for shape in shapes],
        input_output_aliases={first + k: k for k in range(spill)},
        compiler_params=pltpu.CompilerParams(vmem_limit_bytes=WHOLE_LIMIT),
        cost_estimate=pl.CostEstimate(
            flops=blocks * qkv_rows * width * 60,
            bytes_accessed=blocks * qkv_rows * width * 90,
            transcendentals=blocks * qkv_rows * width * 3,
        ),
        name="optimize",
    )(meta, *mine, *other, *qkv, *out, *(buffers or ()))


def expert_kernel(count, tok, spill, meta_ref, *refs):
    x_refs, refs = refs[:count], refs[count:]
    cot_refs, refs = refs[:count], refs[count:]
    gate_ups, downs = refs[:2], refs[2:4]
    refs = refs[4 + spill :]
    mix_refs, refs = refs[:count], refs[count:]
    grad_refs, refs = refs[:count], refs[count:]
    x_all, cot_all, act_all, dgu_all = refs
    width = x_all.shape[-1]

    def run(x_ref, cot_ref, mix_ref, grad_ref):
        x = x_ref[:tok, :]
        cot = cot_ref[...]
        x_all[...] = x
        cot_all[...] = cot
        extra = x_ref[tok:, :].astype(f32)
        extra = extra[:, :tok] + extra[:, tok : 2 * tok]
        row = lax.broadcasted_iota(jnp.int32, extra.shape, 0)
        gates = jnp.zeros_like(extra)
        for e in range(2):
            mine = row == meta_ref[2 + e]
            weight = jnp.sum(jnp.where(mine, extra, 0.0), axis=0, keepdims=True)
            weight = jnp.transpose(jnp.broadcast_to(weight, (128, tok)))
            weight = jnp.concatenate([weight, weight], axis=1)
            gate_grad = jnp.zeros((tok, 1), f32)
            for lo in range(0, EXP_FF, 256):
                hi = lo + 256
                gate = dot(x, gate_ups[e][:, lo:hi])
                up = dot(x, gate_ups[e][:, EXP_FF + lo : EXP_FF + hi])
                dact = dot_nt(cot, downs[e][lo:hi, :])
                sig = 0.5 * jnp.tanh(0.5 * gate) + 0.5
                silu = gate * sig
                act = silu * up
                gate_grad = gate_grad + jnp.sum(act * dact, axis=-1, keepdims=True)
                act_all[:, e * EXP_FF + lo : e * EXP_FF + hi] = (act * weight).astype(bf16)
                dact = dact * weight
                dgate = dact * up * (sig + silu * (1.0 - sig))
                at = 2 * e * EXP_FF
                dgu_all[:, at + lo : at + hi] = dgate.astype(bf16)
                dgu_all[:, at + EXP_FF + lo : at + EXP_FF + hi] = (dact * silu).astype(bf16)
            gate_row = jnp.transpose(jnp.broadcast_to(gate_grad, (tok, 128)))[:1, :]
            gates = jnp.where(mine, gate_row, gates)
        acts = [act_all[:, e * EXP_FF : (e + 1) * EXP_FF] for e in range(2)]
        dgus = [dgu_all[:, 2 * e * EXP_FF : 2 * (e + 1) * EXP_FF] for e in range(2)]
        for lo in range(0, width, 256):
            mix = sum(dot(acts[e], downs[e][:, lo : lo + 256]) for e in range(2))
            mix_ref[:, lo : lo + 256] = mix.astype(bf16)
        for lo in range(0, width, 256):
            grad = sum(dot_nt(dgus[e], gate_ups[e][lo : lo + 256, :]) for e in range(2))
            grad_ref[:tok, lo : lo + 256] = grad.astype(bf16)
        high = gates.astype(bf16)
        grad_ref[tok:, :tok] = high
        grad_ref[tok:, tok : 2 * tok] = (gates - high.astype(f32)).astype(bf16)
        grad_ref[tok:, 2 * tok :] = jnp.zeros((extra.shape[0], width - 2 * tok), bf16)

    for b in range(count):
        body = functools.partial(run, x_refs[b], cot_refs[b], mix_refs[b], grad_refs[b])
        if count == 1:
            body()
        else:
            pl.when(pl.program_id(0) == b)(body)


def run_experts(meta, x_blocks, cot_blocks, weights, buffers, place, total):
    count = len(x_blocks)
    packed, width = x_blocks[0].shape
    tok = cot_blocks[0].shape[0]
    rows = count * tok
    spill = 0 if buffers is None else 4
    any_spec = pl.BlockSpec(memory_space=pl.ANY)
    stream_width = [width, width, 2 * EXP_FF, 4 * EXP_FF]
    stream = [pl.BlockSpec((tok, w), lambda g, ids: (place + g, 0)) for w in stream_width]
    out = pl.pallas_call(
        functools.partial(expert_kernel, count, tok, spill),
        grid_spec=pltpu.PrefetchScalarGridSpec(
            num_scalar_prefetch=1,
            grid=(count,),
            in_specs=[
                whole_spec(a) for a in (*x_blocks, *cot_blocks, *weights)
            ]
            + [any_spec] * spill,
            out_specs=[whole_spec(c) for c in cot_blocks]
            + [whole_spec(x) for x in x_blocks]
            + stream,
        ),
        out_shape=[jax.ShapeDtypeStruct(c.shape, bf16) for c in cot_blocks]
        + [jax.ShapeDtypeStruct(x.shape, bf16) for x in x_blocks]
        + [jax.ShapeDtypeStruct((total, w), bf16) for w in stream_width],
        input_output_aliases={1 + 2 * count + 4 + k: 2 * count + k for k in range(spill)},
        compiler_params=pltpu.CompilerParams(vmem_limit_bytes=VMEM_LIMIT),
        cost_estimate=pl.CostEstimate(
            flops=2 * 2 * rows * width * EXP_FF * 6,
            bytes_accessed=rows * width * 20 + 6 * width * width,
            transcendentals=2 * rows * EXP_FF,
        ),
        name="experts",
    )(meta, *x_blocks, *cot_blocks, *weights, *(buffers or ()))
    return out[:count], out[count : 2 * count], out[2 * count :]


def per_device(
    ring,
    tokens,
    cotangent,
    routes,
    cont_group,
    attn_gain,
    qkv_weight,
    out_weight,
    ffn_gain,
    router_weight,
    gate_up_weight,
    down_weight,
    mean_attn_gain,
    mean_qkv_weight,
    mean_out_weight,
    mean_ffn_gain,
    mean_router_weight,
    mean_gate_up_weight,
    mean_down_weight,
    square_attn_gain,
    square_qkv_weight,
    square_out_weight,
    square_ffn_gain,
    square_router_weight,
    square_gate_up_weight,
    square_down_weight,
):
    chips = ring.chips
    dp_size = lax.axis_size("dp")
    dp = lax.axis_index("dp")
    chip = lax.axis_index("chip")
    core = lax.axis_index("core")
    members = 2 * chips
    tok_count, width = tokens.shape
    experts = router_weight.shape[1]
    capacity = 5 * tok_count * TOPK // (4 * experts)
    prompt_len = PROMPT_DEV * members
    core_heads = HEADS // 2
    core_kv = KV_HEADS // 2
    q_width = core_heads * HEAD_DIM
    k_width = core_kv * HEAD_DIM

    member_pair = jnp.stack([2 * chip + core, 2 * chip + 1 - core])
    groups = jnp.concatenate([cont_group, swap(cont_group)])
    own_place = jnp.stack([core, dp, chip, 0])
    meta = jnp.concatenate([groups, member_pair, own_place, ring.chips_from(chip)])

    tokens = split_rows(tokens)
    cotangent = split_rows(cotangent)
    routes = split_rows(routes)
    tok_float = tokens.astype(f32)

    qkv_core = cast_core_columns(core, qkv_weight, dp_size)
    small = jnp.concatenate([attn_gain[None], ffn_gain[None], router_weight.T], axis=0).astype(bf16)
    small = gather_dp(small, 1)
    qkv_shards = dp_shards(qkv_core)
    gain_attn = small[0].astype(f32)
    gain_ffn = small[1].astype(f32)
    proj_router_t = small[2:]

    scale_attn = lax.rsqrt(jnp.mean(tok_float * tok_float, axis=-1, keepdims=True) + norm_eps)
    attn_in = (tok_float * scale_attn * gain_attn).astype(bf16)
    within = jnp.arange(PROMPT_DEV, dtype=jnp.int32)
    prompt_pos = member_pair[:, None] * PROMPT_DEV + within
    cont_pos = jnp.broadcast_to(prompt_len + within, (2, CLEN))
    position = jnp.stack([prompt_pos, prompt_pos, cont_pos], axis=1).reshape(-1)
    half_dim = HEAD_DIM // 2
    frequency = jnp.exp(
        jnp.arange(half_dim, dtype=f32) * (-2.0 * math.log(10000.0) / HEAD_DIM)
    )
    angles = position.astype(f32)[:, None] * frequency[None, :]
    cosine_part, sine_part = jnp.cos(angles), jnp.sin(angles)
    cosine = jnp.concatenate([cosine_part] * 4, axis=1)
    sine_signed = jnp.concatenate([-sine_part, sine_part] * 2, axis=1)
    cot_ring = RingGather(ring, cotangent)
    cot_ring.step()
    attn_in = after(attn_in, cot_ring.ends())
    cot_ring.step()
    half_rows = out_weight.shape[0] // 2
    late_gate_up, late_down, late_out = after(
        (gate_up_weight[0], down_weight[0], out_weight), cot_ring.ends()
    )
    out_core = pick_core(late_out[:half_rows], late_out[half_rows:]).astype(bf16)
    own_gate_up = lax.all_gather(late_gate_up.astype(bf16), "dp", axis=0, tiled=True)
    own_down = lax.all_gather(late_down.astype(bf16), "dp", axis=0, tiled=True)
    expert_weights = [own_gate_up, swap(own_gate_up), own_down, swap(own_down)]
    attn_other = swap(attn_in)
    attn_in2 = jnp.concatenate([attn_in, attn_other], axis=0)
    qkv_shards = after(qkv_shards, cot_ring.ends())
    while cot_ring.place < ring.half - 1:
        cot_ring.step()
    rows2 = 2 * tok_count
    queries, prompt_kv, cont_kv = project(
        meta, attn_in, attn_other, qkv_shards, cosine, sine_signed
    )
    prompt_kv = prompt_kv.reshape(2 * PROMPT_ROWS, 2 * k_width)
    prompt_kv = after(prompt_kv, cot_ring.ends())
    proj_out = gather_dp(after(out_core, qkv_shards), 0)
    small_state = [
        jnp.concatenate([a[None], f[None], r.T], axis=0)
        for a, f, r in (
            (attn_gain, ffn_gain, router_weight),
            (mean_attn_gain, mean_ffn_gain, mean_router_weight),
            (square_attn_gain, square_ffn_gain, square_router_weight),
        )
    ]
    small_state = gather_dp(after(jnp.stack(small_state), prompt_kv), 2)
    kv_blocks, state = {}, None
    for arrived in ring.gather_steps(prompt_kv):
        kv_blocks.update(arrived)
        if 2 in arrived:
            proj_qkv = join_dp(after(qkv_shards, state), 0)
        if ring.half in arrived:
            state, proj_qkv = after((state, proj_qkv))
        state = attend(
            meta,
            queries,
            ring.by_distance.index(min(arrived)),
            list(arrived.values()),
            state,
            cont_kv if 0 in arrived else None,
            ring.half in arrived,
        )
    mixed, mixed_low, lse = state
    cot_blocks = cot_ring.blocks

    part = dot(mixed_low, proj_out)
    other = swap(part[tok_count:].astype(bf16))
    hidden = tok_float + part[:tok_count] + other.astype(f32)
    scale_ffn = lax.rsqrt(jnp.mean(hidden * hidden, axis=-1, keepdims=True) + norm_eps)
    ffn_in = (hidden * scale_ffn * gain_ffn).astype(bf16)
    logits = dot_nt(proj_router_t, ffn_in)
    expert_ids = jnp.arange(experts, dtype=jnp.int32)
    hot = jnp.any(routes.T[None] == expert_ids[:, None, None], axis=1)
    hot_float = hot.astype(f32)
    shown = jnp.where(hot, logits, masked_score)
    raised = jnp.where(hot, jnp.exp(shown - jnp.max(shown, axis=0, keepdims=True)), 0.0)
    gate_probs = raised / jnp.sum(raised, axis=0, keepdims=True)
    spot = jnp.arange(tok_count, dtype=jnp.int32)
    spot = jnp.where(
        spot < PROMPT_ROWS, (spot % PROMPT_DEV) * NPROMPT + spot // PROMPT_DEV, spot
    )
    earlier = (spot[:, None] < spot[None, :]).astype(bf16)
    placed = dot(hot.astype(bf16), earlier)
    kept = hot & (placed < capacity)
    pair_weight = jnp.where(kept, gate_probs, 0.0)
    weight_high = lax.reduce_precision(pair_weight, 8, 7)
    weight_rows = jnp.concatenate([weight_high, pair_weight - weight_high], axis=1).astype(bf16)
    weight_rows = jnp.pad(weight_rows, ((0, 0), (0, width - 2 * tok_count)))
    packed = jnp.concatenate([ffn_in, weight_rows], axis=0)

    total_rows = chips * tok_count
    mix_parts, grad_parts = {}, {}
    buffers = None
    packed = after(packed, cot_ring.ends())
    ffn_ring = RingGather(ring, packed)
    arrived, place = {0: packed}, 0
    while arrived:
        later = {}
        if ffn_ring.place < ring.half:
            later = ffn_ring.step(*(buffers or ()))
        if ring.half in later:
            cot_ring.step(ffn_ring.before)
        mixes, grads, buffers = run_experts(
            meta,
            list(arrived.values()),
            [cot_blocks[r] for r in arrived],
            expert_weights,
            buffers,
            place,
            total_rows,
        )
        mix_parts.update(zip(arrived, mixes))
        grad_parts.update(zip(arrived, grads))
        place += len(arrived)
        arrived = later

    grad_sum = RingSum(ring, grad_parts[ring.half])
    grad_sum.add(grad_parts)
    x_all, cot_all, act_all, dgu_all = after(buffers, grad_sum.sent)
    other_gate_up = dot_tn(x_all, dgu_all[:, 2 * EXP_FF :]).astype(bf16)
    other_down = dot_tn(act_all[:, EXP_FF:], cot_all).astype(bf16)
    grad_sum.add(grad_parts, other_gate_up, other_down)
    other_gate_up, other_down = after((other_gate_up, other_down), grad_sum.sent)
    other_gate_up, other_down = swap(other_gate_up), swap(other_down)
    while grad_sum.place > 1:
        grad_sum.add(grad_parts, other_gate_up, other_down)
    x_all, cot_all, act_all, dgu_all = after(buffers, grad_sum.sent)
    grad_gate_up = dot_tn(x_all, dgu_all[:, : 2 * EXP_FF]) + other_gate_up.astype(f32)
    grad_gate_up = grad_gate_up.astype(bf16)
    grad_down = dot_tn(act_all[:, :EXP_FF], cot_all) + other_down.astype(f32)
    grad_down = grad_down.astype(bf16)
    grad_packed, grad_gate_up, grad_down = lax.optimization_barrier(
        (grad_sum.finish(grad_parts[0]), grad_gate_up, grad_down)
    )
    mix_sum = RingSum(ring, after(mix_parts[ring.half], grad_sum.arrived()))

    def shards_dp(whole):
        pieces = whole.reshape((dp_size, whole.shape[0] // dp_size) + whole.shape[1:])
        out = [lax.dynamic_index_in_dim(pieces, dp, 0, False)]
        for shift in range(1, dp_size):
            perm = [(k, (k + shift) % dp_size) for k in range(dp_size)]
            part = lax.dynamic_index_in_dim(pieces, (dp + shift) % dp_size, 0, False)
            out.append(lax.ppermute(part, "dp", perm))
        return out

    def sum_of(pieces, *others):
        return sum(piece.astype(f32) for piece in after(pieces, others))


    grad_gate = grad_packed[tok_count:, :tok_count] + grad_packed[tok_count:, tok_count : 2 * tok_count]
    grad_gate = jnp.where(kept, grad_gate, 0.0)
    grad_chosen = gate_probs * (grad_gate - jnp.sum(gate_probs * grad_gate, axis=0, keepdims=True))
    grad_logits = (hot_float * grad_chosen).astype(bf16)
    grad_router_t = dot(grad_logits, ffn_in)
    grad_ffn = grad_packed[:tok_count] + dot_tn(grad_logits, proj_router_t)
    grad_output = cotangent.astype(f32)
    grad_hidden_norm, grad_gain_ffn = norm_back(hidden, scale_ffn, gain_ffn, grad_ffn)
    grad_hidden = grad_output + grad_hidden_norm
    grad_attn = after(grad_hidden.astype(bf16), mix_sum.arrived())
    grad_attn2 = jnp.concatenate([grad_attn, swap(grad_attn)], axis=0)
    grad_mixed = dot_nt(grad_attn2, proj_out).astype(bf16)
    mix_sum.add(mix_parts, grad_mixed)

    grad_scale = (tok_count * dp_size * members) ** (-0.5)

    dq, dkv, dkv_sum = None, (), None
    for turn_no, places in enumerate(ring.groups()[::-1]):
        if turn_no >= 2:
            grad_mixed = after(grad_mixed, dkv_before)
        if 0 in places or (turn_no % 2 == 0 and mix_sum.place > 3):
            grad_mixed = after(grad_mixed, mix_sum.arrived())
            mix_sum.add(mix_parts, dkv)
        dkv = attend_back(
            meta,
            queries,
            grad_mixed,
            mixed,
            lse,
            ring.by_distance.index(min(places)),
            [kv_blocks[r] for r in places],
            dq,
            (cont_kv, cosine, sine_signed) if 0 in places else None,
        )
        parts = dict(zip(places, dkv))
        if ring.half in places:
            dkv_sum = RingSum(ring, parts[ring.half])
        elif 0 not in places:
            grad_out_weight = dot_tn(after(mixed_low, dkv), grad_attn2)
            if turn_no == 1:
                late_gate_up, late_down = after((grad_gate_up, grad_down), dkv)
                gate_up_shards, down_shards = shards_dp(late_gate_up), shards_dp(late_down)
            dkv_before = dkv_sum.arrived()
            dkv_sum.add(parts)
        if 0 not in places:
            dq = dkv[len(places)]
    grad_projected = projected_grad(
        dkv[1], (parts[0], *dkv_sum.arrived()), dkv[2], cosine, sine_signed
    )
    grad_qkv_weight = dot_tn(attn_in2, grad_projected)
    part = dot_nt(grad_projected, proj_qkv)
    other_part = swap(part[tok_count:].astype(bf16))

    qkv_rows = width // dp_size // chips
    out_rows = HEADS * HEAD_DIM // dp_size // 2 // chips
    dense_parts = order_parts(
        meta, grad_qkv_weight.astype(bf16), grad_out_weight.astype(bf16), chips, dp_size
    )
    parts = {r: dense_parts[k] for k, r in enumerate(ring.by_distance)}
    dense_sum = RingSum(ring, parts[ring.half])
    dense_sum.add(parts, mix_sum.arrived())
    gate_up_new = adamw(
        gate_up_weight,
        mean_gate_up_weight,
        square_gate_up_weight,
        sum_of(gate_up_shards, dense_sum.sent)[None],
        grad_scale,
        decay_rate,
    )
    dense_sum.add(parts, gate_up_new, other_part)
    grad_attn_in = part[:tok_count] + after(other_part, dense_sum.sent).astype(f32)
    grad_tok_norm, grad_gain_attn = norm_back(tok_float, scale_attn, gain_attn, grad_attn_in)
    input_grad = grad_hidden + grad_tok_norm
    small_grad = jnp.concatenate(
        [grad_gain_attn[None], grad_gain_ffn[None], grad_router_t], axis=0
    )
    down_new = adamw(
        down_weight,
        mean_down_weight,
        square_down_weight,
        sum_of(down_shards, dense_sum.sent)[None],
        grad_scale,
        decay_rate,
    )
    dense_sum.add(parts, down_new, small_grad)
    while dense_sum.place > 1:
        dense_sum.add(parts)
    for small_grad in total_stages(small_grad, ("core", "dp")):
        pass
    dense = after(dense_sum.finish(parts[0]), small_grad)
    dense = dense.reshape(dp_size, qkv_rows + out_rows, width)
    mix_sum.add(mix_parts, dense)
    shard = lax.dynamic_index_in_dim(dense, dp, 0, False)
    for shift in range(1, dp_size):
        perm = [(k, (k + shift) % dp_size) for k in range(dp_size)]
        sent = lax.dynamic_index_in_dim(dense, (dp + shift) % dp_size, 0, False)
        shard = shard + lax.ppermute(sent.astype(bf16), "dp", perm).astype(f32)
    shard_low = shard.astype(bf16)

    qkv_state = (qkv_weight, mean_qkv_weight, square_qkv_weight)
    out_state = (out_weight, mean_out_weight, square_out_weight)
    step_shard = shard_step(
        meta, shard_low, qkv_state, out_state, chips, dp_size, grad_scale
    )
    small_rows = -(-small_grad.shape[0] // 16) * 16
    small_low = jnp.pad(small_grad.astype(bf16), ((0, small_rows - small_grad.shape[0]), (0, 0)))
    carried = jnp.concatenate([shard_low, *dp_shards(step_shard)[1:], small_low], axis=0)
    input_grad = merge_rows(input_grad)
    carried = after(carried, mix_sum.arrived(), input_grad)
    while mix_sum.place > 1:
        mix_sum.add(mix_parts, step_shard)
    output = hidden + mix_sum.finish(mix_parts[0])
    dense_new = None
    dense_ring = RingGather(ring, carried)
    arrived, first_place, earlier = dict(dense_ring.blocks), 0, ()
    while arrived:
        later = {}
        if dense_ring.place < ring.half:
            later = dense_ring.step(*earlier)
        earlier = tuple(dense_new or ())
        dense_new = optimize(
            meta,
            first_place,
            list(arrived.values()),
            [swap(m) for m in arrived.values()],
            qkv_state,
            out_state,
            dense_new,
            chips,
            dp_size,
            grad_scale,
        )
        first_place += len(arrived)
        arrived = later
    dense_new = [a.reshape(-1, a.shape[-1]) for a in dense_new]

    base = dp_size * (qkv_rows + out_rows)
    count = small_grad.shape[0]
    small_total = sum(
        dense_ring.blocks[r][base : base + count].astype(f32) for r in ring.by_distance
    )
    decays = jnp.full((count, 1), decay_rate, f32).at[:2].set(0.0)
    small_new = adamw(*small_state, small_total, grad_scale, decays)
    shard_cols = width // dp_size
    small_step = small_new[0]
    small_mean, small_square = [
        lax.dynamic_slice_in_dim(a, dp * shard_cols, shard_cols, 1) for a in small_new[1:]
    ]

    step_gate_up = lax.all_gather(gate_up_new[0].astype(bf16), "dp", axis=1, tiled=True)
    step_down = lax.all_gather(down_new[0].astype(bf16), "dp", axis=1, tiled=True)
    return (
        merge_rows(output.astype(bf16)),
        input_grad,
        small_step[0],
        dense_new[0],
        dense_new[3],
        small_step[1],
        small_step[2:].T,
        step_gate_up.astype(f32),
        step_down.astype(f32),
        small_mean[0],
        dense_new[1],
        dense_new[4],
        small_mean[1],
        small_mean[2:].T,
        gate_up_new[1],
        down_new[1],
        small_square[0],
        dense_new[2],
        dense_new[5],
        small_square[1],
        small_square[2:].T,
        gate_up_new[2],
        down_new[2],
    )


def solution(mesh):
    dp_size, members = mesh.shape["dp"], mesh.shape["expert"]
    chips = members // 2
    fine = Mesh(mesh.devices.reshape(dp_size, chips, 2), ("dp", "chip", "core"))
    ring = Ring(chips)
    member = ("chip", "core")
    token = P(("dp",) + member, None)
    matrices = (P("dp"), P("dp", None), P("dp", None), P("dp"), P("dp", None))
    expert = (P(member, "dp", None), P(member, "dp", None))

    def body(*arrays):
        return per_device(ring, *arrays)

    return jax.shard_map(
        body,
        mesh=fine,
        in_specs=(token, token, token, P(("dp",) + member)) + (matrices + expert) * 3,
        out_specs=(token, token)
        + (P(),) * 5
        + (P(member, None, None),) * 2
        + (matrices + expert) * 2,
        check_vma=False,
    )
```

```python
import functools
import math

import jax
import jax.numpy as jnp
from jax import lax
from jax.experimental import pallas as pl
from jax.experimental.pallas import tpu as pltpu
from jax.sharding import Mesh
from jax.sharding import PartitionSpec as P

HEADS = 16
KV_HEADS = 8
HEAD_DIM = 64
EXP_FF = 512
TOPK = 8
NPROMPT = 2
PROMPT_DEV = 128
CLEN = 128
REPEAT = HEADS // KV_HEADS
PROMPT_ROWS = NPROMPT * PROMPT_DEV

norm_eps = 1e-05
masked_score = -1e30
decay_rate = 0.1
adam_eps = 1e-08
bias_first = 0.999973438601112
bias_second = 0.99407947078
score_scale = HEAD_DIM ** (-0.5)

bf16 = jnp.bfloat16
f32 = jnp.float32


def dot(left, right):
    return jnp.dot(left, right, preferred_element_type=f32)


def dot_tn(left, right):
    return lax.dot_general(left, right, (((0,), (0,)), ((), ())), preferred_element_type=f32)


def dot_nt(left, right):
    return lax.dot_general(left, right, (((1,), (1,)), ((), ())), preferred_element_type=f32)


def norm_back(values, scale_rows, gain_row, grad_rows):
    normed = values * scale_rows
    grad_normed = grad_rows * gain_row
    grad_values = scale_rows * (
        grad_normed - normed * jnp.mean(grad_normed * normed, axis=-1, keepdims=True)
    )
    return (grad_values, jnp.sum(grad_rows * normed, axis=0))


def adamw(weight, mean_in, square_in, gradient, grad_scale, decay_factor):
    scaled = gradient * grad_scale
    mean_out = 0.9 * mean_in + 0.1 * scaled
    square_out = 0.95 * square_in + 0.05 * scaled * scaled
    spread = square_out * (1.0 / bias_second)
    spread = spread * lax.rsqrt(spread) + adam_eps
    update = mean_out * (1.0 / bias_first) / spread
    return (update + decay_factor * weight, mean_out, square_out)


def split_rows(values):
    head = values[:PROMPT_ROWS].reshape(PROMPT_DEV, NPROMPT, -1).transpose(1, 0, 2)
    return jnp.concatenate([head.reshape(PROMPT_ROWS, -1), values[PROMPT_ROWS:]], axis=0)


def merge_rows(values):
    head = values[:PROMPT_ROWS].reshape(NPROMPT, PROMPT_DEV, -1).transpose(1, 0, 2)
    return jnp.concatenate([head.reshape(PROMPT_ROWS, -1), values[PROMPT_ROWS:]], axis=0)


def swap(values):
    return lax.ppermute(values, "core", [(0, 1), (1, 0)])


class Ring:
    def __init__(self, chips):
        rows = 4 if chips % 4 == 0 else chips
        cols = chips // rows
        cycle = [(0, x) for x in range(cols)]
        for z in range(1, rows):
            line = [(z, x) for x in range(1, cols)]
            cycle += line[::-1] if z % 2 == 1 else line
        if cols > 1:
            cycle += [(z, 0) for z in range(rows - 1, 0, -1)]
        else:
            cycle = [(z, 0) for z in range(rows)]
        self.chips = chips
        self.order = [z * cols + x for z, x in cycle]
        self.forward = [
            (self.order[k], self.order[(k + 1) % chips]) for k in range(chips)
        ]
        self.backward = [(b, a) for a, b in self.forward]
        self.half = chips // 2
        self.by_distance = [r for group in self.groups() for r in group]

    def chips_from(self, me):
        table = [[0] * self.chips for _ in range(self.chips)]
        for k in range(self.chips):
            for column, offset in enumerate(self.by_distance):
                table[self.order[k]][column] = self.order[(k + offset) % self.chips]
        return lax.dynamic_index_in_dim(jnp.asarray(table, jnp.int32), me, 0, False)

    def gather_steps(self, block):
        gather = RingGather(self, block)
        yield {0: block}
        for _ in range(self.half):
            yield gather.step()

    @staticmethod
    def cut(block):
        return block.shape[0] // 32 * 16

    def groups(self):
        return [[0]] + [[-s, s] for s in range(1, self.half)] + [[self.half]]


class RingGather:
    def __init__(self, ring, block):
        self.ring = ring
        self.place = 0
        self.ahead = self.behind = block
        self.blocks = {0: block}

    def ends(self):
        return (self.ahead, self.behind)

    def step(self, *others):
        ring = self.ring
        self.place += 1
        if others:
            self.ahead, self.behind = after(self.ends(), others)
        self.before = self.ends()
        if self.place < ring.half:
            self.ahead = lax.ppermute(self.ahead, "chip", ring.forward)
            self.behind = lax.ppermute(self.behind, "chip", ring.backward)
            arrived = {-self.place: self.ahead, self.place: self.behind}
        else:
            cut = ring.cut(self.ahead)
            first = lax.ppermute(self.ahead[:cut], "chip", ring.forward)
            second = lax.ppermute(self.behind[cut:], "chip", ring.backward)
            arrived = {ring.half: jnp.concatenate([first, second], axis=0)}
        self.blocks.update(arrived)
        return arrived


class RingSum:
    def __init__(self, ring, part):
        cut = ring.cut(part)
        self.ring = ring
        self.place = ring.half
        self.cut = cut
        self.sent = (part[:cut], part[cut:])
        self.send()

    def send(self):
        self.ahead = lax.ppermute(self.sent[0], "chip", self.ring.forward)
        self.behind = lax.ppermute(self.sent[1], "chip", self.ring.backward)

    def arrived(self):
        return (self.ahead, self.behind)

    def add(self, parts, *others):
        ring, cut = self.ring, self.cut
        self.place -= 1
        up, down = parts[self.place], parts[-self.place]
        if others:
            up, down = after((up, down), others)
        self.ahead, self.behind = lax.optimization_barrier((self.ahead, self.behind))
        if self.place == ring.half - 1:
            ahead = jnp.concatenate([self.ahead + up[:cut], up[cut:]], axis=0)
            behind = jnp.concatenate([down[:cut], self.behind + down[cut:]], axis=0)
        else:
            ahead, behind = self.ahead + up, self.behind + down
        self.sent = (ahead, behind)
        self.send()

    def finish(self, part):
        return part.astype(f32) + self.ahead.astype(f32) + self.behind.astype(f32)


def after(values, *others):
    return lax.optimization_barrier((values, others))[0]


def total_stages(values, axes):
    for axis in axes:
        size = lax.axis_size(axis)
        reach = 1
        while reach < size:
            values = values + lax.ppermute(values, axis, [(k, k ^ reach) for k in range(size)])
            reach *= 2
            yield values


def dp_shards(values):
    size = lax.axis_size("dp")
    pieces = [values]
    for shift in range(1, size):
        perm = [(k, (k - shift) % size) for k in range(size)]
        pieces.append(lax.ppermute(values, "dp", perm))
    return pieces


def join_dp(pieces, axis):
    size = len(pieces)
    dp = lax.axis_index("dp")
    if size == 2:
        return jnp.concatenate(
            [
                jnp.where(dp == 0, pieces[0], pieces[1]),
                jnp.where(dp == 0, pieces[1], pieces[0]),
            ],
            axis=axis,
        )
    twice = jnp.concatenate(pieces + pieces, axis=axis)
    shard = pieces[0].shape[axis]
    return lax.dynamic_slice_in_dim(twice, (size - dp) % size * shard, size * shard, axis)


def gather_dp(values, axis):
    return join_dp(dp_shards(values), axis)


def pick_core(first, second):
    return jnp.where(lax.axis_index("core") == 0, first, second)


LOG2E = 1.4426950408889634


def stack_heads(wide):
    wide = wide.astype(f32)
    first, second = wide[:, :128], wide[:, 128:]
    lane = lax.broadcasted_iota(jnp.int32, first.shape, 1)
    low_lanes = lane < HEAD_DIM
    zero = jnp.zeros_like(first)
    return jnp.concatenate(
        [
            jnp.where(low_lanes, first, zero),
            jnp.where(low_lanes, pltpu.roll(first, HEAD_DIM, 1), zero),
            jnp.where(low_lanes, zero, pltpu.roll(second, HEAD_DIM, 1)),
            jnp.where(low_lanes, zero, second),
        ],
        axis=0,
    )


def unstack_heads(tall):
    rows = tall.shape[0] // 4
    parts = [tall[k * rows : (k + 1) * rows] for k in range(4)]
    lane = lax.broadcasted_iota(jnp.int32, parts[0].shape, 1)
    low_lanes = lane < HEAD_DIM
    return jnp.concatenate(
        [
            jnp.where(low_lanes, parts[0], pltpu.roll(parts[1], HEAD_DIM, 1)),
            jnp.where(low_lanes, pltpu.roll(parts[2], HEAD_DIM, 1), parts[3]),
        ],
        axis=1,
    )


def row_of(column_sum_of):
    return jnp.sum(jnp.transpose(column_sum_of), axis=0, keepdims=True)


def tile_masks(meta_ref, half, is_cont):
    shape = (PROMPT_ROWS, 4 * PROMPT_DEV)
    key = lax.broadcasted_iota(jnp.int32, shape, 0)
    query = lax.broadcasted_iota(jnp.int32, shape, 1) % PROMPT_DEV
    key_member = jnp.where(key < PROMPT_DEV, meta_ref[2], meta_ref[3])
    key_pos = key_member * PROMPT_DEV + key % PROMPT_DEV
    query_pos = meta_ref[2 + half] * PROMPT_DEV + query
    own = (key_pos <= query_pos) | is_cont
    shape = (CLEN, 4 * CLEN)
    key = lax.broadcasted_iota(jnp.int32, shape, 0)
    query = lax.broadcasted_iota(jnp.int32, shape, 1) % CLEN
    self_seen = (key <= query) & is_cont
    return own, self_seen


META = 8


def block_bias(meta_ref, is_cont, first_block, blocks):
    chips = [meta_ref[META + first_block + k] for k in range(blocks)]
    return [jnp.where(is_cont | (c <= meta_ref[6]), 0.0, masked_score) for c in chips]


def attend_kernel(first_block, blocks, first, last, meta_ref, q_ref, *refs):
    kv_refs, refs = refs[:blocks], refs[blocks:]
    if first:
        self_ref, refs = refs[0], refs[1:]
    else:
        acc_in, stat_in = refs[:2]
        refs = refs[2:]
    if last:
        out_ref, low_ref, lse_ref, scores = refs
    else:
        acc_out, stat_out, scores = refs
    tile = pl.program_id(0)
    half = tile // 3
    part = tile % 3
    is_cont = part == NPROMPT
    prompt = jnp.where(is_cont, meta_ref[half], part)
    rows = pl.ds(pl.multiple_of(prompt * PROMPT_ROWS, PROMPT_ROWS), PROMPT_ROWS)
    if first:
        own, self_seen = tile_masks(meta_ref, half, is_cont)
    bias = block_bias(meta_ref, is_cont, first_block, blocks)
    scale = score_scale * LOG2E
    k_width = KV_HEADS // 2 * HEAD_DIM
    for pair in range(2):
        lanes = pl.ds(pair * 128, 128)
        v_lanes = pl.ds(k_width + pair * 128, 128)
        q = stack_heads(q_ref[:, pair * 256 : (pair + 1) * 256]).astype(bf16)
        if first:
            s_self = jnp.where(self_seen, dot_nt(self_ref[0, :, lanes], q), masked_score)
            top = jnp.max(s_self, axis=0, keepdims=True)
        else:
            old = stat_in[0, pair, :1, :]
            top = old
        for k in range(blocks):
            s = dot_nt(kv_refs[k][rows, lanes], q)
            if first:
                s = jnp.where(own, s, masked_score)
            scores[pl.ds(k * PROMPT_ROWS, PROMPT_ROWS), :] = s
            top = jnp.maximum(top, jnp.max(s, axis=0, keepdims=True) + bias[k])
        top2 = top * scale
        if first:
            p = jnp.exp2(s_self * scale - top2)
            total = jnp.sum(p, axis=0, keepdims=True)
            acc = dot(jnp.transpose(self_ref[0, :, v_lanes]), p.astype(bf16))
        else:
            factor = jnp.exp2(old * scale - top2)
            total = stat_in[0, pair, 1:2, :] * factor
            acc = acc_in[0, pair] * factor
        for k in range(blocks):
            s = scores[pl.ds(k * PROMPT_ROWS, PROMPT_ROWS), :]
            p = jnp.exp2(s * scale - (top2 - bias[k]))
            total = total + jnp.sum(p, axis=0, keepdims=True)
            acc = acc + dot(jnp.transpose(kv_refs[k][rows, v_lanes]), p.astype(bf16))
        if last:
            out = unstack_heads(jnp.transpose(acc / total))
            out_ref[:, pair * 256 : (pair + 1) * 256] = out
            low_ref[:, pair * 256 : (pair + 1) * 256] = out.astype(bf16)
            lse = top2 + jnp.log2(total)
            for head in range(4):
                lse_ref[pl.ds(pair * 4 + head, 1), :] = lse[
                    :, head * PROMPT_DEV : (head + 1) * PROMPT_DEV
                ]
        else:
            acc_out[0, pair] = acc
            stat_out[0, pair, :1, :] = top
            stat_out[0, pair, 1:2, :] = total


def attend_back_kernel(first_block, blocks, first, last, meta_ref, q_ref, do_ref, out_ref, lse_ref, *refs):
    kv_refs, refs = refs[:blocks], refs[blocks:]
    if last:
        self_ref, cos_ref, sin_ref = refs[:3]
        refs = refs[3:]
    if not first:
        dq_in, refs = refs[0], refs[1:]
    dkv_refs, refs = refs[:blocks], refs[blocks:]
    if last:
        dq_ref, dself_ref, acc = refs
    else:
        dq_out, acc = refs
    tile = pl.program_id(0)
    half = tile // 3
    part = tile % 3
    is_cont = part == NPROMPT
    prompt = jnp.where(is_cont, meta_ref[half], part)
    start = pl.multiple_of(prompt * PROMPT_ROWS, PROMPT_ROWS)
    rows = pl.ds(start, PROMPT_ROWS)
    if last:
        own, self_seen = tile_masks(meta_ref, half, is_cont)
    bias = block_bias(meta_ref, is_cont, first_block, blocks)
    scale = score_scale * LOG2E
    k_width = KV_HEADS // 2 * HEAD_DIM

    @pl.when(tile == 0)
    def _():
        acc[...] = jnp.zeros_like(acc)

    for pair in range(2):
        lanes = pl.ds(pair * 128, 128)
        v_lanes = pl.ds(k_width + pair * 128, 128)
        cut = slice(pair * 256, (pair + 1) * 256)
        q = stack_heads(q_ref[:, cut]).astype(bf16)
        do_wide = stack_heads(do_ref[:, cut])
        delta = row_of(do_wide * stack_heads(out_ref[:, cut]))
        do = do_wide.astype(bf16)
        lse = jnp.concatenate(
            [lse_ref[pl.ds(pair * 4 + head, 1), :] for head in range(4)], axis=1
        )
        dq = jnp.zeros((128, 4 * PROMPT_DEV), f32) if first else dq_in[0, pair]
        for k in range(blocks):
            key, value = kv_refs[k][rows, lanes], kv_refs[k][rows, v_lanes]
            s = dot_nt(key, q)
            if last:
                s = jnp.where(own, s, masked_score)
            p = jnp.exp2(s * scale - (lse - bias[k]))
            ds = (p * (dot_nt(value, do) - delta)).astype(bf16)
            dq = dq + dot(jnp.transpose(key), ds)
            acc[k, rows, lanes] += dot(ds, q)
            acc[k, rows, v_lanes] += dot(p.astype(bf16), do)
        if last:
            key, value = self_ref[0, :, lanes], self_ref[0, :, v_lanes]
            s = jnp.where(self_seen, dot_nt(key, q), masked_score)
            p = jnp.exp2(s * scale - lse)
            ds = (p * (dot_nt(value, do) - delta)).astype(bf16)
            dq = dq + dot(jnp.transpose(key), ds)
            dself_ref[0, :, lanes] = dot(ds, q) * score_scale
            dself_ref[0, :, v_lanes] = dot(p.astype(bf16), do)
            wide = unstack_heads(jnp.transpose(dq)) * score_scale
            for group in range(2):
                turned = turn(wide[:, group * 128 : (group + 1) * 128], cos_ref[...], -sin_ref[...])
                lo = pair * 256 + group * 128
                dq_ref[:, lo : lo + 128] = turned.astype(bf16)
        else:
            dq_out[0, pair] = dq

    @pl.when(tile == pl.num_programs(0) - 1)
    def _():
        for k in range(blocks):
            dkv_refs[k][:, :k_width] = (acc[k, :, :k_width] * score_scale).astype(bf16)
            dkv_refs[k][:, k_width:] = acc[k, :, k_width:].astype(bf16)


def turn(values, cosine, sine_signed):
    lane = lax.broadcasted_iota(jnp.int32, values.shape, 1) % HEAD_DIM
    swapped = jnp.where(
        lane < HEAD_DIM // 2,
        pltpu.roll(values, 128 - HEAD_DIM // 2, 1),
        pltpu.roll(values, HEAD_DIM // 2, 1),
    )
    return values * cosine + swapped * sine_signed


VMEM_LIMIT = 40 * 1024 * 1024
SMALL_LIMIT = 24 * 1024 * 1024
WHOLE_LIMIT = 60 * 1024 * 1024


def whole_spec(array):
    return pl.BlockSpec(
        array.shape, lambda *_: (0,) * array.ndim, pipeline_mode=pl.Buffered(1)
    )


def attend(meta, queries, first_block, kv_blocks, state, cont_kv=None, last=False):
    blocks = len(kv_blocks)
    first = state is None
    rows, q_width = queries.shape
    tiles = rows // PROMPT_DEV
    columns = 4 * PROMPT_DEV
    row_spec = pl.BlockSpec((PROMPT_DEV, q_width), lambda t, meta: (t, 0))
    lse_spec = pl.BlockSpec((HEADS // 2, PROMPT_DEV), lambda t, meta: (0, t))
    acc_spec = pl.BlockSpec((1, 2, 128, columns), lambda t, meta: (t, 0, 0, 0))
    stat_spec = pl.BlockSpec((1, 2, 8, columns), lambda t, meta: (t, 0, 0, 0))
    pairs = rows * HEADS // 2 * blocks * PROMPT_ROWS
    in_specs = [row_spec] + [whole_spec(b) for b in kv_blocks]
    operands = [meta, queries, *kv_blocks]
    if first:
        in_specs.append(pl.BlockSpec((1,) + cont_kv.shape[1:], lambda t, meta: (t // 3, 0, 0)))
        operands.append(cont_kv)
    else:
        in_specs += [acc_spec, stat_spec]
        operands += list(state)
    if last:
        out_specs = [row_spec, row_spec, lse_spec]
        out_shape = [
            jax.ShapeDtypeStruct((rows, q_width), f32),
            jax.ShapeDtypeStruct((rows, q_width), bf16),
            jax.ShapeDtypeStruct((HEADS // 2, rows), f32),
        ]
    else:
        out_specs = [acc_spec, stat_spec]
        out_shape = [
            jax.ShapeDtypeStruct((tiles, 2, 128, columns), f32),
            jax.ShapeDtypeStruct((tiles, 2, 8, columns), f32),
        ]
    return pl.pallas_call(
        functools.partial(attend_kernel, first_block, blocks, first, last),
        grid_spec=pltpu.PrefetchScalarGridSpec(
            num_scalar_prefetch=1,
            grid=(tiles,),
            in_specs=in_specs,
            out_specs=out_specs,
            scratch_shapes=[pltpu.VMEM((blocks * PROMPT_ROWS, columns), f32)],
        ),
        out_shape=out_shape,
        compiler_params=pltpu.CompilerParams(vmem_limit_bytes=VMEM_LIMIT),
        cost_estimate=pl.CostEstimate(
            flops=48 * 64 * pairs, bytes_accessed=12 << 20, transcendentals=pairs
        ),
        name="attend",
    )(*operands)


def attend_back(meta, queries, grads, mixed, lse, first_block, kv_blocks, dq, own=None):
    blocks = len(kv_blocks)
    first, last = dq is None, own is not None
    rows, q_width = queries.shape
    tiles = rows // PROMPT_DEV
    columns = 4 * PROMPT_DEV
    row_spec = pl.BlockSpec((PROMPT_DEV, q_width), lambda t, meta: (t, 0))
    lse_spec = pl.BlockSpec((HEADS // 2, PROMPT_DEV), lambda t, meta: (0, t))
    dq_spec = pl.BlockSpec((1, 2, 128, columns), lambda t, meta: (t, 0, 0, 0))
    block = kv_blocks[0]
    pairs = rows * HEADS // 2 * blocks * PROMPT_ROWS
    in_specs = [row_spec, row_spec, row_spec, lse_spec] + [whole_spec(b) for b in kv_blocks]
    operands = [meta, queries, grads, mixed, lse, *kv_blocks]
    out_specs = [whole_spec(b) for b in kv_blocks]
    out_shape = [jax.ShapeDtypeStruct(b.shape, bf16) for b in kv_blocks]
    if last:
        cont_kv, cosine, sine = own
        self_spec = pl.BlockSpec((1,) + cont_kv.shape[1:], lambda t, meta: (t // 3, 0, 0))
        turn_spec = pl.BlockSpec((PROMPT_DEV, 128), lambda t, meta: (t, 0))
        in_specs += [self_spec, turn_spec, turn_spec]
        operands += [cont_kv, cosine, sine]
        out_specs += [row_spec, self_spec]
        out_shape += [
            jax.ShapeDtypeStruct((rows, q_width), bf16),
            jax.ShapeDtypeStruct(cont_kv.shape, f32),
        ]
    else:
        out_specs.append(dq_spec)
        out_shape.append(jax.ShapeDtypeStruct((tiles, 2, 128, columns), f32))
    if not first:
        in_specs.append(dq_spec)
        operands.append(dq)
    return pl.pallas_call(
        functools.partial(attend_back_kernel, first_block, blocks, first, last),
        grid_spec=pltpu.PrefetchScalarGridSpec(
            num_scalar_prefetch=1,
            grid=(tiles,),
            in_specs=in_specs,
            out_specs=out_specs,
            scratch_shapes=[pltpu.VMEM((blocks,) + block.shape, f32)],
        ),
        out_shape=out_shape,
        compiler_params=pltpu.CompilerParams(vmem_limit_bytes=VMEM_LIMIT),
        cost_estimate=pl.CostEstimate(
            flops=110 * 64 * pairs, bytes_accessed=16 << 20, transcendentals=pairs
        ),
        name="attend_back",
    )(*operands)


def core_pieces(columns, core, dp_size):
    width = columns.shape[-1] // (2 * dp_size)
    pieces = []
    for s in range(dp_size):
        lo = 2 * s * width
        pieces.append(
            jnp.where(core == 0, columns[:, lo : lo + width], columns[:, lo + width : lo + 2 * width])
        )
    return pieces


def core_heads(columns, core, dp_size):
    q, k = HEADS * HEAD_DIM, KV_HEADS * HEAD_DIM
    cuts = [columns[:, :q], columns[:, q : q + k], columns[:, q + k :]]
    return jnp.concatenate([p for cut in cuts for p in core_pieces(cut, core, dp_size)], axis=1)


def all_heads(mine, other, core, dp_size):
    first, second = jnp.where(core == 0, mine, other), jnp.where(core == 0, other, mine)
    q, k = HEADS // 2 * HEAD_DIM, KV_HEADS // 2 * HEAD_DIM
    pieces = []
    for lo, size in ((0, q), (q, k), (q + k, k)):
        width = size // dp_size
        for s in range(dp_size):
            cut = slice(lo + s * width, lo + (s + 1) * width)
            pieces += [first[:, cut], second[:, cut]]
    return jnp.concatenate(pieces, axis=1)


def cast_kernel(dp_size, meta_ref, weight_ref, out_ref):
    out_ref[...] = core_heads(weight_ref[...], meta_ref[0], dp_size).astype(bf16)


def cast_core_columns(core, weight, dp_size):
    rows, columns = weight.shape
    tile = rows // 4
    return pl.pallas_call(
        functools.partial(cast_kernel, dp_size),
        grid_spec=pltpu.PrefetchScalarGridSpec(
            num_scalar_prefetch=1,
            grid=(4,),
            in_specs=[pl.BlockSpec((tile, columns), lambda t, meta: (t, 0))],
            out_specs=pl.BlockSpec((tile, columns // 2), lambda t, meta: (t, 0)),
        ),
        out_shape=jax.ShapeDtypeStruct((rows, columns // 2), bf16),
        compiler_params=pltpu.CompilerParams(vmem_limit_bytes=SMALL_LIMIT),
        cost_estimate=pl.CostEstimate(
            flops=rows * columns, bytes_accessed=5 * rows * columns, transcendentals=0
        ),
        name="cast_core_columns",
    )(core[None], weight)


def project_kernel(shards, meta_ref, own_ref, other_ref, *refs):
    weights = refs[:shards]
    cos_ref, sin_ref, q_ref, prompt_ref, cont_ref = refs[shards:]
    half = pl.program_id(0)
    depth = weights[0].shape[0]
    q_width = q_ref.shape[-1]
    k_width = cont_ref.shape[-1] // 2
    cosine, sine = cos_ref[...], sin_ref[...]

    def run(x_ref):
        xs = []
        for k in range(shards):
            start = pl.multiple_of((meta_ref[5] + k) % shards * depth, depth)
            xs.append(x_ref[:, pl.ds(start, depth)])
        for lo in range(0, q_width + 2 * k_width, 128):
            if lo % 256 == 0:
                out = sum(dot(x, w[:, lo : lo + 256]) for x, w in zip(xs, weights))
            piece = out[:, lo % 256 : lo % 256 + 128]
            if lo < q_width + k_width:
                piece = turn(piece, cosine, sine)
            piece = piece.astype(bf16)
            if lo < q_width:
                q_ref[:, lo : lo + 128] = piece
            else:
                at = lo - q_width
                for g in range(NPROMPT):
                    rows = piece[g * PROMPT_DEV : (g + 1) * PROMPT_DEV]
                    prompt_ref[g, 0, :, at : at + 128] = rows
                cont_ref[0, :, at : at + 128] = piece[PROMPT_ROWS:]

    pl.when(half == 0)(lambda: run(own_ref))
    pl.when(half == 1)(lambda: run(other_ref))


def project(meta, own, other, weights, cosine, sine):
    rows, width = own.shape
    columns = weights[0].shape[1]
    kv_width = columns // 2
    turn_spec = pl.BlockSpec((rows, 128), lambda h, meta: (h, 0))
    return pl.pallas_call(
        functools.partial(project_kernel, len(weights)),
        grid_spec=pltpu.PrefetchScalarGridSpec(
            num_scalar_prefetch=1,
            grid=(2,),
            in_specs=[whole_spec(a) for a in (own, other, *weights)] + [turn_spec] * 2,
            out_specs=[
                pl.BlockSpec((rows, columns - kv_width), lambda h, meta: (h, 0)),
                pl.BlockSpec((NPROMPT, 1, PROMPT_DEV, kv_width), lambda h, meta: (0, h, 0, 0)),
                pl.BlockSpec((1, CLEN, kv_width), lambda h, meta: (h, 0, 0)),
            ],
        ),
        out_shape=[
            jax.ShapeDtypeStruct((2 * rows, columns - kv_width), bf16),
            jax.ShapeDtypeStruct((NPROMPT, 2, PROMPT_DEV, kv_width), bf16),
            jax.ShapeDtypeStruct((2, CLEN, kv_width), bf16),
        ],
        compiler_params=pltpu.CompilerParams(vmem_limit_bytes=SMALL_LIMIT),
        cost_estimate=pl.CostEstimate(
            flops=4 * rows * width * columns, bytes_accessed=8 << 20, transcendentals=0
        ),
        name="project",
    )(meta, own, other, *weights, cosine, sine)


def projected_grad_kernel(dq_ref, *refs):
    dkv_refs = refs[:3]
    dself_ref, cos_ref, sin_ref, out_ref = refs[3:]
    q_width = dq_ref.shape[-1]
    k_width = dself_ref.shape[-1] // 2
    out_ref[:, :q_width] = dq_ref[...]
    parts = [sum(ref[g, 0].astype(f32) for ref in dkv_refs) for g in range(NPROMPT)]
    dkv = jnp.concatenate(parts + [dself_ref[0]], axis=0)
    cosine, sine = cos_ref[...], -sin_ref[...]
    for lo in range(0, 2 * k_width, 128):
        piece = dkv[:, lo : lo + 128]
        if lo < k_width:
            piece = turn(piece, cosine, sine)
        out_ref[:, q_width + lo : q_width + lo + 128] = piece.astype(bf16)


def projected_grad(dq, dkv_parts, dself, cosine, sine):
    rows2, q_width = dq.shape
    rows = rows2 // 2
    kv_width = dself.shape[-1]
    dkv_parts = [p.reshape(NPROMPT, 2, PROMPT_DEV, kv_width) for p in dkv_parts]
    turn_spec = pl.BlockSpec((rows, 128), lambda h: (h, 0))
    return pl.pallas_call(
        projected_grad_kernel,
        grid=(2,),
        in_specs=[pl.BlockSpec((rows, q_width), lambda h: (h, 0))]
        + [pl.BlockSpec((NPROMPT, 1, PROMPT_DEV, kv_width), lambda h: (0, h, 0, 0))] * 3
        + [pl.BlockSpec((1, CLEN, kv_width), lambda h: (h, 0, 0)), turn_spec, turn_spec],
        out_specs=pl.BlockSpec((rows, q_width + kv_width), lambda h: (h, 0)),
        out_shape=jax.ShapeDtypeStruct((rows2, q_width + kv_width), bf16),
        compiler_params=pltpu.CompilerParams(vmem_limit_bytes=SMALL_LIMIT),
        cost_estimate=pl.CostEstimate(
            flops=20 * rows2 * kv_width, bytes_accessed=6 << 20, transcendentals=0
        ),
        name="projected_grad",
    )(dq, *dkv_parts, dself, cosine, sine)


def order_kernel(meta_ref, qkv_ref, out_ref, parts_ref):
    top = qkv_ref.shape[1]
    shards = qkv_ref.shape[0]
    rows = top + out_ref.shape[1]
    for s in range(shards):
        parts_ref[0, s * rows : s * rows + top, :] = qkv_ref[s]
        parts_ref[0, s * rows + top : (s + 1) * rows, :] = out_ref[s]


def order_parts(meta, qkv, out, chips, dp_size):
    width = qkv.shape[1]
    qkv = qkv.reshape(dp_size, -1, width)
    out = out.reshape(dp_size, -1, width)
    rows = [a.shape[1] // chips for a in (qkv, out)]
    return pl.pallas_call(
        order_kernel,
        grid_spec=pltpu.PrefetchScalarGridSpec(
            num_scalar_prefetch=1,
            grid=(chips,),
            in_specs=[
                pl.BlockSpec((dp_size, r, width), lambda k, meta: (0, meta[META + k], 0))
                for r in rows
            ],
            out_specs=pl.BlockSpec((1, dp_size * sum(rows), width), lambda k, meta: (k, 0, 0)),
        ),
        out_shape=jax.ShapeDtypeStruct((chips, dp_size * sum(rows), width), bf16),
        compiler_params=pltpu.CompilerParams(vmem_limit_bytes=SMALL_LIMIT),
        cost_estimate=pl.CostEstimate(
            flops=qkv.size, bytes_accessed=6 * qkv.size, transcendentals=0
        ),
        name="order_parts",
    )(meta, qkv, out)


def step_kernel(dp_size, grad_scale, meta_ref, grad_ref, *refs):
    qkv, out, step_ref = refs[:3], refs[3:6], refs[6]
    top = qkv[0].shape[0]
    grad = grad_ref[...].astype(f32)
    args = [core_heads(ref[...], meta_ref[4], dp_size) for ref in qkv]
    step_ref[:top, :] = adamw(*args, grad[:top], grad_scale, decay_rate)[0].astype(bf16)
    args = [ref[...] for ref in out]
    step_ref[top:, :] = adamw(*args, grad[top:], grad_scale, decay_rate)[0].astype(bf16)


def shard_step(meta, grad, qkv, out, chips, dp_size, grad_scale):
    qkv_rows, out_rows = qkv[0].shape[0] // chips, out[0].shape[0] // (2 * chips)
    width = grad.shape[1]
    return pl.pallas_call(
        functools.partial(step_kernel, dp_size, grad_scale),
        grid_spec=pltpu.PrefetchScalarGridSpec(
            num_scalar_prefetch=1,
            grid=(1,),
            in_specs=[whole_spec(grad)]
            + [pl.BlockSpec((qkv_rows, 2 * width), lambda t, meta: (meta[6], 0))] * 3
            + [pl.BlockSpec((out_rows, width), lambda t, meta: (meta[4] * chips + meta[6], 0))] * 3,
            out_specs=whole_spec(grad),
        ),
        out_shape=jax.ShapeDtypeStruct(grad.shape, bf16),
        compiler_params=pltpu.CompilerParams(vmem_limit_bytes=WHOLE_LIMIT),
        cost_estimate=pl.CostEstimate(
            flops=20 * grad.size, bytes_accessed=16 * grad.size, transcendentals=grad.size
        ),
        name="shard_step",
    )(meta, grad, *qkv, *out)


def optimizer_kernel(blocks, dp_size, grad_scale, spill, meta_ref, *refs):
    mine, refs = refs[:blocks], refs[blocks:]
    other, refs = refs[:blocks], refs[blocks:]
    qkv, out = refs[:3], refs[3:6]
    refs = refs[6 + spill :]
    step_qkv, mean_qkv, square_qkv, step_out, mean_out, square_out = refs
    core = meta_ref[4]
    top, out_rows = qkv[0].shape[0], out[0].shape[1]

    def run(mine_ref, other_ref):
        for shift in range(dp_size):
            rows = slice(shift * (top + out_rows), (shift + 1) * (top + out_rows))
            a, b = mine_ref[rows, :], other_ref[rows, :]
            whole = all_heads(a[:top], b[:top], core, dp_size).astype(f32)
            low = jnp.concatenate(
                [
                    jnp.where(core == 0, a[top:], b[top:])[None],
                    jnp.where(core == 0, b[top:], a[top:])[None],
                ],
                axis=0,
            ).astype(f32)
            if shift == 0:
                whole, mean, square = adamw(*[r[...] for r in qkv], whole, grad_scale, decay_rate)
                whole = whole.astype(bf16).astype(f32)
                mean_qkv[...] = mean
                square_qkv[...] = square
                low, mean, square = adamw(*[r[...] for r in out], low, grad_scale, decay_rate)
                low = low.astype(bf16).astype(f32)
                mean_out[...] = mean
                square_out[...] = square
            at = (meta_ref[5] + shift) % dp_size
            step_qkv[pl.ds(at, 1)] = whole[None]
            step_out[pl.ds(at, 1)] = low[None]

    for k in range(blocks):
        if blocks == 1:
            run(mine[k], other[k])
        else:
            pl.when(pl.program_id(0) == k)(functools.partial(run, mine[k], other[k]))


def optimize(meta, first_block, mine, other, qkv, out, buffers, chips, dp_size, grad_scale):
    blocks = len(mine)
    spill = 0 if buffers is None else 6
    qkv_rows = qkv[0].shape[0] // chips
    out_rows = out[0].shape[0] // (2 * chips)
    width = out[0].shape[1]
    out = [a.reshape(2, a.shape[0] // 2, width) for a in out]

    def at_chip(block, meta):
        return meta[META + first_block + block]

    own_qkv = pl.BlockSpec((qkv_rows, 2 * width), lambda b, meta: (at_chip(b, meta), 0))
    own_out = pl.BlockSpec((2, out_rows, width), lambda b, meta: (0, at_chip(b, meta), 0))
    step_qkv = pl.BlockSpec(
        (dp_size, qkv_rows, 2 * width), lambda b, meta: (0, at_chip(b, meta), 0)
    )
    step_out = pl.BlockSpec(
        (dp_size, 2, out_rows, width), lambda b, meta: (0, 0, at_chip(b, meta), 0)
    )
    shapes = [
        (dp_size,) + qkv[0].shape,
        qkv[0].shape,
        qkv[0].shape,
        (dp_size,) + out[0].shape,
        out[0].shape,
        out[0].shape,
    ]
    specs = [step_qkv, own_qkv, own_qkv, step_out, own_out, own_out]
    first = 1 + 2 * blocks + 6
    return pl.pallas_call(
        functools.partial(optimizer_kernel, blocks, dp_size, grad_scale, spill),
        grid_spec=pltpu.PrefetchScalarGridSpec(
            num_scalar_prefetch=1,
            grid=(blocks,),
            in_specs=[whole_spec(a) for a in (*mine, *other)]
            + [own_qkv] * 3
            + [own_out] * 3
            + [pl.BlockSpec(memory_space=pl.ANY)] * spill,
            out_specs=specs,
        ),
        out_shape=[jax.ShapeDtypeStruct(shape, f32) for shape in shapes],
        input_output_aliases={first + k: k for k in range(spill)},
        compiler_params=pltpu.CompilerParams(vmem_limit_bytes=WHOLE_LIMIT),
        cost_estimate=pl.CostEstimate(
            flops=blocks * qkv_rows * width * 60,
            bytes_accessed=blocks * qkv_rows * width * 90,
            transcendentals=blocks * qkv_rows * width * 3,
        ),
        name="optimize",
    )(meta, *mine, *other, *qkv, *out, *(buffers or ()))


def expert_kernel(count, tok, spill, meta_ref, *refs):
    x_refs, refs = refs[:count], refs[count:]
    cot_refs, refs = refs[:count], refs[count:]
    gate_ups, downs = refs[:2], refs[2:4]
    refs = refs[4 + spill :]
    mix_refs, refs = refs[:count], refs[count:]
    grad_refs, refs = refs[:count], refs[count:]
    x_all, cot_all, act_all, dgu_all = refs
    width = x_all.shape[-1]

    def run(x_ref, cot_ref, mix_ref, grad_ref):
        x = x_ref[:tok, :]
        cot = cot_ref[...]
        x_all[...] = x
        cot_all[...] = cot
        extra = x_ref[tok:, :].astype(f32)
        extra = extra[:, :tok] + extra[:, tok : 2 * tok]
        row = lax.broadcasted_iota(jnp.int32, extra.shape, 0)
        gates = jnp.zeros_like(extra)
        for e in range(2):
            mine = row == meta_ref[2 + e]
            weight = jnp.sum(jnp.where(mine, extra, 0.0), axis=0, keepdims=True)
            weight = jnp.transpose(jnp.broadcast_to(weight, (128, tok)))
            weight = jnp.concatenate([weight, weight], axis=1)
            gate_grad = jnp.zeros((tok, 1), f32)
            for lo in range(0, EXP_FF, 256):
                hi = lo + 256
                gate = dot(x, gate_ups[e][:, lo:hi])
                up = dot(x, gate_ups[e][:, EXP_FF + lo : EXP_FF + hi])
                dact = dot_nt(cot, downs[e][lo:hi, :])
                sig = 0.5 * jnp.tanh(0.5 * gate) + 0.5
                silu = gate * sig
                act = silu * up
                gate_grad = gate_grad + jnp.sum(act * dact, axis=-1, keepdims=True)
                act_all[:, e * EXP_FF + lo : e * EXP_FF + hi] = (act * weight).astype(bf16)
                dact = dact * weight
                dgate = dact * up * (sig + silu * (1.0 - sig))
                at = 2 * e * EXP_FF
                dgu_all[:, at + lo : at + hi] = dgate.astype(bf16)
                dgu_all[:, at + EXP_FF + lo : at + EXP_FF + hi] = (dact * silu).astype(bf16)
            gate_row = jnp.transpose(jnp.broadcast_to(gate_grad, (tok, 128)))[:1, :]
            gates = jnp.where(mine, gate_row, gates)
        acts = [act_all[:, e * EXP_FF : (e + 1) * EXP_FF] for e in range(2)]
        dgus = [dgu_all[:, 2 * e * EXP_FF : 2 * (e + 1) * EXP_FF] for e in range(2)]
        for lo in range(0, width, 256):
            mix = sum(dot(acts[e], downs[e][:, lo : lo + 256]) for e in range(2))
            mix_ref[:, lo : lo + 256] = mix.astype(bf16)
        for lo in range(0, width, 256):
            grad = sum(dot_nt(dgus[e], gate_ups[e][lo : lo + 256, :]) for e in range(2))
            grad_ref[:tok, lo : lo + 256] = grad.astype(bf16)
        high = gates.astype(bf16)
        grad_ref[tok:, :tok] = high
        grad_ref[tok:, tok : 2 * tok] = (gates - high.astype(f32)).astype(bf16)
        grad_ref[tok:, 2 * tok :] = jnp.zeros((extra.shape[0], width - 2 * tok), bf16)

    for b in range(count):
        body = functools.partial(run, x_refs[b], cot_refs[b], mix_refs[b], grad_refs[b])
        if count == 1:
            body()
        else:
            pl.when(pl.program_id(0) == b)(body)


def run_experts(meta, x_blocks, cot_blocks, weights, buffers, place, total):
    count = len(x_blocks)
    packed, width = x_blocks[0].shape
    tok = cot_blocks[0].shape[0]
    rows = count * tok
    spill = 0 if buffers is None else 4
    any_spec = pl.BlockSpec(memory_space=pl.ANY)
    stream_width = [width, width, 2 * EXP_FF, 4 * EXP_FF]
    stream = [pl.BlockSpec((tok, w), lambda g, ids: (place + g, 0)) for w in stream_width]
    out = pl.pallas_call(
        functools.partial(expert_kernel, count, tok, spill),
        grid_spec=pltpu.PrefetchScalarGridSpec(
            num_scalar_prefetch=1,
            grid=(count,),
            in_specs=[
                whole_spec(a) for a in (*x_blocks, *cot_blocks, *weights)
            ]
            + [any_spec] * spill,
            out_specs=[whole_spec(c) for c in cot_blocks]
            + [whole_spec(x) for x in x_blocks]
            + stream,
        ),
        out_shape=[jax.ShapeDtypeStruct(c.shape, bf16) for c in cot_blocks]
        + [jax.ShapeDtypeStruct(x.shape, bf16) for x in x_blocks]
        + [jax.ShapeDtypeStruct((total, w), bf16) for w in stream_width],
        input_output_aliases={1 + 2 * count + 4 + k: 2 * count + k for k in range(spill)},
        compiler_params=pltpu.CompilerParams(vmem_limit_bytes=VMEM_LIMIT),
        cost_estimate=pl.CostEstimate(
            flops=2 * 2 * rows * width * EXP_FF * 6,
            bytes_accessed=rows * width * 20 + 6 * width * width,
            transcendentals=2 * rows * EXP_FF,
        ),
        name="experts",
    )(meta, *x_blocks, *cot_blocks, *weights, *(buffers or ()))
    return out[:count], out[count : 2 * count], out[2 * count :]


def per_device(
    ring,
    tokens,
    cotangent,
    routes,
    cont_group,
    attn_gain,
    qkv_weight,
    out_weight,
    ffn_gain,
    router_weight,
    gate_up_weight,
    down_weight,
    mean_attn_gain,
    mean_qkv_weight,
    mean_out_weight,
    mean_ffn_gain,
    mean_router_weight,
    mean_gate_up_weight,
    mean_down_weight,
    square_attn_gain,
    square_qkv_weight,
    square_out_weight,
    square_ffn_gain,
    square_router_weight,
    square_gate_up_weight,
    square_down_weight,
):
    chips = ring.chips
    dp_size = lax.axis_size("dp")
    dp = lax.axis_index("dp")
    chip = lax.axis_index("chip")
    core = lax.axis_index("core")
    members = 2 * chips
    tok_count, width = tokens.shape
    experts = router_weight.shape[1]
    capacity = 5 * tok_count * TOPK // (4 * experts)
    prompt_len = PROMPT_DEV * members
    core_heads = HEADS // 2
    core_kv = KV_HEADS // 2
    q_width = core_heads * HEAD_DIM
    k_width = core_kv * HEAD_DIM

    member_pair = jnp.stack([2 * chip + core, 2 * chip + 1 - core])
    groups = jnp.concatenate([cont_group, swap(cont_group)])
    own_place = jnp.stack([core, dp, chip, 0])
    meta = jnp.concatenate([groups, member_pair, own_place, ring.chips_from(chip)])

    tokens = split_rows(tokens)
    cotangent = split_rows(cotangent)
    routes = split_rows(routes)
    tok_float = tokens.astype(f32)

    qkv_core = cast_core_columns(core, qkv_weight, dp_size)
    small = jnp.concatenate([attn_gain[None], ffn_gain[None], router_weight.T], axis=0).astype(bf16)
    small = gather_dp(small, 1)
    qkv_shards = dp_shards(qkv_core)
    gain_attn = small[0].astype(f32)
    gain_ffn = small[1].astype(f32)
    proj_router_t = small[2:]

    scale_attn = lax.rsqrt(jnp.mean(tok_float * tok_float, axis=-1, keepdims=True) + norm_eps)
    attn_in = (tok_float * scale_attn * gain_attn).astype(bf16)
    cot_ring = RingGather(ring, cotangent)
    cot_ring.step()
    attn_in = after(attn_in, cot_ring.ends())
    cot_ring.step()
    attn_other = swap(attn_in)
    qkv_shards = after(qkv_shards, cot_ring.ends())
    while cot_ring.place < ring.half - 1:
        cot_ring.step()
    within = jnp.arange(PROMPT_DEV, dtype=jnp.int32)
    prompt_pos = member_pair[:, None] * PROMPT_DEV + within
    cont_pos = jnp.broadcast_to(prompt_len + within, (2, CLEN))
    position = jnp.stack([prompt_pos, prompt_pos, cont_pos], axis=1).reshape(-1)
    half_dim = HEAD_DIM // 2
    frequency = jnp.exp(
        jnp.arange(half_dim, dtype=f32) * (-2.0 * math.log(10000.0) / HEAD_DIM)
    )
    angles = position.astype(f32)[:, None] * frequency[None, :]
    cosine_part, sine_part = jnp.cos(angles), jnp.sin(angles)
    cosine = jnp.concatenate([cosine_part] * 4, axis=1)
    sine_signed = jnp.concatenate([-sine_part, sine_part] * 2, axis=1)
    rows2 = 2 * tok_count
    queries, prompt_kv, cont_kv = project(
        meta, attn_in, attn_other, qkv_shards, cosine, sine_signed
    )
    prompt_kv = prompt_kv.reshape(2 * PROMPT_ROWS, 2 * k_width)
    prompt_kv = after(prompt_kv, cot_ring.ends())
    half_rows = out_weight.shape[0] // 2
    late_gate_up, late_down, late_out = after(
        (gate_up_weight[0], down_weight[0], out_weight), prompt_kv
    )
    out_core = pick_core(late_out[:half_rows], late_out[half_rows:]).astype(bf16)
    own_gate_up = lax.all_gather(late_gate_up.astype(bf16), "dp", axis=0, tiled=True)
    own_down = lax.all_gather(late_down.astype(bf16), "dp", axis=0, tiled=True)
    expert_weights = [own_gate_up, swap(own_gate_up), own_down, swap(own_down)]
    attn_in2 = jnp.concatenate([attn_in, attn_other], axis=0)
    proj_qkv = join_dp(after(qkv_shards, prompt_kv), 0)
    proj_out = gather_dp(after(out_core, prompt_kv), 0)
    kv_blocks, state = {}, None
    for arrived in ring.gather_steps(prompt_kv):
        kv_blocks.update(arrived)
        if 2 in arrived:
            state, proj_qkv = after((state, proj_qkv))
            small_state = [
                jnp.concatenate([a[None], f[None], r.T], axis=0)
                for a, f, r in (
                    (attn_gain, ffn_gain, router_weight),
                    (mean_attn_gain, mean_ffn_gain, mean_router_weight),
                    (square_attn_gain, square_ffn_gain, square_router_weight),
                )
            ]
            small_state = gather_dp(after(jnp.stack(small_state), state), 2)
        if ring.half in arrived:
            state, small_state = after((state, small_state))
        state = attend(
            meta,
            queries,
            ring.by_distance.index(min(arrived)),
            list(arrived.values()),
            state,
            cont_kv if 0 in arrived else None,
            ring.half in arrived,
        )
    mixed, mixed_low, lse = state
    cot_blocks = cot_ring.blocks

    part = dot(mixed_low, proj_out)
    other = swap(part[tok_count:].astype(bf16))
    hidden = tok_float + part[:tok_count] + other.astype(f32)
    scale_ffn = lax.rsqrt(jnp.mean(hidden * hidden, axis=-1, keepdims=True) + norm_eps)
    ffn_in = (hidden * scale_ffn * gain_ffn).astype(bf16)
    logits = dot_nt(proj_router_t, ffn_in)
    expert_ids = jnp.arange(experts, dtype=jnp.int32)
    hot = jnp.any(routes.T[None] == expert_ids[:, None, None], axis=1)
    hot_float = hot.astype(f32)
    shown = jnp.where(hot, logits, masked_score)
    raised = jnp.where(hot, jnp.exp(shown - jnp.max(shown, axis=0, keepdims=True)), 0.0)
    gate_probs = raised / jnp.sum(raised, axis=0, keepdims=True)
    spot = jnp.arange(tok_count, dtype=jnp.int32)
    spot = jnp.where(
        spot < PROMPT_ROWS, (spot % PROMPT_DEV) * NPROMPT + spot // PROMPT_DEV, spot
    )
    earlier = (spot[:, None] < spot[None, :]).astype(bf16)
    placed = dot(hot.astype(bf16), earlier)
    kept = hot & (placed < capacity)
    pair_weight = jnp.where(kept, gate_probs, 0.0)
    weight_high = lax.reduce_precision(pair_weight, 8, 7)
    weight_rows = jnp.concatenate([weight_high, pair_weight - weight_high], axis=1).astype(bf16)
    weight_rows = jnp.pad(weight_rows, ((0, 0), (0, width - 2 * tok_count)))
    packed = jnp.concatenate([ffn_in, weight_rows], axis=0)

    total_rows = chips * tok_count
    mix_parts, grad_parts = {}, {}
    buffers = None
    packed = after(packed, cot_ring.ends())
    ffn_ring = RingGather(ring, packed)
    arrived, place = {0: packed}, 0
    while arrived:
        later = {}
        if ffn_ring.place < ring.half:
            later = ffn_ring.step(*(buffers or ()))
        if ring.half in later:
            cot_ring.step(ffn_ring.before)
        mixes, grads, buffers = run_experts(
            meta,
            list(arrived.values()),
            [cot_blocks[r] for r in arrived],
            expert_weights,
            buffers,
            place,
            total_rows,
        )
        mix_parts.update(zip(arrived, mixes))
        grad_parts.update(zip(arrived, grads))
        place += len(arrived)
        arrived = later

    grad_sum = RingSum(ring, grad_parts[ring.half])
    grad_sum.add(grad_parts)
    x_all, cot_all, act_all, dgu_all = after(buffers, grad_sum.sent)
    other_gate_up = dot_tn(x_all, dgu_all[:, 2 * EXP_FF :]).astype(bf16)
    other_down = dot_tn(act_all[:, EXP_FF:], cot_all).astype(bf16)
    grad_sum.add(grad_parts, other_gate_up, other_down)
    other_gate_up, other_down = after((other_gate_up, other_down), grad_sum.sent)
    other_gate_up, other_down = swap(other_gate_up), swap(other_down)
    while grad_sum.place > 1:
        grad_sum.add(grad_parts, other_gate_up, other_down)
    x_all, cot_all, act_all, dgu_all = after(buffers, grad_sum.sent)
    grad_gate_up = dot_tn(x_all, dgu_all[:, : 2 * EXP_FF]) + other_gate_up.astype(f32)
    grad_gate_up = grad_gate_up.astype(bf16)
    grad_down = dot_tn(act_all[:, :EXP_FF], cot_all) + other_down.astype(f32)
    grad_down = grad_down.astype(bf16)
    grad_packed, grad_gate_up, grad_down = lax.optimization_barrier(
        (grad_sum.finish(grad_parts[0]), grad_gate_up, grad_down)
    )
    mix_sum = RingSum(ring, after(mix_parts[ring.half], grad_sum.arrived()))

    def shards_dp(whole):
        pieces = whole.reshape((dp_size, whole.shape[0] // dp_size) + whole.shape[1:])
        out = [lax.dynamic_index_in_dim(pieces, dp, 0, False)]
        for shift in range(1, dp_size):
            perm = [(k, (k + shift) % dp_size) for k in range(dp_size)]
            part = lax.dynamic_index_in_dim(pieces, (dp + shift) % dp_size, 0, False)
            out.append(lax.ppermute(part, "dp", perm))
        return out

    def sum_of(pieces, *others):
        return sum(piece.astype(f32) for piece in after(pieces, others))


    grad_gate = grad_packed[tok_count:, :tok_count] + grad_packed[tok_count:, tok_count : 2 * tok_count]
    grad_gate = jnp.where(kept, grad_gate, 0.0)
    grad_chosen = gate_probs * (grad_gate - jnp.sum(gate_probs * grad_gate, axis=0, keepdims=True))
    grad_logits = (hot_float * grad_chosen).astype(bf16)
    grad_router_t = dot(grad_logits, ffn_in)
    grad_ffn = grad_packed[:tok_count] + dot_tn(grad_logits, proj_router_t)
    grad_output = cotangent.astype(f32)
    grad_hidden_norm, grad_gain_ffn = norm_back(hidden, scale_ffn, gain_ffn, grad_ffn)
    grad_hidden = grad_output + grad_hidden_norm
    grad_attn = after(grad_hidden.astype(bf16), mix_sum.arrived())
    grad_attn2 = jnp.concatenate([grad_attn, swap(grad_attn)], axis=0)
    grad_mixed = dot_nt(grad_attn2, proj_out).astype(bf16)
    mix_sum.add(mix_parts, grad_mixed)

    grad_scale = (tok_count * dp_size * members) ** (-0.5)

    dq, dkv, dkv_sum = None, (), None
    for turn_no, places in enumerate(ring.groups()[::-1]):
        if turn_no >= 2:
            grad_mixed = after(grad_mixed, dkv_before)
        if 0 in places or (turn_no % 2 == 0 and mix_sum.place > 3):
            grad_mixed = after(grad_mixed, mix_sum.arrived())
            mix_sum.add(mix_parts, dkv)
        dkv = attend_back(
            meta,
            queries,
            grad_mixed,
            mixed,
            lse,
            ring.by_distance.index(min(places)),
            [kv_blocks[r] for r in places],
            dq,
            (cont_kv, cosine, sine_signed) if 0 in places else None,
        )
        parts = dict(zip(places, dkv))
        if ring.half in places:
            dkv_sum = RingSum(ring, parts[ring.half])
        elif 0 not in places:
            grad_out_weight = dot_tn(after(mixed_low, dkv), grad_attn2)
            if turn_no == 1:
                late_gate_up, late_down = after((grad_gate_up, grad_down), dkv)
                gate_up_shards, down_shards = shards_dp(late_gate_up), shards_dp(late_down)
            dkv_before = dkv_sum.arrived()
            dkv_sum.add(parts)
        if 0 not in places:
            dq = dkv[len(places)]
    grad_projected = projected_grad(
        dkv[1], (parts[0], *dkv_sum.arrived()), dkv[2], cosine, sine_signed
    )
    grad_qkv_weight = dot_tn(attn_in2, grad_projected)
    part = dot_nt(grad_projected, proj_qkv)
    other_part = swap(part[tok_count:].astype(bf16))

    qkv_rows = width // dp_size // chips
    out_rows = HEADS * HEAD_DIM // dp_size // 2 // chips
    dense_parts = order_parts(
        meta, grad_qkv_weight.astype(bf16), grad_out_weight.astype(bf16), chips, dp_size
    )
    parts = {r: dense_parts[k] for k, r in enumerate(ring.by_distance)}
    dense_sum = RingSum(ring, parts[ring.half])
    dense_sum.add(parts, mix_sum.arrived())
    gate_up_new = adamw(
        gate_up_weight,
        mean_gate_up_weight,
        square_gate_up_weight,
        sum_of(gate_up_shards, dense_sum.sent)[None],
        grad_scale,
        decay_rate,
    )
    dense_sum.add(parts, gate_up_new, other_part)
    grad_attn_in = part[:tok_count] + after(other_part, dense_sum.sent).astype(f32)
    grad_tok_norm, grad_gain_attn = norm_back(tok_float, scale_attn, gain_attn, grad_attn_in)
    input_grad = grad_hidden + grad_tok_norm
    small_grad = jnp.concatenate(
        [grad_gain_attn[None], grad_gain_ffn[None], grad_router_t], axis=0
    )
    down_new = adamw(
        down_weight,
        mean_down_weight,
        square_down_weight,
        sum_of(down_shards, dense_sum.sent)[None],
        grad_scale,
        decay_rate,
    )
    dense_sum.add(parts, down_new, small_grad)
    while dense_sum.place > 1:
        dense_sum.add(parts)
    for small_grad in total_stages(small_grad, ("core", "dp")):
        pass
    dense = after(dense_sum.finish(parts[0]), small_grad)
    dense = dense.reshape(dp_size, qkv_rows + out_rows, width)
    mix_sum.add(mix_parts, dense)
    shard = lax.dynamic_index_in_dim(dense, dp, 0, False)
    for shift in range(1, dp_size):
        perm = [(k, (k + shift) % dp_size) for k in range(dp_size)]
        sent = lax.dynamic_index_in_dim(dense, (dp + shift) % dp_size, 0, False)
        shard = shard + lax.ppermute(sent.astype(bf16), "dp", perm).astype(f32)
    shard_low = shard.astype(bf16)

    qkv_state = (qkv_weight, mean_qkv_weight, square_qkv_weight)
    out_state = (out_weight, mean_out_weight, square_out_weight)
    step_shard = shard_step(
        meta, shard_low, qkv_state, out_state, chips, dp_size, grad_scale
    )
    small_rows = -(-small_grad.shape[0] // 16) * 16
    small_low = jnp.pad(small_grad.astype(bf16), ((0, small_rows - small_grad.shape[0]), (0, 0)))
    carried = jnp.concatenate([shard_low, *dp_shards(step_shard)[1:], small_low], axis=0)
    input_grad = merge_rows(input_grad)
    carried = after(carried, mix_sum.arrived(), input_grad)
    while mix_sum.place > 1:
        mix_sum.add(mix_parts, step_shard)
    output = hidden + mix_sum.finish(mix_parts[0])
    dense_new = None
    dense_ring = RingGather(ring, carried)
    arrived, first_place, earlier = dict(dense_ring.blocks), 0, [(), ()]
    while arrived:
        later = {}
        if dense_ring.place < ring.half:
            later = dense_ring.step(*earlier.pop(0))
        earlier.append(tuple(dense_new or ()))
        dense_new = optimize(
            meta,
            first_place,
            list(arrived.values()),
            [swap(m) for m in arrived.values()],
            qkv_state,
            out_state,
            dense_new,
            chips,
            dp_size,
            grad_scale,
        )
        first_place += len(arrived)
        if ring.half - 2 in arrived:
            dense_most = dense_new
        arrived = later
    dense_new = [a.reshape(-1, a.shape[-1]) for a in dense_new]

    base = dp_size * (qkv_rows + out_rows)
    count = small_grad.shape[0]
    small_total = sum(
        dense_ring.blocks[r][base : base + count].astype(f32) for r in ring.by_distance
    )
    decays = jnp.full((count, 1), decay_rate, f32).at[:2].set(0.0)
    small_new = adamw(*small_state, small_total, grad_scale, decays)
    shard_cols = width // dp_size
    small_step = small_new[0]
    small_mean, small_square = [
        lax.dynamic_slice_in_dim(a, dp * shard_cols, shard_cols, 1) for a in small_new[1:]
    ]

    step_gate_up = lax.all_gather(gate_up_new[0].astype(bf16), "dp", axis=1, tiled=True)
    step_down = lax.all_gather(down_new[0].astype(bf16), "dp", axis=1, tiled=True)
    step_gate_up, step_down = after((step_gate_up, step_down), dense_most)
    return (
        merge_rows(output.astype(bf16)),
        input_grad,
        small_step[0],
        dense_new[0],
        dense_new[3],
        small_step[1],
        small_step[2:].T,
        step_gate_up.astype(f32),
        step_down.astype(f32),
        small_mean[0],
        dense_new[1],
        dense_new[4],
        small_mean[1],
        small_mean[2:].T,
        gate_up_new[1],
        down_new[1],
        small_square[0],
        dense_new[2],
        dense_new[5],
        small_square[1],
        small_square[2:].T,
        gate_up_new[2],
        down_new[2],
    )


def solution(mesh):
    dp_size, members = mesh.shape["dp"], mesh.shape["expert"]
    chips = members // 2
    fine = Mesh(mesh.devices.reshape(dp_size, chips, 2), ("dp", "chip", "core"))
    ring = Ring(chips)
    member = ("chip", "core")
    token = P(("dp",) + member, None)
    matrices = (P("dp"), P("dp", None), P("dp", None), P("dp"), P("dp", None))
    expert = (P(member, "dp", None), P(member, "dp", None))

    def body(*arrays):
        return per_device(ring, *arrays)

    return jax.shard_map(
        body,
        mesh=fine,
        in_specs=(token, token, token, P(("dp",) + member)) + (matrices + expert) * 3,
        out_specs=(token, token)
        + (P(),) * 5
        + (P(member, None, None),) * 2
        + (matrices + expert) * 2,
        check_vma=False,
    )
```

```python
import functools
import math

import jax
import jax.numpy as jnp
from jax import lax
from jax.experimental import pallas as pl
from jax.experimental.pallas import tpu as pltpu
from jax.sharding import Mesh
from jax.sharding import PartitionSpec as P

HEADS = 16
KV_HEADS = 8
HEAD_DIM = 64
EXP_FF = 512
TOPK = 8
NPROMPT = 2
PROMPT_DEV = 128
CLEN = 128
REPEAT = HEADS // KV_HEADS
PROMPT_ROWS = NPROMPT * PROMPT_DEV

norm_eps = 1e-05
masked_score = -1e30
decay_rate = 0.1
adam_eps = 1e-08
bias_first = 0.999973438601112
bias_second = 0.99407947078
score_scale = HEAD_DIM ** (-0.5)

bf16 = jnp.bfloat16
f32 = jnp.float32


def dot(left, right):
    return jnp.dot(left, right, preferred_element_type=f32)


def dot_tn(left, right):
    return lax.dot_general(left, right, (((0,), (0,)), ((), ())), preferred_element_type=f32)


def dot_nt(left, right):
    return lax.dot_general(left, right, (((1,), (1,)), ((), ())), preferred_element_type=f32)


def norm_back(values, scale_rows, gain_row, grad_rows):
    normed = values * scale_rows
    grad_normed = grad_rows * gain_row
    grad_values = scale_rows * (
        grad_normed - normed * jnp.mean(grad_normed * normed, axis=-1, keepdims=True)
    )
    return (grad_values, jnp.sum(grad_rows * normed, axis=0))


def adamw(weight, mean_in, square_in, gradient, grad_scale, decay_factor):
    scaled = gradient * grad_scale
    mean_out = 0.9 * mean_in + 0.1 * scaled
    square_out = 0.95 * square_in + 0.05 * scaled * scaled
    spread = square_out * (1.0 / bias_second)
    spread = spread * lax.rsqrt(spread) + adam_eps
    update = mean_out * (1.0 / bias_first) / spread
    return (update + decay_factor * weight, mean_out, square_out)


def split_rows(values):
    head = values[:PROMPT_ROWS].reshape(PROMPT_DEV, NPROMPT, -1).transpose(1, 0, 2)
    return jnp.concatenate([head.reshape(PROMPT_ROWS, -1), values[PROMPT_ROWS:]], axis=0)


def merge_rows(values):
    head = values[:PROMPT_ROWS].reshape(NPROMPT, PROMPT_DEV, -1).transpose(1, 0, 2)
    return jnp.concatenate([head.reshape(PROMPT_ROWS, -1), values[PROMPT_ROWS:]], axis=0)


def swap(values):
    return lax.ppermute(values, "core", [(0, 1), (1, 0)])


class Ring:
    def __init__(self, chips):
        rows = 4 if chips % 4 == 0 else chips
        cols = chips // rows
        cycle = [(0, x) for x in range(cols)]
        for z in range(1, rows):
            line = [(z, x) for x in range(1, cols)]
            cycle += line[::-1] if z % 2 == 1 else line
        if cols > 1:
            cycle += [(z, 0) for z in range(rows - 1, 0, -1)]
        else:
            cycle = [(z, 0) for z in range(rows)]
        self.chips = chips
        self.order = [z * cols + x for z, x in cycle]
        self.forward = [
            (self.order[k], self.order[(k + 1) % chips]) for k in range(chips)
        ]
        self.backward = [(b, a) for a, b in self.forward]
        self.half = chips // 2
        self.by_distance = [r for group in self.groups() for r in group]

    def chips_from(self, me):
        table = [[0] * self.chips for _ in range(self.chips)]
        for k in range(self.chips):
            for column, offset in enumerate(self.by_distance):
                table[self.order[k]][column] = self.order[(k + offset) % self.chips]
        return lax.dynamic_index_in_dim(jnp.asarray(table, jnp.int32), me, 0, False)

    def gather_steps(self, block):
        gather = RingGather(self, block)
        yield {0: block}
        for _ in range(self.half):
            yield gather.step()

    @staticmethod
    def cut(block):
        return block.shape[0] // 32 * 16

    def groups(self):
        return [[0]] + [[-s, s] for s in range(1, self.half)] + [[self.half]]


class RingGather:
    def __init__(self, ring, block):
        self.ring = ring
        self.place = 0
        self.ahead = self.behind = block
        self.blocks = {0: block}

    def ends(self):
        return (self.ahead, self.behind)

    def step(self, *others):
        ring = self.ring
        self.place += 1
        if others:
            self.ahead, self.behind = after(self.ends(), others)
        self.before = self.ends()
        if self.place < ring.half:
            self.ahead = lax.ppermute(self.ahead, "chip", ring.forward)
            self.behind = lax.ppermute(self.behind, "chip", ring.backward)
            arrived = {-self.place: self.ahead, self.place: self.behind}
        else:
            cut = ring.cut(self.ahead)
            first = lax.ppermute(self.ahead[:cut], "chip", ring.forward)
            second = lax.ppermute(self.behind[cut:], "chip", ring.backward)
            arrived = {ring.half: jnp.concatenate([first, second], axis=0)}
        self.blocks.update(arrived)
        return arrived


class RingSum:
    def __init__(self, ring, part):
        cut = ring.cut(part)
        self.ring = ring
        self.place = ring.half
        self.cut = cut
        self.sent = (part[:cut], part[cut:])
        self.send()

    def send(self):
        self.ahead = lax.ppermute(self.sent[0], "chip", self.ring.forward)
        self.behind = lax.ppermute(self.sent[1], "chip", self.ring.backward)

    def arrived(self):
        return (self.ahead, self.behind)

    def add(self, parts, *others):
        ring, cut = self.ring, self.cut
        self.place -= 1
        up, down = parts[self.place], parts[-self.place]
        if others:
            up, down = after((up, down), others)
        self.ahead, self.behind = lax.optimization_barrier((self.ahead, self.behind))
        if self.place == ring.half - 1:
            ahead = jnp.concatenate([self.ahead + up[:cut], up[cut:]], axis=0)
            behind = jnp.concatenate([down[:cut], self.behind + down[cut:]], axis=0)
        else:
            ahead, behind = self.ahead + up, self.behind + down
        self.sent = (ahead, behind)
        self.send()

    def finish(self, part):
        return part.astype(f32) + self.ahead.astype(f32) + self.behind.astype(f32)


def after(values, *others):
    return lax.optimization_barrier((values, others))[0]


def total_stages(values, axes):
    for axis in axes:
        size = lax.axis_size(axis)
        reach = 1
        while reach < size:
            values = values + lax.ppermute(values, axis, [(k, k ^ reach) for k in range(size)])
            reach *= 2
            yield values


def dp_shards(values):
    size = lax.axis_size("dp")
    pieces = [values]
    for shift in range(1, size):
        perm = [(k, (k - shift) % size) for k in range(size)]
        pieces.append(lax.ppermute(values, "dp", perm))
    return pieces


def join_dp(pieces, axis):
    size = len(pieces)
    dp = lax.axis_index("dp")
    if size == 2:
        return jnp.concatenate(
            [
                jnp.where(dp == 0, pieces[0], pieces[1]),
                jnp.where(dp == 0, pieces[1], pieces[0]),
            ],
            axis=axis,
        )
    twice = jnp.concatenate(pieces + pieces, axis=axis)
    shard = pieces[0].shape[axis]
    return lax.dynamic_slice_in_dim(twice, (size - dp) % size * shard, size * shard, axis)


def gather_dp(values, axis):
    return join_dp(dp_shards(values), axis)


def pick_core(first, second):
    return jnp.where(lax.axis_index("core") == 0, first, second)


LOG2E = 1.4426950408889634


def stack_heads(wide):
    wide = wide.astype(f32)
    first, second = wide[:, :128], wide[:, 128:]
    lane = lax.broadcasted_iota(jnp.int32, first.shape, 1)
    low_lanes = lane < HEAD_DIM
    zero = jnp.zeros_like(first)
    return jnp.concatenate(
        [
            jnp.where(low_lanes, first, zero),
            jnp.where(low_lanes, pltpu.roll(first, HEAD_DIM, 1), zero),
            jnp.where(low_lanes, zero, pltpu.roll(second, HEAD_DIM, 1)),
            jnp.where(low_lanes, zero, second),
        ],
        axis=0,
    )


def unstack_heads(tall):
    rows = tall.shape[0] // 4
    parts = [tall[k * rows : (k + 1) * rows] for k in range(4)]
    lane = lax.broadcasted_iota(jnp.int32, parts[0].shape, 1)
    low_lanes = lane < HEAD_DIM
    return jnp.concatenate(
        [
            jnp.where(low_lanes, parts[0], pltpu.roll(parts[1], HEAD_DIM, 1)),
            jnp.where(low_lanes, pltpu.roll(parts[2], HEAD_DIM, 1), parts[3]),
        ],
        axis=1,
    )


def row_of(column_sum_of):
    return jnp.sum(jnp.transpose(column_sum_of), axis=0, keepdims=True)


def tile_masks(meta_ref, half, is_cont):
    shape = (PROMPT_ROWS, 4 * PROMPT_DEV)
    key = lax.broadcasted_iota(jnp.int32, shape, 0)
    query = lax.broadcasted_iota(jnp.int32, shape, 1) % PROMPT_DEV
    key_member = jnp.where(key < PROMPT_DEV, meta_ref[2], meta_ref[3])
    key_pos = key_member * PROMPT_DEV + key % PROMPT_DEV
    query_pos = meta_ref[2 + half] * PROMPT_DEV + query
    own = (key_pos <= query_pos) | is_cont
    shape = (CLEN, 4 * CLEN)
    key = lax.broadcasted_iota(jnp.int32, shape, 0)
    query = lax.broadcasted_iota(jnp.int32, shape, 1) % CLEN
    self_seen = (key <= query) & is_cont
    return own, self_seen


META = 8


def block_bias(meta_ref, is_cont, first_block, blocks):
    chips = [meta_ref[META + first_block + k] for k in range(blocks)]
    return [jnp.where(is_cont | (c <= meta_ref[6]), 0.0, masked_score) for c in chips]


def attend_kernel(first_block, blocks, first, last, meta_ref, q_ref, *refs):
    kv_refs, refs = refs[:blocks], refs[blocks:]
    if first:
        self_ref, refs = refs[0], refs[1:]
    else:
        acc_in, stat_in = refs[:2]
        refs = refs[2:]
    if last:
        out_ref, low_ref, lse_ref, scores = refs
    else:
        acc_out, stat_out, scores = refs
    tile = pl.program_id(0)
    half = tile // 3
    part = tile % 3
    is_cont = part == NPROMPT
    prompt = jnp.where(is_cont, meta_ref[half], part)
    rows = pl.ds(pl.multiple_of(prompt * PROMPT_ROWS, PROMPT_ROWS), PROMPT_ROWS)
    if first:
        own, self_seen = tile_masks(meta_ref, half, is_cont)
    bias = block_bias(meta_ref, is_cont, first_block, blocks)
    scale = score_scale * LOG2E
    k_width = KV_HEADS // 2 * HEAD_DIM
    for pair in range(2):
        lanes = pl.ds(pair * 128, 128)
        v_lanes = pl.ds(k_width + pair * 128, 128)
        q = stack_heads(q_ref[:, pair * 256 : (pair + 1) * 256]).astype(bf16)
        if first:
            s_self = jnp.where(self_seen, dot_nt(self_ref[0, :, lanes], q), masked_score)
            top = jnp.max(s_self, axis=0, keepdims=True)
        else:
            old = stat_in[0, pair, :1, :]
            top = old
        for k in range(blocks):
            s = dot_nt(kv_refs[k][rows, lanes], q)
            if first:
                s = jnp.where(own, s, masked_score)
            scores[pl.ds(k * PROMPT_ROWS, PROMPT_ROWS), :] = s
            top = jnp.maximum(top, jnp.max(s, axis=0, keepdims=True) + bias[k])
        top2 = top * scale
        if first:
            p = jnp.exp2(s_self * scale - top2)
            total = jnp.sum(p, axis=0, keepdims=True)
            acc = dot(jnp.transpose(self_ref[0, :, v_lanes]), p.astype(bf16))
        else:
            factor = jnp.exp2(old * scale - top2)
            total = stat_in[0, pair, 1:2, :] * factor
            acc = acc_in[0, pair] * factor
        for k in range(blocks):
            s = scores[pl.ds(k * PROMPT_ROWS, PROMPT_ROWS), :]
            p = jnp.exp2(s * scale - (top2 - bias[k]))
            total = total + jnp.sum(p, axis=0, keepdims=True)
            acc = acc + dot(jnp.transpose(kv_refs[k][rows, v_lanes]), p.astype(bf16))
        if last:
            out = unstack_heads(jnp.transpose(acc / total))
            out_ref[:, pair * 256 : (pair + 1) * 256] = out
            low_ref[:, pair * 256 : (pair + 1) * 256] = out.astype(bf16)
            lse = top2 + jnp.log2(total)
            for head in range(4):
                lse_ref[pl.ds(pair * 4 + head, 1), :] = lse[
                    :, head * PROMPT_DEV : (head + 1) * PROMPT_DEV
                ]
        else:
            acc_out[0, pair] = acc
            stat_out[0, pair, :1, :] = top
            stat_out[0, pair, 1:2, :] = total


def attend_back_kernel(first_block, blocks, first, last, meta_ref, q_ref, do_ref, out_ref, lse_ref, *refs):
    kv_refs, refs = refs[:blocks], refs[blocks:]
    if last:
        self_ref, cos_ref, sin_ref = refs[:3]
        refs = refs[3:]
    if not first:
        dq_in, refs = refs[0], refs[1:]
    dkv_refs, refs = refs[:blocks], refs[blocks:]
    if last:
        dq_ref, dself_ref, acc = refs
    else:
        dq_out, acc = refs
    tile = pl.program_id(0)
    half = tile // 3
    part = tile % 3
    is_cont = part == NPROMPT
    prompt = jnp.where(is_cont, meta_ref[half], part)
    start = pl.multiple_of(prompt * PROMPT_ROWS, PROMPT_ROWS)
    rows = pl.ds(start, PROMPT_ROWS)
    if last:
        own, self_seen = tile_masks(meta_ref, half, is_cont)
    bias = block_bias(meta_ref, is_cont, first_block, blocks)
    scale = score_scale * LOG2E
    k_width = KV_HEADS // 2 * HEAD_DIM

    @pl.when(tile == 0)
    def _():
        acc[...] = jnp.zeros_like(acc)

    for pair in range(2):
        lanes = pl.ds(pair * 128, 128)
        v_lanes = pl.ds(k_width + pair * 128, 128)
        cut = slice(pair * 256, (pair + 1) * 256)
        q = stack_heads(q_ref[:, cut]).astype(bf16)
        do_wide = stack_heads(do_ref[:, cut])
        delta = row_of(do_wide * stack_heads(out_ref[:, cut]))
        do = do_wide.astype(bf16)
        lse = jnp.concatenate(
            [lse_ref[pl.ds(pair * 4 + head, 1), :] for head in range(4)], axis=1
        )
        dq = jnp.zeros((128, 4 * PROMPT_DEV), f32) if first else dq_in[0, pair]
        for k in range(blocks):
            key, value = kv_refs[k][rows, lanes], kv_refs[k][rows, v_lanes]
            s = dot_nt(key, q)
            if last:
                s = jnp.where(own, s, masked_score)
            p = jnp.exp2(s * scale - (lse - bias[k]))
            ds = (p * (dot_nt(value, do) - delta)).astype(bf16)
            dq = dq + dot(jnp.transpose(key), ds)
            acc[k, rows, lanes] += dot(ds, q)
            acc[k, rows, v_lanes] += dot(p.astype(bf16), do)
        if last:
            key, value = self_ref[0, :, lanes], self_ref[0, :, v_lanes]
            s = jnp.where(self_seen, dot_nt(key, q), masked_score)
            p = jnp.exp2(s * scale - lse)
            ds = (p * (dot_nt(value, do) - delta)).astype(bf16)
            dq = dq + dot(jnp.transpose(key), ds)
            dself_ref[0, :, lanes] = dot(ds, q) * score_scale
            dself_ref[0, :, v_lanes] = dot(p.astype(bf16), do)
            wide = unstack_heads(jnp.transpose(dq)) * score_scale
            for group in range(2):
                turned = turn(wide[:, group * 128 : (group + 1) * 128], cos_ref[...], -sin_ref[...])
                lo = pair * 256 + group * 128
                dq_ref[:, lo : lo + 128] = turned.astype(bf16)
        else:
            dq_out[0, pair] = dq

    @pl.when(tile == pl.num_programs(0) - 1)
    def _():
        for k in range(blocks):
            dkv_refs[k][:, :k_width] = (acc[k, :, :k_width] * score_scale).astype(bf16)
            dkv_refs[k][:, k_width:] = acc[k, :, k_width:].astype(bf16)


def turn(values, cosine, sine_signed):
    lane = lax.broadcasted_iota(jnp.int32, values.shape, 1) % HEAD_DIM
    swapped = jnp.where(
        lane < HEAD_DIM // 2,
        pltpu.roll(values, 128 - HEAD_DIM // 2, 1),
        pltpu.roll(values, HEAD_DIM // 2, 1),
    )
    return values * cosine + swapped * sine_signed


VMEM_LIMIT = 40 * 1024 * 1024
SMALL_LIMIT = 24 * 1024 * 1024
WHOLE_LIMIT = 60 * 1024 * 1024


def whole_spec(array):
    return pl.BlockSpec(
        array.shape, lambda *_: (0,) * array.ndim, pipeline_mode=pl.Buffered(1)
    )


def attend(meta, queries, first_block, kv_blocks, state, cont_kv=None, last=False):
    blocks = len(kv_blocks)
    first = state is None
    rows, q_width = queries.shape
    tiles = rows // PROMPT_DEV
    columns = 4 * PROMPT_DEV
    row_spec = pl.BlockSpec((PROMPT_DEV, q_width), lambda t, meta: (t, 0))
    lse_spec = pl.BlockSpec((HEADS // 2, PROMPT_DEV), lambda t, meta: (0, t))
    acc_spec = pl.BlockSpec((1, 2, 128, columns), lambda t, meta: (t, 0, 0, 0))
    stat_spec = pl.BlockSpec((1, 2, 8, columns), lambda t, meta: (t, 0, 0, 0))
    pairs = rows * HEADS // 2 * blocks * PROMPT_ROWS
    in_specs = [row_spec] + [whole_spec(b) for b in kv_blocks]
    operands = [meta, queries, *kv_blocks]
    if first:
        in_specs.append(pl.BlockSpec((1,) + cont_kv.shape[1:], lambda t, meta: (t // 3, 0, 0)))
        operands.append(cont_kv)
    else:
        in_specs += [acc_spec, stat_spec]
        operands += list(state)
    if last:
        out_specs = [row_spec, row_spec, lse_spec]
        out_shape = [
            jax.ShapeDtypeStruct((rows, q_width), f32),
            jax.ShapeDtypeStruct((rows, q_width), bf16),
            jax.ShapeDtypeStruct((HEADS // 2, rows), f32),
        ]
    else:
        out_specs = [acc_spec, stat_spec]
        out_shape = [
            jax.ShapeDtypeStruct((tiles, 2, 128, columns), f32),
            jax.ShapeDtypeStruct((tiles, 2, 8, columns), f32),
        ]
    return pl.pallas_call(
        functools.partial(attend_kernel, first_block, blocks, first, last),
        grid_spec=pltpu.PrefetchScalarGridSpec(
            num_scalar_prefetch=1,
            grid=(tiles,),
            in_specs=in_specs,
            out_specs=out_specs,
            scratch_shapes=[pltpu.VMEM((blocks * PROMPT_ROWS, columns), f32)],
        ),
        out_shape=out_shape,
        compiler_params=pltpu.CompilerParams(vmem_limit_bytes=VMEM_LIMIT),
        cost_estimate=pl.CostEstimate(
            flops=48 * 64 * pairs, bytes_accessed=12 << 20, transcendentals=pairs
        ),
        name="attend",
    )(*operands)


def attend_back(meta, queries, grads, mixed, lse, first_block, kv_blocks, dq, own=None):
    blocks = len(kv_blocks)
    first, last = dq is None, own is not None
    rows, q_width = queries.shape
    tiles = rows // PROMPT_DEV
    columns = 4 * PROMPT_DEV
    row_spec = pl.BlockSpec((PROMPT_DEV, q_width), lambda t, meta: (t, 0))
    lse_spec = pl.BlockSpec((HEADS // 2, PROMPT_DEV), lambda t, meta: (0, t))
    dq_spec = pl.BlockSpec((1, 2, 128, columns), lambda t, meta: (t, 0, 0, 0))
    block = kv_blocks[0]
    pairs = rows * HEADS // 2 * blocks * PROMPT_ROWS
    in_specs = [row_spec, row_spec, row_spec, lse_spec] + [whole_spec(b) for b in kv_blocks]
    operands = [meta, queries, grads, mixed, lse, *kv_blocks]
    out_specs = [whole_spec(b) for b in kv_blocks]
    out_shape = [jax.ShapeDtypeStruct(b.shape, bf16) for b in kv_blocks]
    if last:
        cont_kv, cosine, sine = own
        self_spec = pl.BlockSpec((1,) + cont_kv.shape[1:], lambda t, meta: (t // 3, 0, 0))
        turn_spec = pl.BlockSpec((PROMPT_DEV, 128), lambda t, meta: (t, 0))
        in_specs += [self_spec, turn_spec, turn_spec]
        operands += [cont_kv, cosine, sine]
        out_specs += [row_spec, self_spec]
        out_shape += [
            jax.ShapeDtypeStruct((rows, q_width), bf16),
            jax.ShapeDtypeStruct(cont_kv.shape, f32),
        ]
    else:
        out_specs.append(dq_spec)
        out_shape.append(jax.ShapeDtypeStruct((tiles, 2, 128, columns), f32))
    if not first:
        in_specs.append(dq_spec)
        operands.append(dq)
    return pl.pallas_call(
        functools.partial(attend_back_kernel, first_block, blocks, first, last),
        grid_spec=pltpu.PrefetchScalarGridSpec(
            num_scalar_prefetch=1,
            grid=(tiles,),
            in_specs=in_specs,
            out_specs=out_specs,
            scratch_shapes=[pltpu.VMEM((blocks,) + block.shape, f32)],
        ),
        out_shape=out_shape,
        compiler_params=pltpu.CompilerParams(vmem_limit_bytes=VMEM_LIMIT),
        cost_estimate=pl.CostEstimate(
            flops=110 * 64 * pairs, bytes_accessed=16 << 20, transcendentals=pairs
        ),
        name="attend_back",
    )(*operands)


def core_pieces(columns, core, dp_size):
    width = columns.shape[-1] // (2 * dp_size)
    pieces = []
    for s in range(dp_size):
        lo = 2 * s * width
        pieces.append(
            jnp.where(core == 0, columns[:, lo : lo + width], columns[:, lo + width : lo + 2 * width])
        )
    return pieces


def core_heads(columns, core, dp_size):
    q, k = HEADS * HEAD_DIM, KV_HEADS * HEAD_DIM
    cuts = [columns[:, :q], columns[:, q : q + k], columns[:, q + k :]]
    return jnp.concatenate([p for cut in cuts for p in core_pieces(cut, core, dp_size)], axis=1)


def all_heads(mine, other, core, dp_size):
    first, second = jnp.where(core == 0, mine, other), jnp.where(core == 0, other, mine)
    q, k = HEADS // 2 * HEAD_DIM, KV_HEADS // 2 * HEAD_DIM
    pieces = []
    for lo, size in ((0, q), (q, k), (q + k, k)):
        width = size // dp_size
        for s in range(dp_size):
            cut = slice(lo + s * width, lo + (s + 1) * width)
            pieces += [first[:, cut], second[:, cut]]
    return jnp.concatenate(pieces, axis=1)


def cast_kernel(dp_size, meta_ref, weight_ref, out_ref):
    out_ref[...] = core_heads(weight_ref[...], meta_ref[0], dp_size).astype(bf16)


def cast_core_columns(core, weight, dp_size):
    rows, columns = weight.shape
    tile = rows // 4
    return pl.pallas_call(
        functools.partial(cast_kernel, dp_size),
        grid_spec=pltpu.PrefetchScalarGridSpec(
            num_scalar_prefetch=1,
            grid=(4,),
            in_specs=[pl.BlockSpec((tile, columns), lambda t, meta: (t, 0))],
            out_specs=pl.BlockSpec((tile, columns // 2), lambda t, meta: (t, 0)),
        ),
        out_shape=jax.ShapeDtypeStruct((rows, columns // 2), bf16),
        compiler_params=pltpu.CompilerParams(vmem_limit_bytes=SMALL_LIMIT),
        cost_estimate=pl.CostEstimate(
            flops=rows * columns, bytes_accessed=5 * rows * columns, transcendentals=0
        ),
        name="cast_core_columns",
    )(core[None], weight)


def project_kernel(shards, meta_ref, own_ref, other_ref, *refs):
    weights = refs[:shards]
    cos_ref, sin_ref, q_ref, prompt_ref, cont_ref = refs[shards:]
    half = pl.program_id(0)
    depth = weights[0].shape[0]
    q_width = q_ref.shape[-1]
    k_width = cont_ref.shape[-1] // 2
    cosine, sine = cos_ref[...], sin_ref[...]

    def run(x_ref):
        xs = []
        for k in range(shards):
            start = pl.multiple_of((meta_ref[5] + k) % shards * depth, depth)
            xs.append(x_ref[:, pl.ds(start, depth)])
        for lo in range(0, q_width + 2 * k_width, 128):
            if lo % 256 == 0:
                out = sum(dot(x, w[:, lo : lo + 256]) for x, w in zip(xs, weights))
            piece = out[:, lo % 256 : lo % 256 + 128]
            if lo < q_width + k_width:
                piece = turn(piece, cosine, sine)
            piece = piece.astype(bf16)
            if lo < q_width:
                q_ref[:, lo : lo + 128] = piece
            else:
                at = lo - q_width
                for g in range(NPROMPT):
                    rows = piece[g * PROMPT_DEV : (g + 1) * PROMPT_DEV]
                    prompt_ref[g, 0, :, at : at + 128] = rows
                cont_ref[0, :, at : at + 128] = piece[PROMPT_ROWS:]

    pl.when(half == 0)(lambda: run(own_ref))
    pl.when(half == 1)(lambda: run(other_ref))


def project(meta, own, other, weights, cosine, sine):
    rows, width = own.shape
    columns = weights[0].shape[1]
    kv_width = columns // 2
    turn_spec = pl.BlockSpec((rows, 128), lambda h, meta: (h, 0))
    return pl.pallas_call(
        functools.partial(project_kernel, len(weights)),
        grid_spec=pltpu.PrefetchScalarGridSpec(
            num_scalar_prefetch=1,
            grid=(2,),
            in_specs=[whole_spec(a) for a in (own, other, *weights)] + [turn_spec] * 2,
            out_specs=[
                pl.BlockSpec((rows, columns - kv_width), lambda h, meta: (h, 0)),
                pl.BlockSpec((NPROMPT, 1, PROMPT_DEV, kv_width), lambda h, meta: (0, h, 0, 0)),
                pl.BlockSpec((1, CLEN, kv_width), lambda h, meta: (h, 0, 0)),
            ],
        ),
        out_shape=[
            jax.ShapeDtypeStruct((2 * rows, columns - kv_width), bf16),
            jax.ShapeDtypeStruct((NPROMPT, 2, PROMPT_DEV, kv_width), bf16),
            jax.ShapeDtypeStruct((2, CLEN, kv_width), bf16),
        ],
        compiler_params=pltpu.CompilerParams(vmem_limit_bytes=SMALL_LIMIT),
        cost_estimate=pl.CostEstimate(
            flops=4 * rows * width * columns, bytes_accessed=8 << 20, transcendentals=0
        ),
        name="project",
    )(meta, own, other, *weights, cosine, sine)


def projected_grad_kernel(dq_ref, *refs):
    dkv_refs = refs[:3]
    dself_ref, cos_ref, sin_ref, out_ref = refs[3:]
    q_width = dq_ref.shape[-1]
    k_width = dself_ref.shape[-1] // 2
    out_ref[:, :q_width] = dq_ref[...]
    parts = [sum(ref[g, 0].astype(f32) for ref in dkv_refs) for g in range(NPROMPT)]
    dkv = jnp.concatenate(parts + [dself_ref[0]], axis=0)
    cosine, sine = cos_ref[...], -sin_ref[...]
    for lo in range(0, 2 * k_width, 128):
        piece = dkv[:, lo : lo + 128]
        if lo < k_width:
            piece = turn(piece, cosine, sine)
        out_ref[:, q_width + lo : q_width + lo + 128] = piece.astype(bf16)


def projected_grad(dq, dkv_parts, dself, cosine, sine):
    rows2, q_width = dq.shape
    rows = rows2 // 2
    kv_width = dself.shape[-1]
    dkv_parts = [p.reshape(NPROMPT, 2, PROMPT_DEV, kv_width) for p in dkv_parts]
    turn_spec = pl.BlockSpec((rows, 128), lambda h: (h, 0))
    return pl.pallas_call(
        projected_grad_kernel,
        grid=(2,),
        in_specs=[pl.BlockSpec((rows, q_width), lambda h: (h, 0))]
        + [pl.BlockSpec((NPROMPT, 1, PROMPT_DEV, kv_width), lambda h: (0, h, 0, 0))] * 3
        + [pl.BlockSpec((1, CLEN, kv_width), lambda h: (h, 0, 0)), turn_spec, turn_spec],
        out_specs=pl.BlockSpec((rows, q_width + kv_width), lambda h: (h, 0)),
        out_shape=jax.ShapeDtypeStruct((rows2, q_width + kv_width), bf16),
        compiler_params=pltpu.CompilerParams(vmem_limit_bytes=SMALL_LIMIT),
        cost_estimate=pl.CostEstimate(
            flops=20 * rows2 * kv_width, bytes_accessed=6 << 20, transcendentals=0
        ),
        name="projected_grad",
    )(dq, *dkv_parts, dself, cosine, sine)


def order_kernel(meta_ref, qkv_ref, out_ref, parts_ref):
    top = qkv_ref.shape[1]
    shards = qkv_ref.shape[0]
    rows = top + out_ref.shape[1]
    for s in range(shards):
        parts_ref[0, s * rows : s * rows + top, :] = qkv_ref[s]
        parts_ref[0, s * rows + top : (s + 1) * rows, :] = out_ref[s]


def order_parts(meta, qkv, out, chips, dp_size):
    width = qkv.shape[1]
    qkv = qkv.reshape(dp_size, -1, width)
    out = out.reshape(dp_size, -1, width)
    rows = [a.shape[1] // chips for a in (qkv, out)]
    return pl.pallas_call(
        order_kernel,
        grid_spec=pltpu.PrefetchScalarGridSpec(
            num_scalar_prefetch=1,
            grid=(chips,),
            in_specs=[
                pl.BlockSpec((dp_size, r, width), lambda k, meta: (0, meta[META + k], 0))
                for r in rows
            ],
            out_specs=pl.BlockSpec((1, dp_size * sum(rows), width), lambda k, meta: (k, 0, 0)),
        ),
        out_shape=jax.ShapeDtypeStruct((chips, dp_size * sum(rows), width), bf16),
        compiler_params=pltpu.CompilerParams(vmem_limit_bytes=SMALL_LIMIT),
        cost_estimate=pl.CostEstimate(
            flops=qkv.size, bytes_accessed=6 * qkv.size, transcendentals=0
        ),
        name="order_parts",
    )(meta, qkv, out)


def step_kernel(dp_size, grad_scale, meta_ref, grad_ref, *refs):
    qkv, out, step_ref = refs[:3], refs[3:6], refs[6]
    top = qkv[0].shape[0]
    grad = grad_ref[...].astype(f32)
    args = [core_heads(ref[...], meta_ref[4], dp_size) for ref in qkv]
    step_ref[:top, :] = adamw(*args, grad[:top], grad_scale, decay_rate)[0].astype(bf16)
    args = [ref[...] for ref in out]
    step_ref[top:, :] = adamw(*args, grad[top:], grad_scale, decay_rate)[0].astype(bf16)


def shard_step(meta, grad, qkv, out, chips, dp_size, grad_scale):
    qkv_rows, out_rows = qkv[0].shape[0] // chips, out[0].shape[0] // (2 * chips)
    width = grad.shape[1]
    return pl.pallas_call(
        functools.partial(step_kernel, dp_size, grad_scale),
        grid_spec=pltpu.PrefetchScalarGridSpec(
            num_scalar_prefetch=1,
            grid=(1,),
            in_specs=[whole_spec(grad)]
            + [pl.BlockSpec((qkv_rows, 2 * width), lambda t, meta: (meta[6], 0))] * 3
            + [pl.BlockSpec((out_rows, width), lambda t, meta: (meta[4] * chips + meta[6], 0))] * 3,
            out_specs=whole_spec(grad),
        ),
        out_shape=jax.ShapeDtypeStruct(grad.shape, bf16),
        compiler_params=pltpu.CompilerParams(vmem_limit_bytes=WHOLE_LIMIT),
        cost_estimate=pl.CostEstimate(
            flops=20 * grad.size, bytes_accessed=16 * grad.size, transcendentals=grad.size
        ),
        name="shard_step",
    )(meta, grad, *qkv, *out)


def optimizer_kernel(blocks, dp_size, grad_scale, spill, meta_ref, *refs):
    mine, refs = refs[:blocks], refs[blocks:]
    other, refs = refs[:blocks], refs[blocks:]
    qkv, out = refs[:3], refs[3:6]
    refs = refs[6 + spill :]
    step_qkv, mean_qkv, square_qkv, step_out, mean_out, square_out = refs
    core = meta_ref[4]
    top, out_rows = qkv[0].shape[0], out[0].shape[1]

    def run(mine_ref, other_ref):
        for shift in range(dp_size):
            rows = slice(shift * (top + out_rows), (shift + 1) * (top + out_rows))
            a, b = mine_ref[rows, :], other_ref[rows, :]
            whole = all_heads(a[:top], b[:top], core, dp_size).astype(f32)
            low = jnp.concatenate(
                [
                    jnp.where(core == 0, a[top:], b[top:])[None],
                    jnp.where(core == 0, b[top:], a[top:])[None],
                ],
                axis=0,
            ).astype(f32)
            if shift == 0:
                whole, mean, square = adamw(*[r[...] for r in qkv], whole, grad_scale, decay_rate)
                whole = whole.astype(bf16).astype(f32)
                mean_qkv[...] = mean
                square_qkv[...] = square
                low, mean, square = adamw(*[r[...] for r in out], low, grad_scale, decay_rate)
                low = low.astype(bf16).astype(f32)
                mean_out[...] = mean
                square_out[...] = square
            at = (meta_ref[5] + shift) % dp_size
            step_qkv[pl.ds(at, 1)] = whole[None]
            step_out[pl.ds(at, 1)] = low[None]

    for k in range(blocks):
        if blocks == 1:
            run(mine[k], other[k])
        else:
            pl.when(pl.program_id(0) == k)(functools.partial(run, mine[k], other[k]))


def optimize(meta, first_block, mine, other, qkv, out, buffers, chips, dp_size, grad_scale):
    blocks = len(mine)
    spill = 0 if buffers is None else 6
    qkv_rows = qkv[0].shape[0] // chips
    out_rows = out[0].shape[0] // (2 * chips)
    width = out[0].shape[1]
    out = [a.reshape(2, a.shape[0] // 2, width) for a in out]

    def at_chip(block, meta):
        return meta[META + first_block + block]

    own_qkv = pl.BlockSpec((qkv_rows, 2 * width), lambda b, meta: (at_chip(b, meta), 0))
    own_out = pl.BlockSpec((2, out_rows, width), lambda b, meta: (0, at_chip(b, meta), 0))
    step_qkv = pl.BlockSpec(
        (dp_size, qkv_rows, 2 * width), lambda b, meta: (0, at_chip(b, meta), 0)
    )
    step_out = pl.BlockSpec(
        (dp_size, 2, out_rows, width), lambda b, meta: (0, 0, at_chip(b, meta), 0)
    )
    shapes = [
        (dp_size,) + qkv[0].shape,
        qkv[0].shape,
        qkv[0].shape,
        (dp_size,) + out[0].shape,
        out[0].shape,
        out[0].shape,
    ]
    specs = [step_qkv, own_qkv, own_qkv, step_out, own_out, own_out]
    first = 1 + 2 * blocks + 6
    return pl.pallas_call(
        functools.partial(optimizer_kernel, blocks, dp_size, grad_scale, spill),
        grid_spec=pltpu.PrefetchScalarGridSpec(
            num_scalar_prefetch=1,
            grid=(blocks,),
            in_specs=[whole_spec(a) for a in (*mine, *other)]
            + [own_qkv] * 3
            + [own_out] * 3
            + [pl.BlockSpec(memory_space=pl.ANY)] * spill,
            out_specs=specs,
        ),
        out_shape=[jax.ShapeDtypeStruct(shape, f32) for shape in shapes],
        input_output_aliases={first + k: k for k in range(spill)},
        compiler_params=pltpu.CompilerParams(vmem_limit_bytes=WHOLE_LIMIT),
        cost_estimate=pl.CostEstimate(
            flops=blocks * qkv_rows * width * 60,
            bytes_accessed=blocks * qkv_rows * width * 90,
            transcendentals=blocks * qkv_rows * width * 3,
        ),
        name="optimize",
    )(meta, *mine, *other, *qkv, *out, *(buffers or ()))


def expert_kernel(count, tok, spill, meta_ref, *refs):
    x_refs, refs = refs[:count], refs[count:]
    cot_refs, refs = refs[:count], refs[count:]
    gate_ups, downs = refs[:2], refs[2:4]
    refs = refs[4 + spill :]
    mix_refs, refs = refs[:count], refs[count:]
    grad_refs, refs = refs[:count], refs[count:]
    x_all, cot_all, act_all, dgu_all = refs
    width = x_all.shape[-1]

    def run(x_ref, cot_ref, mix_ref, grad_ref):
        x = x_ref[:tok, :]
        cot = cot_ref[...]
        x_all[...] = x
        cot_all[...] = cot
        extra = x_ref[tok:, :].astype(f32)
        extra = extra[:, :tok] + extra[:, tok : 2 * tok]
        row = lax.broadcasted_iota(jnp.int32, extra.shape, 0)
        gates = jnp.zeros_like(extra)
        for e in range(2):
            mine = row == meta_ref[2 + e]
            weight = jnp.sum(jnp.where(mine, extra, 0.0), axis=0, keepdims=True)
            weight = jnp.transpose(jnp.broadcast_to(weight, (128, tok)))
            weight = jnp.concatenate([weight, weight], axis=1)
            gate_grad = jnp.zeros((tok, 1), f32)
            for lo in range(0, EXP_FF, 256):
                hi = lo + 256
                gate = dot(x, gate_ups[e][:, lo:hi])
                up = dot(x, gate_ups[e][:, EXP_FF + lo : EXP_FF + hi])
                dact = dot_nt(cot, downs[e][lo:hi, :])
                sig = 0.5 * jnp.tanh(0.5 * gate) + 0.5
                silu = gate * sig
                act = silu * up
                gate_grad = gate_grad + jnp.sum(act * dact, axis=-1, keepdims=True)
                act_all[:, e * EXP_FF + lo : e * EXP_FF + hi] = (act * weight).astype(bf16)
                dact = dact * weight
                dgate = dact * up * (sig + silu * (1.0 - sig))
                at = 2 * e * EXP_FF
                dgu_all[:, at + lo : at + hi] = dgate.astype(bf16)
                dgu_all[:, at + EXP_FF + lo : at + EXP_FF + hi] = (dact * silu).astype(bf16)
            gate_row = jnp.transpose(jnp.broadcast_to(gate_grad, (tok, 128)))[:1, :]
            gates = jnp.where(mine, gate_row, gates)
        acts = [act_all[:, e * EXP_FF : (e + 1) * EXP_FF] for e in range(2)]
        dgus = [dgu_all[:, 2 * e * EXP_FF : 2 * (e + 1) * EXP_FF] for e in range(2)]
        for lo in range(0, width, 256):
            mix = sum(dot(acts[e], downs[e][:, lo : lo + 256]) for e in range(2))
            mix_ref[:, lo : lo + 256] = mix.astype(bf16)
        for lo in range(0, width, 256):
            grad = sum(dot_nt(dgus[e], gate_ups[e][lo : lo + 256, :]) for e in range(2))
            grad_ref[:tok, lo : lo + 256] = grad.astype(bf16)
        high = gates.astype(bf16)
        grad_ref[tok:, :tok] = high
        grad_ref[tok:, tok : 2 * tok] = (gates - high.astype(f32)).astype(bf16)
        grad_ref[tok:, 2 * tok :] = jnp.zeros((extra.shape[0], width - 2 * tok), bf16)

    for b in range(count):
        body = functools.partial(run, x_refs[b], cot_refs[b], mix_refs[b], grad_refs[b])
        if count == 1:
            body()
        else:
            pl.when(pl.program_id(0) == b)(body)


def run_experts(meta, x_blocks, cot_blocks, weights, buffers, place, total):
    count = len(x_blocks)
    packed, width = x_blocks[0].shape
    tok = cot_blocks[0].shape[0]
    rows = count * tok
    spill = 0 if buffers is None else 4
    any_spec = pl.BlockSpec(memory_space=pl.ANY)
    stream_width = [width, width, 2 * EXP_FF, 4 * EXP_FF]
    stream = [pl.BlockSpec((tok, w), lambda g, ids: (place + g, 0)) for w in stream_width]
    out = pl.pallas_call(
        functools.partial(expert_kernel, count, tok, spill),
        grid_spec=pltpu.PrefetchScalarGridSpec(
            num_scalar_prefetch=1,
            grid=(count,),
            in_specs=[
                whole_spec(a) for a in (*x_blocks, *cot_blocks, *weights)
            ]
            + [any_spec] * spill,
            out_specs=[whole_spec(c) for c in cot_blocks]
            + [whole_spec(x) for x in x_blocks]
            + stream,
        ),
        out_shape=[jax.ShapeDtypeStruct(c.shape, bf16) for c in cot_blocks]
        + [jax.ShapeDtypeStruct(x.shape, bf16) for x in x_blocks]
        + [jax.ShapeDtypeStruct((total, w), bf16) for w in stream_width],
        input_output_aliases={1 + 2 * count + 4 + k: 2 * count + k for k in range(spill)},
        compiler_params=pltpu.CompilerParams(vmem_limit_bytes=VMEM_LIMIT),
        cost_estimate=pl.CostEstimate(
            flops=2 * 2 * rows * width * EXP_FF * 6,
            bytes_accessed=rows * width * 20 + 6 * width * width,
            transcendentals=2 * rows * EXP_FF,
        ),
        name="experts",
    )(meta, *x_blocks, *cot_blocks, *weights, *(buffers or ()))
    return out[:count], out[count : 2 * count], out[2 * count :]


def per_device(
    ring,
    tokens,
    cotangent,
    routes,
    cont_group,
    attn_gain,
    qkv_weight,
    out_weight,
    ffn_gain,
    router_weight,
    gate_up_weight,
    down_weight,
    mean_attn_gain,
    mean_qkv_weight,
    mean_out_weight,
    mean_ffn_gain,
    mean_router_weight,
    mean_gate_up_weight,
    mean_down_weight,
    square_attn_gain,
    square_qkv_weight,
    square_out_weight,
    square_ffn_gain,
    square_router_weight,
    square_gate_up_weight,
    square_down_weight,
):
    chips = ring.chips
    dp_size = lax.axis_size("dp")
    dp = lax.axis_index("dp")
    chip = lax.axis_index("chip")
    core = lax.axis_index("core")
    members = 2 * chips
    tok_count, width = tokens.shape
    experts = router_weight.shape[1]
    capacity = 5 * tok_count * TOPK // (4 * experts)
    prompt_len = PROMPT_DEV * members
    core_heads = HEADS // 2
    core_kv = KV_HEADS // 2
    q_width = core_heads * HEAD_DIM
    k_width = core_kv * HEAD_DIM

    member_pair = jnp.stack([2 * chip + core, 2 * chip + 1 - core])
    groups = jnp.concatenate([cont_group, swap(cont_group)])
    own_place = jnp.stack([core, dp, chip, 0])
    meta = jnp.concatenate([groups, member_pair, own_place, ring.chips_from(chip)])

    tokens = split_rows(tokens)
    cotangent = split_rows(cotangent)
    routes = split_rows(routes)
    tok_float = tokens.astype(f32)

    qkv_core = cast_core_columns(core, qkv_weight, dp_size)
    small = jnp.concatenate([attn_gain[None], ffn_gain[None], router_weight.T], axis=0).astype(bf16)
    small = gather_dp(small, 1)
    qkv_shards = dp_shards(qkv_core)
    gain_attn = small[0].astype(f32)
    gain_ffn = small[1].astype(f32)
    proj_router_t = small[2:]

    scale_attn = lax.rsqrt(jnp.mean(tok_float * tok_float, axis=-1, keepdims=True) + norm_eps)
    attn_in = (tok_float * scale_attn * gain_attn).astype(bf16)
    cot_ring = RingGather(ring, cotangent)
    cot_ring.step()
    attn_in = after(attn_in, cot_ring.ends())
    cot_ring.step()
    attn_other = swap(attn_in)
    qkv_shards = after(qkv_shards, cot_ring.ends())
    while cot_ring.place < ring.half - 1:
        cot_ring.step()
    within = jnp.arange(PROMPT_DEV, dtype=jnp.int32)
    prompt_pos = member_pair[:, None] * PROMPT_DEV + within
    cont_pos = jnp.broadcast_to(prompt_len + within, (2, CLEN))
    position = jnp.stack([prompt_pos, prompt_pos, cont_pos], axis=1).reshape(-1)
    half_dim = HEAD_DIM // 2
    frequency = jnp.exp(
        jnp.arange(half_dim, dtype=f32) * (-2.0 * math.log(10000.0) / HEAD_DIM)
    )
    angles = position.astype(f32)[:, None] * frequency[None, :]
    cosine_part, sine_part = jnp.cos(angles), jnp.sin(angles)
    cosine = jnp.concatenate([cosine_part] * 4, axis=1)
    sine_signed = jnp.concatenate([-sine_part, sine_part] * 2, axis=1)
    rows2 = 2 * tok_count
    queries, prompt_kv, cont_kv = project(
        meta, attn_in, attn_other, qkv_shards, cosine, sine_signed
    )
    prompt_kv = prompt_kv.reshape(2 * PROMPT_ROWS, 2 * k_width)
    prompt_kv = after(prompt_kv, cot_ring.ends())
    half_rows = out_weight.shape[0] // 2
    late_gate_up, late_down, late_out = after(
        (gate_up_weight[0], down_weight[0], out_weight), prompt_kv
    )
    out_core = pick_core(late_out[:half_rows], late_out[half_rows:]).astype(bf16)
    own_gate_up = lax.all_gather(late_gate_up.astype(bf16), "dp", axis=0, tiled=True)
    own_down = lax.all_gather(late_down.astype(bf16), "dp", axis=0, tiled=True)
    expert_weights = [own_gate_up, swap(own_gate_up), own_down, swap(own_down)]
    attn_in2 = jnp.concatenate([attn_in, attn_other], axis=0)
    proj_qkv = join_dp(after(qkv_shards, prompt_kv), 0)
    proj_out = gather_dp(after(out_core, prompt_kv), 0)
    kv_blocks, state = {}, None
    for arrived in ring.gather_steps(prompt_kv):
        kv_blocks.update(arrived)
        if 2 in arrived:
            state, proj_qkv = after((state, proj_qkv))
            small_state = [
                jnp.concatenate([a[None], f[None], r.T], axis=0)
                for a, f, r in (
                    (attn_gain, ffn_gain, router_weight),
                    (mean_attn_gain, mean_ffn_gain, mean_router_weight),
                    (square_attn_gain, square_ffn_gain, square_router_weight),
                )
            ]
            small_state = gather_dp(after(jnp.stack(small_state), state), 2)
        if ring.half in arrived:
            state, small_state = after((state, small_state))
        state = attend(
            meta,
            queries,
            ring.by_distance.index(min(arrived)),
            list(arrived.values()),
            state,
            cont_kv if 0 in arrived else None,
            ring.half in arrived,
        )
    mixed, mixed_low, lse = state
    cot_blocks = cot_ring.blocks

    part = dot(mixed_low, proj_out)
    other = swap(part[tok_count:].astype(bf16))
    hidden = tok_float + part[:tok_count] + other.astype(f32)
    scale_ffn = lax.rsqrt(jnp.mean(hidden * hidden, axis=-1, keepdims=True) + norm_eps)
    ffn_in = (hidden * scale_ffn * gain_ffn).astype(bf16)
    logits = dot_nt(proj_router_t, ffn_in)
    expert_ids = jnp.arange(experts, dtype=jnp.int32)
    hot = jnp.any(routes.T[None] == expert_ids[:, None, None], axis=1)
    hot_float = hot.astype(f32)
    shown = jnp.where(hot, logits, masked_score)
    raised = jnp.where(hot, jnp.exp(shown - jnp.max(shown, axis=0, keepdims=True)), 0.0)
    gate_probs = raised / jnp.sum(raised, axis=0, keepdims=True)
    spot = jnp.arange(tok_count, dtype=jnp.int32)
    spot = jnp.where(
        spot < PROMPT_ROWS, (spot % PROMPT_DEV) * NPROMPT + spot // PROMPT_DEV, spot
    )
    earlier = (spot[:, None] < spot[None, :]).astype(bf16)
    placed = dot(hot.astype(bf16), earlier)
    kept = hot & (placed < capacity)
    pair_weight = jnp.where(kept, gate_probs, 0.0)
    weight_high = lax.reduce_precision(pair_weight, 8, 7)
    weight_rows = jnp.concatenate([weight_high, pair_weight - weight_high], axis=1).astype(bf16)
    weight_rows = jnp.pad(weight_rows, ((0, 0), (0, width - 2 * tok_count)))
    packed = jnp.concatenate([ffn_in, weight_rows], axis=0)

    total_rows = chips * tok_count
    mix_parts, grad_parts = {}, {}
    buffers = None
    packed = after(packed, cot_ring.ends())
    ffn_ring = RingGather(ring, packed)
    arrived, place = {0: packed}, 0
    while arrived:
        later = {}
        if ffn_ring.place < ring.half:
            later = ffn_ring.step(*(buffers or ()))
        if ring.half in later:
            cot_ring.step(ffn_ring.before)
        mixes, grads, buffers = run_experts(
            meta,
            list(arrived.values()),
            [cot_blocks[r] for r in arrived],
            expert_weights,
            buffers,
            place,
            total_rows,
        )
        mix_parts.update(zip(arrived, mixes))
        grad_parts.update(zip(arrived, grads))
        place += len(arrived)
        arrived = later

    grad_sum = RingSum(ring, grad_parts[ring.half])
    grad_sum.add(grad_parts)
    x_all, cot_all, act_all, dgu_all = after(buffers, grad_sum.sent)
    other_gate_up = dot_tn(x_all, dgu_all[:, 2 * EXP_FF :]).astype(bf16)
    other_down = dot_tn(act_all[:, EXP_FF:], cot_all).astype(bf16)
    grad_sum.add(grad_parts, other_gate_up, other_down)
    other_gate_up, other_down = after((other_gate_up, other_down), grad_sum.sent)
    other_gate_up, other_down = swap(other_gate_up), swap(other_down)
    while grad_sum.place > 1:
        grad_sum.add(grad_parts, other_gate_up, other_down)
    x_all, cot_all, act_all, dgu_all = after(buffers, grad_sum.sent)
    grad_gate_up = dot_tn(x_all, dgu_all[:, : 2 * EXP_FF]) + other_gate_up.astype(f32)
    grad_gate_up = grad_gate_up.astype(bf16)
    grad_down = dot_tn(act_all[:, :EXP_FF], cot_all) + other_down.astype(f32)
    grad_down = grad_down.astype(bf16)
    grad_packed, grad_gate_up, grad_down = lax.optimization_barrier(
        (grad_sum.finish(grad_parts[0]), grad_gate_up, grad_down)
    )
    mix_sum = RingSum(ring, after(mix_parts[ring.half], grad_sum.arrived()))

    def shards_dp(whole):
        pieces = whole.reshape((dp_size, whole.shape[0] // dp_size) + whole.shape[1:])
        out = [lax.dynamic_index_in_dim(pieces, dp, 0, False)]
        for shift in range(1, dp_size):
            perm = [(k, (k + shift) % dp_size) for k in range(dp_size)]
            part = lax.dynamic_index_in_dim(pieces, (dp + shift) % dp_size, 0, False)
            out.append(lax.ppermute(part, "dp", perm))
        return out

    def sum_of(pieces, *others):
        return sum(piece.astype(f32) for piece in after(pieces, others))


    grad_gate = grad_packed[tok_count:, :tok_count] + grad_packed[tok_count:, tok_count : 2 * tok_count]
    grad_gate = jnp.where(kept, grad_gate, 0.0)
    grad_chosen = gate_probs * (grad_gate - jnp.sum(gate_probs * grad_gate, axis=0, keepdims=True))
    grad_logits = (hot_float * grad_chosen).astype(bf16)
    grad_router_t = dot(grad_logits, ffn_in)
    grad_ffn = grad_packed[:tok_count] + dot_tn(grad_logits, proj_router_t)
    grad_output = cotangent.astype(f32)
    grad_hidden_norm, grad_gain_ffn = norm_back(hidden, scale_ffn, gain_ffn, grad_ffn)
    grad_hidden = grad_output + grad_hidden_norm
    grad_attn = after(grad_hidden.astype(bf16), mix_sum.arrived())
    grad_attn2 = jnp.concatenate([grad_attn, swap(grad_attn)], axis=0)
    grad_mixed = dot_nt(grad_attn2, proj_out).astype(bf16)
    mix_sum.add(mix_parts, grad_mixed)

    grad_scale = (tok_count * dp_size * members) ** (-0.5)

    dq, dkv, dkv_sum = None, (), None
    for turn_no, places in enumerate(ring.groups()[::-1]):
        if turn_no >= 2:
            grad_mixed = after(grad_mixed, dkv_before)
        if 0 in places or (turn_no % 2 == 0 and mix_sum.place > 3):
            grad_mixed = after(grad_mixed, mix_sum.arrived())
            mix_sum.add(mix_parts, dkv)
        dkv = attend_back(
            meta,
            queries,
            grad_mixed,
            mixed,
            lse,
            ring.by_distance.index(min(places)),
            [kv_blocks[r] for r in places],
            dq,
            (cont_kv, cosine, sine_signed) if 0 in places else None,
        )
        parts = dict(zip(places, dkv))
        if ring.half in places:
            dkv_sum = RingSum(ring, parts[ring.half])
        elif 0 not in places:
            grad_out_weight = dot_tn(after(mixed_low, dkv), grad_attn2)
            if turn_no == 1:
                late_gate_up, late_down = after((grad_gate_up, grad_down), dkv)
                gate_up_shards, down_shards = shards_dp(late_gate_up), shards_dp(late_down)
            dkv_before = dkv_sum.arrived()
            dkv_sum.add(parts)
        if 0 not in places:
            dq = dkv[len(places)]
    grad_projected = projected_grad(
        dkv[1], (parts[0], *dkv_sum.arrived()), dkv[2], cosine, sine_signed
    )
    grad_qkv_weight = dot_tn(attn_in2, grad_projected)
    part = dot_nt(grad_projected, proj_qkv)
    other_part = swap(part[tok_count:].astype(bf16))

    qkv_rows = width // dp_size // chips
    out_rows = HEADS * HEAD_DIM // dp_size // 2 // chips
    dense_parts = order_parts(
        meta, grad_qkv_weight.astype(bf16), grad_out_weight.astype(bf16), chips, dp_size
    )
    parts = {r: dense_parts[k] for k, r in enumerate(ring.by_distance)}
    dense_sum = RingSum(ring, parts[ring.half])
    dense_sum.add(parts, mix_sum.arrived())
    gate_up_new = adamw(
        gate_up_weight,
        mean_gate_up_weight,
        square_gate_up_weight,
        sum_of(gate_up_shards, dense_sum.sent)[None],
        grad_scale,
        decay_rate,
    )
    dense_sum.add(parts, gate_up_new, other_part)
    grad_attn_in = part[:tok_count] + after(other_part, dense_sum.sent).astype(f32)
    grad_tok_norm, grad_gain_attn = norm_back(tok_float, scale_attn, gain_attn, grad_attn_in)
    input_grad = grad_hidden + grad_tok_norm
    small_grad = jnp.concatenate(
        [grad_gain_attn[None], grad_gain_ffn[None], grad_router_t], axis=0
    )
    down_new = adamw(
        down_weight,
        mean_down_weight,
        square_down_weight,
        sum_of(down_shards, dense_sum.sent)[None],
        grad_scale,
        decay_rate,
    )
    dense_sum.add(parts, down_new, small_grad)
    while dense_sum.place > 1:
        dense_sum.add(parts)
    for small_grad in total_stages(small_grad, ("core", "dp")):
        pass
    dense = after(dense_sum.finish(parts[0]), small_grad)
    dense = dense.reshape(dp_size, qkv_rows + out_rows, width)
    mix_sum.add(mix_parts, dense)
    shard = lax.dynamic_index_in_dim(dense, dp, 0, False)
    for shift in range(1, dp_size):
        perm = [(k, (k + shift) % dp_size) for k in range(dp_size)]
        sent = lax.dynamic_index_in_dim(dense, (dp + shift) % dp_size, 0, False)
        shard = shard + lax.ppermute(sent.astype(bf16), "dp", perm).astype(f32)
    shard_low = shard.astype(bf16)

    qkv_state = (qkv_weight, mean_qkv_weight, square_qkv_weight)
    out_state = (out_weight, mean_out_weight, square_out_weight)
    step_shard = shard_step(
        meta, shard_low, qkv_state, out_state, chips, dp_size, grad_scale
    )
    small_rows = -(-small_grad.shape[0] // 16) * 16
    small_low = jnp.pad(small_grad.astype(bf16), ((0, small_rows - small_grad.shape[0]), (0, 0)))
    carried = jnp.concatenate([shard_low, *dp_shards(step_shard)[1:], small_low], axis=0)
    input_grad = merge_rows(input_grad)
    carried = after(carried, mix_sum.arrived(), input_grad)
    while mix_sum.place > 1:
        mix_sum.add(mix_parts, step_shard)
    output = hidden + mix_sum.finish(mix_parts[0])
    dense_new = None
    dense_ring = RingGather(ring, carried)
    arrived, first_place, earlier = dict(dense_ring.blocks), 0, [()]
    while arrived:
        later = {}
        if dense_ring.place < ring.half:
            later = dense_ring.step(*earlier.pop(0))
        earlier.append(tuple(dense_new or ()))
        dense_new = optimize(
            meta,
            first_place,
            list(arrived.values()),
            [swap(m) for m in arrived.values()],
            qkv_state,
            out_state,
            dense_new,
            chips,
            dp_size,
            grad_scale,
        )
        first_place += len(arrived)
        if ring.half - 2 in arrived:
            dense_most = dense_new
        arrived = later
    dense_new = [a.reshape(-1, a.shape[-1]) for a in dense_new]

    base = dp_size * (qkv_rows + out_rows)
    count = small_grad.shape[0]
    small_total = sum(
        dense_ring.blocks[r][base : base + count].astype(f32) for r in ring.by_distance
    )
    decays = jnp.full((count, 1), decay_rate, f32).at[:2].set(0.0)
    small_new = adamw(*small_state, small_total, grad_scale, decays)
    shard_cols = width // dp_size
    small_step = small_new[0]
    small_mean, small_square = [
        lax.dynamic_slice_in_dim(a, dp * shard_cols, shard_cols, 1) for a in small_new[1:]
    ]

    step_gate_up = lax.all_gather(gate_up_new[0].astype(bf16), "dp", axis=1, tiled=True)
    step_down = lax.all_gather(down_new[0].astype(bf16), "dp", axis=1, tiled=True)
    step_gate_up, step_down = after((step_gate_up, step_down), dense_most)
    return (
        merge_rows(output.astype(bf16)),
        input_grad,
        small_step[0],
        dense_new[0],
        dense_new[3],
        small_step[1],
        small_step[2:].T,
        step_gate_up.astype(f32),
        step_down.astype(f32),
        small_mean[0],
        dense_new[1],
        dense_new[4],
        small_mean[1],
        small_mean[2:].T,
        gate_up_new[1],
        down_new[1],
        small_square[0],
        dense_new[2],
        dense_new[5],
        small_square[1],
        small_square[2:].T,
        gate_up_new[2],
        down_new[2],
    )


def solution(mesh):
    dp_size, members = mesh.shape["dp"], mesh.shape["expert"]
    chips = members // 2
    fine = Mesh(mesh.devices.reshape(dp_size, chips, 2), ("dp", "chip", "core"))
    ring = Ring(chips)
    member = ("chip", "core")
    token = P(("dp",) + member, None)
    matrices = (P("dp"), P("dp", None), P("dp", None), P("dp"), P("dp", None))
    expert = (P(member, "dp", None), P(member, "dp", None))

    def body(*arrays):
        return per_device(ring, *arrays)

    return jax.shard_map(
        body,
        mesh=fine,
        in_specs=(token, token, token, P(("dp",) + member)) + (matrices + expert) * 3,
        out_specs=(token, token)
        + (P(),) * 5
        + (P(member, None, None),) * 2
        + (matrices + expert) * 2,
        check_vma=False,
    )
```
